32 devices in a mesh: illum: 2 (over x), row: 4 (over y, core), col: 4 (over z).
Axes of the slice: x: 2, y: 2, z: 4, core: 2. Of those that a mesh axis runs over, the one named last changes fastest.
Arguments:
- phase_delay: float32 [2, 512, 4096], P(None, ('row', 'illum'), 'col'), may hold values from -1 to 1
- angles: int32 [2, 2], P('illum'), may hold values from -8 to 8
- measured: bfloat16 [2, 2, 512, 4096], P(None, 'illum', 'row', 'col'), may hold values from -120 to 120, as said below
Outputs:
- phase_grad: float32 [2, 512, 4096], P(None, ('row', 'illum'), 'col')
The draws below stay inside these ranges and needn't reach their ends.
Inputs may be any that keep to these rules, and one draw needn't show every extreme that they name: Real and imaginary parts of a measured field, with scales that vary over rows and columns.
All inputs are finite; a program needn't handle non-finite values.
Results may differ from the reference program's by a relative error of at most 0.0003.
Values sent between devices are 32-bit elements; how exact they have to be, the bound alone decides.
No kernel may reach another device: no remote copies, remote signals or barrier semaphores. Data moves between devices by JAX's collectives and lax.ppermute only.
A program may use at most 64 MiB of HBM per device.

```python
import math
import jax
import jax.numpy as jnp
from jax import lax

SLICES = 2
SWEEPS = 2
NX = 512
NY = 4096
ILLUMS = 2


def draw_measured(key, part):
    key_base, key_rows, key_cols = jax.random.split(key, 3)
    ramp = 3.0 ** (jnp.arange(NX, dtype=jnp.float32) / max(NX - 1, 1))
    base = jnp.clip(jax.random.normal(key_base, (2, ILLUMS, NX, NY), jnp.float32), -4.0, 4.0)
    row_scale = jnp.exp(jax.random.uniform(key_rows, (NX,), jnp.float32, 0.0, 1.1513))
    col_scale = jnp.exp(jax.random.uniform(key_cols, (NY,), jnp.float32, 0.0, 1.1513))
    scaled = base * (row_scale * ramp)[:, None] * col_scale[None, :]
    return scaled.astype(jnp.bfloat16)


def with_ends(drawn, rng, least, high):
    dims = drawn.shape
    spot = [jax.random.randint(jax.random.fold_in(rng, axis), (), 0, dims[axis]) for axis in range(len(dims))]
    drawn = drawn.at[tuple(spot)].set(least)
    longest = dims.index(max(dims))
    spot[longest] = (spot[longest] + 1) % dims[longest]
    return drawn.at[tuple(spot)].set(high)


def steps_of(rng, extent, cuts, smallest, largest):
    def one(dim, parts):
        draws = jax.random.uniform(jax.random.fold_in(jax.random.fold_in(rng, 6), dim), (parts,), jnp.float32, smallest / len(cuts), largest / len(cuts))
        return jnp.repeat(jnp.exp(draws), extent[dim] // parts).reshape((-1,) + (1,) * (len(extent) - dim - 1))

    factor_of = one(*cuts[0])
    for cut in cuts[1:]:
        factor_of = factor_of * one(*cut)
    return factor_of


def setup_inputs(seed: int = 0) -> dict:
    arg_keys = jax.random.split(jax.random.key(seed), 4)
    return {
        "phase_delay": jnp.clip(jax.random.uniform(arg_keys[0], (SLICES, NX, NY), jnp.float32, -1.0, 1.0) * steps_of(arg_keys[0], (SLICES, NX, NY), ((1, 8), (2, 4)), -0.4, 0.0), -1.0, 1.0),
        "angles": with_ends(jax.random.randint(arg_keys[1], (ILLUMS, 2), -8, 9), jax.random.fold_in(arg_keys[1], 1), -8, 8).astype(jnp.int32),
        "measured": draw_measured(jax.random.fold_in(arg_keys[3], 71), 0),
    }


beta_step = 0.5
eps_energy = 1e-06

def neighbour_sum(padded):
    return padded[..., 2:, 1:-1] + padded[..., :-2, 1:-1] + padded[..., 1:-1, 2:] + padded[..., 1:-1, :-2]

def around_of(wave_field):
    return neighbour_sum(jnp.pad(wave_field, ((0, 0), (1, 1), (1, 1))))

def propagate(wave_field, direction):
    beta_sign = direction * beta_step
    divisor = 1.0 + 16.0 * beta_sign * beta_sign
    beside_all = around_of(wave_field)
    real_part, imag_part = (wave_field[0], wave_field[1])
    rhs_real = real_part + 4.0 * beta_sign * imag_part - beta_sign * beside_all[1]
    rhs_imag = imag_part - 4.0 * beta_sign * real_part + beta_sign * beside_all[0]
    for sweep in range(SWEEPS):
        if sweep > 0:
            beside_all = around_of(jnp.stack([real_part, imag_part]))
        total_real = rhs_real - beta_sign * beside_all[1]
        total_imag = rhs_imag + beta_sign * beside_all[0]
        real_part = (total_real + 4.0 * beta_sign * total_imag) / divisor
        imag_part = (total_imag - 4.0 * beta_sign * total_real) / divisor
    return jnp.stack([real_part, imag_part])

def incident(angle_pair):
    row_ids = lax.iota(jnp.int32, NX)
    col_ids = lax.iota(jnp.int32, NY)
    along_x = angle_pair[0] * row_ids % NX
    along_y = angle_pair[1] * col_ids % NY
    angle_phase = 2.0 * math.pi * (along_x.astype(jnp.float32)[:, None] / NX + along_y.astype(jnp.float32)[None, :] / NY)
    return jnp.stack([jnp.cos(angle_phase), jnp.sin(angle_phase)])

def reference(phase_delay, angles, measured):

    def one_wave(carry, which):
        angle_pair = lax.dynamic_index_in_dim(angles, which, 0, keepdims=False)
        target = lax.dynamic_index_in_dim(measured, which, 1, keepdims=False).astype(jnp.float32)
        energy = jnp.sum(target * target) / (NX * NY) + eps_energy

        def loss_of(phases):
            wave_field = incident(angle_pair)
            for depth_index in range(SLICES):
                cosine = jnp.cos(phases[depth_index])
                sine_part = jnp.sin(phases[depth_index])
                modulated = jnp.stack([wave_field[0] * cosine - wave_field[1] * sine_part, wave_field[0] * sine_part + wave_field[1] * cosine])
                wave_field = propagate(modulated, 1.0)
            return jnp.sum((wave_field - target) ** 2) / energy
        return (carry + jax.grad(loss_of)(phase_delay), None)
    zeros = jnp.zeros(phase_delay.shape, jnp.float32)
    summed, _ = lax.scan(one_wave, zeros, jnp.arange(ILLUMS, dtype=jnp.int32))
    return summed
```

```python
import functools
import math

import jax
import jax.numpy as jnp
from jax import lax
from jax.experimental import pallas as pl
from jax.experimental.pallas import tpu as pltpu
from jax.sharding import PartitionSpec as P

EPS_ENERGY = 1e-06
RIM = 8
REACH = 4
LANES = 128
F32 = jnp.float32


def sine_cosine(x):
    y = x * x
    s = -2.5052108385441718e-08
    for c in (2.7557319223985893e-06, -1.9841269841269841e-04, 8.333333333333333e-03, -1.6666666666666666e-01):
        s = s * y + c
    c_ = -2.7557319223985888e-07
    for c in (2.48015873015873e-05, -1.3888888888888889e-03, 4.1666666666666664e-02, -0.5, 1.0):
        c_ = c_ * y + c
    return x + x * y * s, c_


def sine_cosine_of_turns(turns):
    quarters = 4.0 * (turns - jnp.floor(turns))
    nearest = jnp.floor(quarters + 0.5)
    s, c = sine_cosine((quarters - nearest) * (0.5 * math.pi))
    odd = (nearest == 1.0) | (nearest == 3.0)
    s, c = jnp.where(odd, c, s), jnp.where(odd, s, c)
    s = jnp.where((nearest == 2.0) | (nearest == 3.0), -s, s)
    c = jnp.where((nearest == 1.0) | (nearest == 2.0), -c, c)
    return s, c


def lane_ids(shape):
    return lax.broadcasted_iota(jnp.int32, shape, len(shape) - 1)


class Tile:
    def __init__(self, stripe, tiles, top, bottom, rim_lanes):
        self.stripe, self.tiles = stripe, tiles
        self.rows = stripe + 2 * RIM
        self.top, self.bottom, self.rim_lanes = top, bottom, rim_lanes
        step = 32 if stripe % 32 == 0 else 8
        self.inner = [(2 * RIM + r, step, None) for r in range(0, stripe, step)]
        self.blocks = [(RIM, RIM, top)] + self.inner + [(2 * RIM + stripe, RIM, bottom)]

    def sweep(self, body, blocks):
        def one(t, last):
            left = jnp.where(t == 0, self.tiles - 1, t - 1) if not last else self.tiles - 2
            right = t + 1 if not last else 0
            for first, count, factor in blocks:
                mask = (lambda x: x) if factor is None else (lambda x, f=factor: x * f)
                if last:
                    mask = lambda x, m=mask: m(x) * self.rim_lanes
                body(t, left, right, pl.ds(first, count), mask)

        def step(t, carry):
            one(t, False)
            return carry

        lax.fori_loop(0, self.tiles - 1, step, 0)
        one(self.tiles - 1, True)


def beside(ref, t, left, right, rows):
    above = pl.ds(rows.start - 1, rows.size)
    below = pl.ds(rows.start + 1, rows.size)
    here = ref[t, rows, :]
    lane = lane_ids(here.shape)
    west = pltpu.roll(jnp.where(lane == LANES - 1, ref[left, rows, :], here), 1, 1)
    east = pltpu.roll(jnp.where(lane == 0, ref[right, rows, :], here), LANES - 1, 1)
    return here, (ref[t, above, :] + ref[t, below, :]) + (west + east)


def first_half(tile, field, half, sign, blocks):
    fr, fi = field
    hr, hi = half

    def body(t, left, right, rows, mask):
        real, beside_real = beside(fr, t, left, right, rows)
        imag, beside_imag = beside(fi, t, left, right, rows)
        hr[t, rows, :] = mask(beside_real + (2.0 * sign) * imag)
        hi[t, rows, :] = mask(beside_imag - (2.0 * sign) * real)

    tile.sweep(body, blocks)


def second_half(tile, field, half, blocks, use):
    fr, fi = field
    hr, hi = half

    def body(t, left, right, rows, mask):
        _, beside_real = beside(hr, t, left, right, rows)
        _, beside_imag = beside(hi, t, left, right, rows)
        use(t, rows, mask, 0.1 * beside_real - fr[t, rows, :], 0.1 * beside_imag - fi[t, rows, :])

    tile.sweep(body, blocks)


def gradient_kernel(sizes, place_ref, angles_ref, scale_ref, phase_ref, target_ref, out_ref,
                    c0, s0, c1, s1, w0r, w0i, w1r, w1i, gr, gi, hr, hi, row_r, row_i, col_r, col_i):
    stripe, tiles, illums, total_rows, total_cols = sizes
    row_first, col_first = place_ref[0], place_ref[1]
    width = (tiles - 1) * LANES
    top = jnp.where(row_first == 0, 0.0, 1.0).astype(F32)
    bottom = jnp.where(row_first + stripe == total_rows, 0.0, 1.0).astype(F32)
    lane = lane_ids((1, LANES))
    in_west = (lane >= LANES - RIM) & (col_first > 0)
    in_east = (lane < RIM) & (col_first + width < total_cols)
    rim_lanes = jnp.where(in_west | in_east, 1.0, 0.0).astype(F32)
    tile = Tile(stripe, tiles, top, bottom, rim_lanes)
    rows_all = tile.rows
    span = pl.ds(RIM, rows_all)

    for ref in (w0r, w0i, w1r, w1i, gr, gi, hr, hi):
        ref[:, 0:RIM, :] = jnp.zeros((tiles, RIM, LANES), F32)
        ref[:, rows_all + RIM :, :] = jnp.zeros((tiles, RIM, LANES), F32)
    out_ref[...] = jnp.zeros(out_ref.shape, F32)

    def trig(t, carry):
        here = pl.ds(pl.multiple_of(t * LANES, LANES), LANES)
        for k, (c, s) in enumerate(((c0, s0), (c1, s1))):
            s[t, span, :], c[t, span, :] = sine_cosine(phase_ref[k, :, here])
        return carry

    lax.fori_loop(0, tiles, trig, 0)

    def illum(j, carry):
        tilt_x, tilt_y = angles_ref[j, 0].astype(F32), angles_ref[j, 1].astype(F32)
        scale = scale_ref[j]
        ids = lax.broadcasted_iota(jnp.int32, (rows_all, LANES), 0) + (row_first - RIM)
        s, c = sine_cosine_of_turns(ids.astype(F32) * tilt_x / total_rows)
        row_r[...] = (-7.0 * c - 24.0 * s) * 0.04
        row_i[...] = (-7.0 * s + 24.0 * c) * 0.04
        at = lax.broadcasted_iota(jnp.int32, (col_r.shape[0], LANES), 0)
        on = lane_ids((col_r.shape[0], LANES))
        ids = col_first + at * LANES + on
        ids = jnp.where((at >= tiles - 1) & (on >= LANES // 2), col_first - LANES + on, ids)
        col_i[...], col_r[...] = sine_cosine_of_turns(ids.astype(F32) * tilt_y / total_cols)

        def start(t, left, right, rows, mask):
            ar, ai = row_r[pl.ds(rows.start - RIM, rows.size), :], row_i[pl.ds(rows.start - RIM, rows.size), :]
            br, bi = col_r[pl.ds(t, 1), :], col_i[pl.ds(t, 1), :]
            ur, ui = ar * br - ai * bi, ar * bi + ai * br
            c, s = c0[t, rows, :], s0[t, rows, :]
            w0r[t, rows, :] = mask(ur * c - ui * s)
            w0i[t, rows, :] = mask(ur * s + ui * c)

        tile.sweep(start, tile.blocks)
        first_half(tile, (w0r, w0i), (hr, hi), 1.0, tile.blocks)

        def modulate(t, rows, mask, ur, ui):
            c, s = c1[t, rows, :], s1[t, rows, :]
            w1r[t, rows, :] = mask(ur * c - ui * s)
            w1i[t, rows, :] = mask(ur * s + ui * c)

        second_half(tile, (w0r, w0i), (hr, hi), tile.blocks, modulate)
        first_half(tile, (w1r, w1i), (hr, hi), 1.0, tile.blocks)

        def residual(t, rows, mask, ur, ui):
            here = pl.ds(t * LANES if isinstance(t, int) else pl.multiple_of(t * LANES, LANES), LANES)
            at = pl.ds(rows.start - RIM, rows.size)
            gr[t, rows, :] = mask(ur - target_ref[j, 0, at, here])
            gi[t, rows, :] = mask(ui - target_ref[j, 1, at, here])

        second_half(tile, (w1r, w1i), (hr, hi), tile.blocks, residual)
        first_half(tile, (gr, gi), (hr, hi), -1.0, tile.blocks)

        def put(k, t, rows, value):
            here = pl.ds(t * LANES if isinstance(t, int) else pl.multiple_of(t * LANES, LANES), LANES)
            at = pl.ds(rows.start - 2 * RIM, rows.size)
            out_ref[k, at, here] = out_ref[k, at, here] + scale * value

        def back(t, rows, mask, ur, ui):
            if not isinstance(t, int) and 2 * RIM <= rows.start < 2 * RIM + stripe:
                put(1, t, rows, ui * w1r[t, rows, :] - ur * w1i[t, rows, :])
            c, s = c1[t, rows, :], s1[t, rows, :]
            gr[t, rows, :] = mask(ur * c + ui * s)
            gi[t, rows, :] = mask(ui * c - ur * s)

        second_half(tile, (gr, gi), (hr, hi), tile.blocks, back)
        first_half(tile, (gr, gi), (hr, hi), -1.0, tile.blocks)

        def last(t, rows, mask, ur, ui):
            if not isinstance(t, int):
                put(0, t, rows, ui * w0r[t, rows, :] - ur * w0i[t, rows, :])

        second_half(tile, (gr, gi), (hr, hi), tile.inner, last)
        return carry

    lax.fori_loop(0, illums, illum, 0)


def halo(x, axis, dim, width, index_of=None):
    peers = lax.axis_size(axis)
    up = [(i, i + 1) for i in range(peers - 1)]
    before = lax.ppermute(lax.slice_in_dim(x, x.shape[dim] - width, x.shape[dim], axis=dim), axis, up)
    after = lax.ppermute(lax.slice_in_dim(x, 0, width, axis=dim), axis, [(j, i) for i, j in up])
    return before, after


def with_column_rims(x, width):
    before, after = halo(x, "col", x.ndim - 1, width)
    gap = jnp.zeros(x.shape[:-1] + (LANES - 2 * width,), x.dtype)
    return jnp.concatenate([x, after, gap, before], axis=-1)


def stripe_halo(x, width):
    illums, rows = lax.axis_size("illum"), lax.axis_size("row")
    where = [(s % illums) * rows + s // illums for s in range(illums * rows)]
    up = [(where[s], where[s + 1]) for s in range(illums * rows - 1)]
    before = lax.ppermute(x[:, -width:], ("illum", "row"), up)
    after = lax.ppermute(x[:, :width], ("illum", "row"), [(b, a) for a, b in up])
    return jnp.concatenate([before, x, after], axis=1)


def per_device(phase_delay, angles, measured):
    illums = lax.axis_size("illum")
    slices, stripe, width = phase_delay.shape
    tile_rows = measured.shape[2]
    total_rows, total_cols = tile_rows * lax.axis_size("row"), width * lax.axis_size("col")
    tiles = width // LANES + 1
    row_first = lax.axis_index("row") * tile_rows + lax.axis_index("illum") * stripe
    col_first = lax.axis_index("col") * width

    target = measured[:, 0].astype(F32)
    energy = lax.psum(jnp.sum(target * target).reshape(1), ("row", "col"))
    energies = lax.all_gather(energy, "illum", tiled=True) / (total_rows * total_cols) + EPS_ENERGY
    tilts = lax.all_gather(angles, "illum", tiled=True)

    phase = with_column_rims(stripe_halo(phase_delay, RIM), RIM)
    above, below = halo(target, "row", 1, REACH)
    target = with_column_rims(jnp.concatenate([above, target, below], axis=1), REACH)
    windows = jnp.stack([target[:, i * stripe : (i + 1) * stripe + 2 * REACH] for i in range(illums)])
    windows = lax.all_to_all(windows, "illum", 0, 0, tiled=True)
    windows = jnp.pad(windows, ((0, 0), (0, 0), (RIM - REACH, RIM - REACH), (0, 0)))

    field = pltpu.VMEM((tiles, stripe + 4 * RIM, LANES), F32)
    rows_all = stripe + 2 * RIM
    return pl.pallas_call(
        functools.partial(gradient_kernel, (stripe, tiles, illums, total_rows, total_cols)),
        out_shape=jax.ShapeDtypeStruct(phase_delay.shape, F32),
        in_specs=[pl.BlockSpec(memory_space=pltpu.SMEM)] * 3 + [pl.BlockSpec(memory_space=pltpu.VMEM)] * 2,
        out_specs=pl.BlockSpec(memory_space=pltpu.VMEM),
        scratch_shapes=[field] * 12
        + [pltpu.VMEM((rows_all, LANES), F32)] * 2
        + [pltpu.VMEM((-(-tiles // 8) * 8, LANES), F32)] * 2,
        compiler_params=pltpu.CompilerParams(vmem_limit_bytes=48 * 2**20),
    )(jnp.stack([row_first, col_first]), tilts, 2.0 / energies, phase, windows)


def solution(mesh):
    placed = (P(None, ("row", "illum"), "col"), P("illum", None), P(None, "illum", "row", "col"))
    return jax.shard_map(
        per_device,
        mesh=mesh,
        in_specs=placed,
        out_specs=P(None, ("row", "illum"), "col"),
        check_vma=False,
    )
```

```python
import functools
import math

import jax
import jax.numpy as jnp
from jax import lax
from jax.experimental import pallas as pl
from jax.experimental.pallas import tpu as pltpu
from jax.sharding import PartitionSpec as P

EPS_ENERGY = 1e-06
RIM = 8
REACH = 4
LANES = 128
F32 = jnp.float32


def sine_cosine(x):
    y = x * x
    s = -2.5052108385441718e-08
    for c in (2.7557319223985893e-06, -1.9841269841269841e-04, 8.333333333333333e-03, -1.6666666666666666e-01):
        s = s * y + c
    c_ = -2.7557319223985888e-07
    for c in (2.48015873015873e-05, -1.3888888888888889e-03, 4.1666666666666664e-02, -0.5, 1.0):
        c_ = c_ * y + c
    return x + x * y * s, c_


def sine_cosine_of_turns(turns):
    quarters = 4.0 * (turns - jnp.floor(turns))
    nearest = jnp.floor(quarters + 0.5)
    s, c = sine_cosine((quarters - nearest) * (0.5 * math.pi))
    odd = (nearest == 1.0) | (nearest == 3.0)
    s, c = jnp.where(odd, c, s), jnp.where(odd, s, c)
    s = jnp.where((nearest == 2.0) | (nearest == 3.0), -s, s)
    c = jnp.where((nearest == 1.0) | (nearest == 2.0), -c, c)
    return s, c


def lane_ids(shape):
    return lax.broadcasted_iota(jnp.int32, shape, len(shape) - 1)


class Tile:
    def __init__(self, stripe, tiles, top, bottom, rim_lanes):
        self.stripe, self.tiles = stripe, tiles
        self.rows = stripe + 2 * RIM
        self.top, self.bottom, self.rim_lanes = top, bottom, rim_lanes
        step = 32 if stripe % 32 == 0 else 8
        self.inner = [(2 * RIM + r, step, None) for r in range(0, stripe, step)]
        self.blocks = [(RIM, RIM, top)] + self.inner + [(2 * RIM + stripe, RIM, bottom)]

    def sweep(self, body, blocks):
        for t in range(self.tiles):
            last = t == self.tiles - 1
            for first, count, factor in blocks:

                def mask(x, factor=factor, last=last):
                    x = x if factor is None else x * factor
                    return x * self.rim_lanes if last else x

                body(t, (t - 1) % self.tiles, (t + 1) % self.tiles, pl.ds(first, count), mask)


def beside(ref, t, left, right, rows):
    above = pl.ds(rows.start - 1, rows.size)
    below = pl.ds(rows.start + 1, rows.size)
    here = ref[t, rows, :]
    lane = lane_ids(here.shape)
    west = pltpu.roll(jnp.where(lane == LANES - 1, ref[left, rows, :], here), 1, 1)
    east = pltpu.roll(jnp.where(lane == 0, ref[right, rows, :], here), LANES - 1, 1)
    return here, (ref[t, above, :] + ref[t, below, :]) + (west + east)


def first_half(tile, field, half, sign, blocks):
    fr, fi = field
    hr, hi = half

    def body(t, left, right, rows, mask):
        real, beside_real = beside(fr, t, left, right, rows)
        imag, beside_imag = beside(fi, t, left, right, rows)
        hr[t, rows, :] = mask(beside_real + (2.0 * sign) * imag)
        hi[t, rows, :] = mask(beside_imag - (2.0 * sign) * real)

    tile.sweep(body, blocks)


def second_half(tile, field, half, blocks, use):
    fr, fi = field
    hr, hi = half

    def body(t, left, right, rows, mask):
        _, beside_real = beside(hr, t, left, right, rows)
        _, beside_imag = beside(hi, t, left, right, rows)
        use(t, rows, mask, 0.1 * beside_real - fr[t, rows, :], 0.1 * beside_imag - fi[t, rows, :])

    tile.sweep(body, blocks)


def blank_rims(refs, tile):
    for ref in refs:
        for first in (0, tile.rows + RIM):
            ref[:, first : first + RIM, :] = jnp.zeros((tile.tiles, RIM, LANES), F32)


def incident_tables(tile, tilts, row_first, col_first, total_rows, total_cols, tables):
    row_r, row_i, col_r, col_i = tables
    ids = lax.broadcasted_iota(jnp.int32, (tile.rows, LANES), 0) + (row_first - RIM)
    s, c = sine_cosine_of_turns(ids.astype(F32) * tilts[0] / total_rows)
    row_r[...] = (-7.0 * c - 24.0 * s) * 0.04
    row_i[...] = (-7.0 * s + 24.0 * c) * 0.04
    at = lax.broadcasted_iota(jnp.int32, col_r.shape, 0)
    on = lane_ids(col_r.shape)
    ids = col_first + at * LANES + on
    ids = jnp.where((at >= tile.tiles - 1) & (on >= LANES // 2), col_first - LANES + on, ids)
    col_i[...], col_r[...] = sine_cosine_of_turns(ids.astype(F32) * tilts[1] / total_cols)


def enter(tile, tables, trig, field):
    row_r, row_i, col_r, col_i = tables
    fr, fi = field

    def start(t, left, right, rows, mask):
        at = pl.ds(rows.start - RIM, rows.size)
        ar, ai = row_r[at, :], row_i[at, :]
        br, bi = col_r[t : t + 1, :], col_i[t : t + 1, :]
        ur, ui = ar * br - ai * bi, ar * bi + ai * br
        c, s = trig[0][t, rows, :], trig[1][t, rows, :]
        fr[t, rows, :] = mask(ur * c - ui * s)
        fi[t, rows, :] = mask(ur * s + ui * c)

    tile.sweep(start, tile.blocks)


def modulate_into(trig, field):
    def use(t, rows, mask, ur, ui):
        c, s = trig[0][t, rows, :], trig[1][t, rows, :]
        field[0][t, rows, :] = mask(ur * c - ui * s)
        field[1][t, rows, :] = mask(ur * s + ui * c)

    return use


def backward(tile, adjoint, half, w0, w1, trig1, put):
    gr, gi = adjoint
    own_tiles = tile.tiles - 1
    inner = [first for first, _, _ in tile.inner]

    def back(t, rows, mask, ur, ui):
        if t < own_tiles and rows.start in inner:
            put(1, t, rows, ui * w1[0][t, rows, :] - ur * w1[1][t, rows, :])
        c, s = trig1[0][t, rows, :], trig1[1][t, rows, :]
        gr[t, rows, :] = mask(ur * c + ui * s)
        gi[t, rows, :] = mask(ui * c - ur * s)

    def last(t, rows, mask, ur, ui):
        if t < own_tiles:
            put(0, t, rows, ui * w0[0][t, rows, :] - ur * w0[1][t, rows, :])

    first_half(tile, adjoint, half, -1.0, tile.blocks)
    second_half(tile, adjoint, half, tile.blocks, back)
    first_half(tile, adjoint, half, -1.0, tile.blocks)
    second_half(tile, adjoint, half, tile.inner, last)


def own_columns(t):
    return slice(t * LANES, (t + 1) * LANES)


def own_rows(rows):
    return slice(rows.start - 2 * RIM, rows.start - 2 * RIM + rows.size)


def gradient_kernel(sizes, place_ref, angles_ref, scale_ref, phase_ref, target_ref, out_ref,
                    c0, s0, c1, s1, w0r, w0i, w1r, w1i, gr, gi, hr, hi, row_r, row_i, col_r, col_i):
    stripe, tiles, illums, total_rows, total_cols = sizes
    row_first, col_first = place_ref[0], place_ref[1]
    tile = Tile(stripe, tiles, *edges_of(row_first, col_first, stripe, tiles, total_rows, total_cols))
    blank_rims((w0r, w0i, w1r, w1i, gr, gi, hr, hi), tile)
    out_ref[...] = jnp.zeros(out_ref.shape, F32)
    span = slice(RIM, RIM + tile.rows)
    for t in range(tiles):
        for k, (c, s) in enumerate(((c0, s0), (c1, s1))):
            s[t, span, :], c[t, span, :] = sine_cosine(phase_ref[k, :, own_columns(t)])
    tables, half = (row_r, row_i, col_r, col_i), (hr, hi)

    def illum(j, carry):
        tilts = angles_ref[j, 0].astype(F32), angles_ref[j, 1].astype(F32)
        incident_tables(tile, tilts, row_first, col_first, total_rows, total_cols, tables)
        enter(tile, tables, (c0, s0), (w0r, w0i))
        first_half(tile, (w0r, w0i), half, 1.0, tile.blocks)
        second_half(tile, (w0r, w0i), half, tile.blocks, modulate_into((c1, s1), (w1r, w1i)))
        first_half(tile, (w1r, w1i), half, 1.0, tile.blocks)

        def residual(t, rows, mask, ur, ui):
            at = slice(rows.start - RIM, rows.start - RIM + rows.size)
            gr[t, rows, :] = mask(ur - target_ref[j, 0, at, own_columns(t)])
            gi[t, rows, :] = mask(ui - target_ref[j, 1, at, own_columns(t)])

        second_half(tile, (w1r, w1i), half, tile.blocks, residual)

        def put(k, t, rows, value):
            at = (k, own_rows(rows), own_columns(t))
            out_ref[at] = out_ref[at] + scale_ref[j] * value

        backward(tile, (gr, gi), half, (w0r, w0i), (w1r, w1i), (c1, s1), put)
        return carry

    lax.fori_loop(0, illums, illum, 0)


def edges_of(row_first, col_first, stripe, tiles, total_rows, total_cols):
    width = (tiles - 1) * LANES
    top = jnp.where(row_first == 0, 0.0, 1.0).astype(F32)
    bottom = jnp.where(row_first + stripe == total_rows, 0.0, 1.0).astype(F32)
    lane = lane_ids((1, LANES))
    in_west = (lane >= LANES - RIM) & (col_first > 0)
    in_east = (lane < RIM) & (col_first + width < total_cols)
    return top, bottom, jnp.where(in_west | in_east, 1.0, 0.0).astype(F32)


def pack_rows(real, imag, low):
    first = lax.broadcasted_iota(jnp.int32, real.shape, 0) < 4
    if low:
        return jnp.where(first, real, pltpu.roll(imag, 4, 0))
    return jnp.where(first, pltpu.roll(real, 4, 0), imag)


def unpack_rows(packed, low):
    turned = pltpu.roll(packed, 4, 0)
    return (packed, turned) if low else (turned, packed)


def edge_blocks(measured_ref, first):
    base = first // 16 * 16
    at = first - base
    return [measured_ref[p, 0, base : base + 16, :].astype(F32)[at : at + 8] for p in range(2)]


def energy_kernel(place_ref, tilt_ref, measured_ref, note_ref):
    rows, cols = measured_ref.shape[2:]
    total = jnp.zeros((8, cols), F32)
    for p in range(2):
        for r in range(0, rows, 16):
            x = measured_ref[p, 0, r : r + 16, :].astype(F32)
            x = x * x
            total = total + (x[:8] + x[8:])
    energy = jnp.sum(jnp.sum(total, axis=1, keepdims=True), axis=0, keepdims=True)
    lane = lane_ids((8, LANES))
    note = jnp.where(lane == place_ref[0] * 4 + place_ref[1], energy, 0.0)
    note = jnp.where(lane == 16, tilt_ref[0, 0].astype(F32), note)
    note_ref[...] = jnp.where(lane == 17, tilt_ref[0, 1].astype(F32), note)


def send_kernel(place_ref, phase_ref, measured_ref, swap_ref, along_ref, same_ref):
    stripe, width = phase_ref.shape[1:]
    rows = 2 * stripe

    def fill(other, near, low, phase_from, along, along_low, same, same_low):
        for p in range(2):
            for r in range(0, stripe, 16):
                swap_ref[p * stripe + r : p * stripe + r + 16, :] = measured_ref[p, 0, other + r : other + r + 16, :].astype(F32)
        swap_ref[rows:, :] = pack_rows(*edge_blocks(measured_ref, near), low)
        for k in range(2):
            along_ref[:, k * width : (k + 1) * width] = phase_ref[k, phase_from : phase_from + 8, :]
        along_ref[:, 2 * width :] = pack_rows(*edge_blocks(measured_ref, along), along_low)
        same_ref[...] = pack_rows(*edge_blocks(measured_ref, same), same_low)

    @pl.when(place_ref[0] == 0)
    def _():
        fill(stripe, stripe - 8, False, 0, 0, True, rows - 8, False)

    @pl.when(place_ref[0] == 1)
    def _():
        fill(0, stripe, True, stripe - 8, rows - 8, False, 0, True)


def partner_kernel(place_ref, phase_ref, note_ref, core_note_ref, partner_ref, known_ref):
    stripe, width = phase_ref.shape[1:]
    for which, first in ((0, stripe - 8), (1, 0)):

        @pl.when(place_ref[0] == which)
        def _():
            for k in range(2):
                partner_ref[:, k * width : (k + 1) * width] = phase_ref[k, first : first + 8, :]

    lane = lane_ids((8, LANES))
    known = jnp.where(lane < 16, jnp.maximum(note_ref[...], core_note_ref[...]), note_ref[...])
    partner_ref[:, 2 * width :] = known
    known_ref[...] = known


def same_kernel(packed_ref, known_ref, partner_ref, same_ref):
    width = packed_ref.shape[1]
    same_ref[:, :width] = packed_ref[...]
    same_ref[:, width:] = jnp.maximum(known_ref[...], partner_ref[:, 2 * width :])


def rim_pack_kernel(place_ref, phase_ref, measured_ref, known_ref, partner_ref, along_ref, same_ref, out_ref):
    stripe, width = phase_ref.shape[1:]
    rows = 2 * stripe
    low_illum = place_ref[0] == 0
    col, cols = place_ref[2], out_ref.shape[0]
    lane = lane_ids((8, LANES))
    known = jnp.maximum(jnp.maximum(known_ref[...], partner_ref[:, 2 * width :]), same_ref[:, width:])
    for c in range(cols):
        out_ref[c, out_ref.shape[1] - 8 :, :] = known

    for east in (True, False):
        edge = slice(width - LANES, width) if east else slice(0, LANES)
        base = LANES - RIM if east else 0

        @pl.when(col < cols - 1 if east else col > 0)
        def _():
            to = col + 1 if east else col - 1
            groups = []
            for j in range(stripe // 8 + 2):
                items = []
                for k in range(2):
                    tile = slice(k * width + edge.start, k * width + edge.stop)
                    if j == 0:
                        items.append(jnp.where(low_illum, along_ref[:, tile], partner_ref[:, tile]))
                    elif j == stripe // 8 + 1:
                        items.append(jnp.where(low_illum, partner_ref[:, tile], along_ref[:, tile]))
                    else:
                        items.append(phase_ref[k, 8 * (j - 1) : 8 * j, edge])
                groups.append(items)
            while len(groups) < rows // 8 + 1:
                groups.append([None, None])
            for r in range(0, rows, 16):
                both = [measured_ref[p, 0, r : r + 16, edge].astype(F32) for p in range(2)]
                for h in range(2):
                    groups[r // 8 + h] += [b[8 * h : 8 * h + 8] for b in both]
            groups[rows // 8] += [same_ref[:, edge], along_ref[:, 2 * width + edge.start : 2 * width + edge.stop]]
            for g in range(0, len(groups), 4):
                acc = jnp.zeros((8, LANES), F32)
                for q, items in enumerate(groups[g : g + 4]):
                    for k, item in enumerate(items):
                        if item is not None:
                            slot = 4 * q + k
                            shift = (8 * slot - base) % LANES
                            moved = pltpu.roll(item, shift, 1) if shift else item
                            acc = jnp.where((lane >= 8 * slot) & (lane < 8 * slot + 8), moved, acc)
                out_ref[to, 2 * g : 2 * g + 8, :] = acc


def rim_unpack_kernel(place_ref, got_ref, phase_rim_ref, rim_ref, relay_ref):
    cols, depth = got_ref.shape[:2]
    stripe = phase_rim_ref.shape[1] - 2 * RIM
    rows = 2 * stripe
    col = place_ref[2]
    west, east = jnp.maximum(col - 1, 0), jnp.minimum(col + 1, cols - 1)
    lane = lane_ids((8, LANES))
    in_west = (lane >= LANES - RIM) & (col > 0)
    in_east = (lane < RIM) & (col < cols - 1)
    for g in range(0, rows // 8 + 1, 4):
        a, b = got_ref[west, 2 * g : 2 * g + 8, :], got_ref[east, 2 * g : 2 * g + 8, :]
        for j in range(g, min(g + 4, rows // 8 + 1)):
            for k in range(4):
                if k < 2 and j >= stripe // 8 + 2:
                    continue
                slot = 4 * (j - g) + k
                from_west = pltpu.roll(a, (LANES - RIM - 8 * slot) % LANES, 1)
                from_east = pltpu.roll(b, (-8 * slot) % LANES, 1) if slot else b
                item = jnp.where(in_west, from_west, jnp.where(in_east, from_east, 0.0))
                (phase_rim_ref if k < 2 else rim_ref)[k % 2, 8 * j : 8 * j + 8, :] = item
    for which, other, near in ((0, stripe, stripe - 8), (1, 0, stripe)):

        @pl.when(place_ref[0] == which)
        def _():
            for r in range(0, stripe, 8):
                at = slice(other + r, other + r + 8)
                relay_ref[r : r + 8, :] = rim_ref[0, at, :] + pltpu.roll(rim_ref[1, at, :], LANES // 2, 1)
            at = slice(near, near + 8)
            relay_ref[stripe : stripe + 8, :] = rim_ref[0, at, :] + pltpu.roll(rim_ref[1, at, :], LANES // 2, 1)

    total = got_ref[0, depth - 8 :, :]
    for c in range(1, cols):
        total = total + got_ref[c, depth - 8 :, :]
    relay_ref[stripe + 8 :, :] = total


def tile_of(place_ref, sizes):
    stripe, tiles, total_rows, total_cols = sizes
    row_first = (place_ref[1] * 2 + place_ref[0]) * stripe
    col_first = place_ref[2] * (tiles - 1) * LANES
    edges = edges_of(row_first, col_first, stripe, tiles, total_rows, total_cols)
    return Tile(stripe, tiles, *edges), row_first, col_first


def fill_target(tile, target, low_illum, middle, near, far):
    end = 2 * RIM + tile.stripe
    for t in range(tile.tiles):
        beside_rows, packed = near(t), far(t)
        for part, ref in enumerate(target):
            for r in range(0, tile.stripe, 16):
                ref[t, 2 * RIM + r : 2 * RIM + r + 16, :] = middle(part, t, r)
            ref[t, RIM : 2 * RIM, :] = jnp.where(low_illum, unpack_rows(packed, False)[part], beside_rows[part])
            ref[t, end : end + RIM, :] = jnp.where(low_illum, beside_rows[part], unpack_rows(packed, True)[part])


def forward_kernel(sizes, place_ref, phase_ref, measured_ref, known_ref, partner_ref, along_ref, same_ref, phase_rim_ref, rim_ref,
                   own_ref, o0r, o0i, o1r, o1i, o2r, o2i, c1, s1,
                   c0, s0, w0r, w0i, w1r, w1i, gr, gi, hr, hi, mr, mi, row_r, row_i, col_r, col_i):
    stripe, tiles, total_rows, total_cols = sizes
    tile, row_first, col_first = tile_of(place_ref, sizes)
    width = (tiles - 1) * LANES
    low_illum = place_ref[0] == 0
    blank_rims((w0r, w0i, w1r, w1i, gr, gi, hr, hi, o0r, o0i, o1r, o1i), tile)

    for t in range(tiles):
        for k, (c, s) in enumerate(((c0, s0), (c1, s1))):
            if t < tiles - 1:
                at = own_columns(t + k * (tiles - 1))
                far, near = along_ref[:, at], partner_ref[:, at]
                here = [(RIM, jnp.where(low_illum, far, near)), (2 * RIM + stripe, jnp.where(low_illum, near, far))]
                here += [(2 * RIM + r, phase_ref[k, r : r + 16, own_columns(t)]) for r in range(0, stripe, 16)]
            else:
                here = [(RIM + r, phase_rim_ref[k, r : r + 16, :]) for r in range(0, tile.rows, 16)]
            for first, x in here:
                s[t, first : first + x.shape[0], :], c[t, first : first + x.shape[0], :] = sine_cosine(x)

    mine = place_ref[0] * stripe
    near_base = pl.multiple_of(stripe - 16 * place_ref[0], 16)
    near_rim = pl.multiple_of(stripe - 8 * place_ref[0], 8)

    def middle(part, t, r):
        at = pl.ds(pl.multiple_of(mine + r, 16), 16)
        if t < tiles - 1:
            return measured_ref[part, 0, at, own_columns(t)].astype(F32)
        return rim_ref[part, at, :]

    def near(t):
        if t < tiles - 1:
            both = [measured_ref[part, 0, pl.ds(near_base, 16), own_columns(t)].astype(F32) for part in range(2)]
            return [jnp.where(low_illum, x[:8], x[8:]) for x in both]
        return [rim_ref[part, pl.ds(near_rim, 8), :] for part in range(2)]

    def far(t):
        return same_ref[:, own_columns(t)] if t < tiles - 1 else rim_ref[0, 2 * stripe :, :]

    fill_target(tile, (mr, mi), low_illum, middle, near, far)

    lane = lane_ids((8, LANES))

    def tilts(note):
        return [jnp.sum(jnp.where(lane == n, note, 0.0)[:1], axis=1, keepdims=True) for n in (16, 17)]

    tables, half = (row_r, row_i, col_r, col_i), (hr, hi)
    trig0, trig1 = (c0, s0), (c1, s1)

    def forward(note, w0, w1, use):
        incident_tables(tile, tilts(note), row_first, col_first, total_rows, total_cols, tables)
        enter(tile, tables, trig0, w0)
        first_half(tile, w0, half, 1.0, tile.blocks)
        second_half(tile, w0, half, tile.blocks, modulate_into(trig1, w1))
        first_half(tile, w1, half, 1.0, tile.blocks)
        second_half(tile, w1, half, tile.blocks, use)

    def keep(t, rows, mask, ur, ui):
        o2r[t, rows, :] = ur
        o2i[t, rows, :] = ui

    def residual(t, rows, mask, ur, ui):
        gr[t, rows, :] = mask(ur - mr[t, rows, :])
        gi[t, rows, :] = mask(ui - mi[t, rows, :])

    def put(k, t, rows, value):
        own_ref[k, own_rows(rows), own_columns(t)] = value

    forward(partner_ref[:, 2 * width :], (o0r, o0i), (o1r, o1i), keep)
    forward(known_ref[...], (w0r, w0i), (w1r, w1i), residual)
    backward(tile, (gr, gi), half, (w0r, w0i), (w1r, w1i), trig1, put)


def finish_kernel(sizes, place_ref, own_ref, swap_ref, along_ref, rim_ref, relay_ref, partner_relay_ref,
                  w0r, w0i, w1r, w1i, ur_ref, ui_ref, c1, s1, out_ref, gr, gi, hr, hi, mr, mi):
    stripe, tiles, total_rows, total_cols = sizes
    tile, _, _ = tile_of(place_ref, sizes)
    width = (tiles - 1) * LANES
    low_illum = place_ref[0] == 0
    blank_rims((gr, gi, hr, hi), tile)

    lane = lane_ids((8, LANES))
    sums = jnp.maximum(relay_ref[stripe + 8 :, :], partner_relay_ref[stripe + 8 :, :])
    scales = []
    for which in range(2):
        here = jnp.where((lane >= 4 * which) & (lane < 4 * which + 4), sums, 0.0)
        energy = jnp.sum(here[:1], axis=1, keepdims=True) / (total_rows * total_cols) + EPS_ENERGY
        scales.append(2.0 / energy)
    mine = jnp.where(low_illum, scales[0], scales[1])
    others = jnp.where(low_illum, scales[1], scales[0])

    def middle(part, t, r):
        if t < tiles - 1:
            return swap_ref[part * stripe + r : part * stripe + r + 16, own_columns(t)]
        x = partner_relay_ref[r : r + 16, :]
        return pltpu.roll(x, LANES // 2, 1) if part else x

    def near(t):
        if t < tiles - 1:
            packed = swap_ref[2 * stripe :, own_columns(t)]
            high, low = unpack_rows(packed, False), unpack_rows(packed, True)
            return [jnp.where(low_illum, low[part], high[part]) for part in range(2)]
        x = partner_relay_ref[stripe : stripe + 8, :]
        return [x, pltpu.roll(x, LANES // 2, 1)]

    def far(t):
        return along_ref[:, own_columns(t + 2 * (tiles - 1))] if t < tiles - 1 else rim_ref[1, 2 * stripe :, :]

    fill_target(tile, (mr, mi), low_illum, middle, near, far)

    def residual(t, left, right, rows, mask):
        gr[t, rows, :] = mask(ur_ref[t, rows, :] - mr[t, rows, :])
        gi[t, rows, :] = mask(ui_ref[t, rows, :] - mi[t, rows, :])

    tile.sweep(residual, tile.blocks)

    def put(k, t, rows, value):
        at = (k, own_rows(rows), own_columns(t))
        out_ref[at] = own_ref[at] * mine + value * others

    backward(tile, (gr, gi), (hr, hi), (w0r, w0i), (w1r, w1i), (c1, s1), put)


def call(kernel, outs, *args, scratch=(), scalars=1, flops=0):
    shapes = [jax.ShapeDtypeStruct(shape, F32) for shape in outs]
    return pl.pallas_call(
        kernel,
        out_shape=shapes,
        in_specs=[pl.BlockSpec(memory_space=pltpu.SMEM)] * scalars
        + [pl.BlockSpec(memory_space=pltpu.VMEM)] * (len(args) - scalars),
        out_specs=[pl.BlockSpec(memory_space=pltpu.VMEM)] * len(outs),
        scratch_shapes=[pltpu.VMEM(shape, F32) for shape in scratch],
        compiler_params=pltpu.CompilerParams(vmem_limit_bytes=32 * 2**20),
        cost_estimate=pl.CostEstimate(flops=flops, bytes_accessed=2**20, transcendentals=0),
    )(*args)


def paired(phase_delay, angles, measured):
    slices, stripe, width = phase_delay.shape
    rows, cols = lax.axis_size("row"), lax.axis_size("col")
    tiles = width // LANES + 1
    sizes = (stripe, tiles, 2 * stripe * rows, width * cols)
    place = jnp.stack([lax.axis_index("illum"), lax.axis_index("row"), lax.axis_index("col")])
    swap = [(0, 1), (1, 0)]
    along = []
    for r in range(rows - 1):
        along += [(rows + r, r + 1), (r + 1, rows + r)]
    same = [(r, (r + 1) % rows) for r in range(rows)] + [(rows + (r + 1) % rows, rows + r) for r in range(rows)]

    (note,) = call(energy_kernel, [(8, LANES)], place, angles, measured, scalars=2)
    core_note = lax.ppermute(note, "row", [(r, r ^ 1) for r in range(rows)])
    swap_out, along_out, same_packed = call(
        send_kernel, [(2 * stripe + 8, width), (8, 3 * width), (8, width)], place, phase_delay, measured
    )
    partner_out, known = call(partner_kernel, [(8, 2 * width + LANES), (8, LANES)], place, phase_delay, note, core_note)
    partner_in = lax.ppermute(partner_out, "illum", swap)
    along_in = lax.ppermute(along_out, ("illum", "row"), along)
    swap_in = lax.ppermute(swap_out, "illum", swap)
    (same_out,) = call(same_kernel, [(8, width + LANES)], same_packed, known, partner_in, scalars=0)
    same_in = lax.ppermute(same_out, ("illum", "row"), same)
    depth = 8 * (-(-(stripe // 4 + 1) // 4)) + 8
    (rims_out,) = call(
        rim_pack_kernel, [(cols, depth, LANES)], place, phase_delay, measured, known, partner_in, along_in, same_in
    )
    rims_in = lax.all_to_all(rims_out, "col", 0, 0, tiled=True)
    phase_rim, rim, relay = call(
        rim_unpack_kernel,
        [(2, stripe + 2 * RIM, LANES), (2, 2 * stripe + 8, LANES), (stripe + 16, LANES)],
        place, rims_in,
    )
    partner_relay = lax.ppermute(relay, "illum", swap)

    field = (tiles, stripe + 4 * RIM, LANES)
    tables = [(stripe + 2 * RIM, LANES)] * 2 + [(-(-tiles // 8) * 8, LANES)] * 2
    own, *kept = call(
        functools.partial(forward_kernel, sizes),
        [phase_delay.shape] + [field] * 8,
        place, phase_delay, measured, known, partner_in, along_in, same_in, phase_rim, rim,
        scratch=[field] * 12 + tables, flops=10**9,
    )
    (out,) = call(
        functools.partial(finish_kernel, sizes),
        [phase_delay.shape],
        place, own, swap_in, along_in, rim, relay, partner_relay, *kept,
        scratch=[field] * 6,
    )
    return out


def halo(x, axis, dim, width, index_of=None):
    peers = lax.axis_size(axis)
    up = [(i, i + 1) for i in range(peers - 1)]
    before = lax.ppermute(lax.slice_in_dim(x, x.shape[dim] - width, x.shape[dim], axis=dim), axis, up)
    after = lax.ppermute(lax.slice_in_dim(x, 0, width, axis=dim), axis, [(j, i) for i, j in up])
    return before, after


def with_column_rims(x, width):
    before, after = halo(x, "col", x.ndim - 1, width)
    gap = jnp.zeros(x.shape[:-1] + (LANES - 2 * width,), x.dtype)
    return jnp.concatenate([x, after, gap, before], axis=-1)


def stripe_halo(x, width):
    illums, rows = lax.axis_size("illum"), lax.axis_size("row")
    where = [(s % illums) * rows + s // illums for s in range(illums * rows)]
    up = [(where[s], where[s + 1]) for s in range(illums * rows - 1)]
    before = lax.ppermute(x[:, -width:], ("illum", "row"), up)
    after = lax.ppermute(x[:, :width], ("illum", "row"), [(b, a) for a, b in up])
    return jnp.concatenate([before, x, after], axis=1)


def per_device(phase_delay, angles, measured):
    illums = lax.axis_size("illum")
    if illums == 2 and lax.axis_size("row") == 4:
        return paired(phase_delay, angles, measured)
    slices, stripe, width = phase_delay.shape
    tile_rows = measured.shape[2]
    total_rows, total_cols = tile_rows * lax.axis_size("row"), width * lax.axis_size("col")
    tiles = width // LANES + 1
    row_first = lax.axis_index("row") * tile_rows + lax.axis_index("illum") * stripe
    col_first = lax.axis_index("col") * width

    target = measured[:, 0].astype(F32)
    energy = lax.psum(jnp.sum(target * target).reshape(1), ("row", "col"))
    energies = lax.all_gather(energy, "illum", tiled=True) / (total_rows * total_cols) + EPS_ENERGY
    tilts = lax.all_gather(angles, "illum", tiled=True)

    phase = with_column_rims(stripe_halo(phase_delay, RIM), RIM)
    above, below = halo(target, "row", 1, REACH)
    target = with_column_rims(jnp.concatenate([above, target, below], axis=1), REACH)
    windows = jnp.stack([target[:, i * stripe : (i + 1) * stripe + 2 * REACH] for i in range(illums)])
    windows = lax.all_to_all(windows, "illum", 0, 0, tiled=True)
    windows = jnp.pad(windows, ((0, 0), (0, 0), (RIM - REACH, RIM - REACH), (0, 0)))

    field = pltpu.VMEM((tiles, stripe + 4 * RIM, LANES), F32)
    rows_all = stripe + 2 * RIM
    return pl.pallas_call(
        functools.partial(gradient_kernel, (stripe, tiles, illums, total_rows, total_cols)),
        out_shape=jax.ShapeDtypeStruct(phase_delay.shape, F32),
        in_specs=[pl.BlockSpec(memory_space=pltpu.SMEM)] * 3 + [pl.BlockSpec(memory_space=pltpu.VMEM)] * 2,
        out_specs=pl.BlockSpec(memory_space=pltpu.VMEM),
        scratch_shapes=[field] * 12
        + [pltpu.VMEM((rows_all, LANES), F32)] * 2
        + [pltpu.VMEM((-(-tiles // 8) * 8, LANES), F32)] * 2,
        compiler_params=pltpu.CompilerParams(vmem_limit_bytes=48 * 2**20),
    )(jnp.stack([row_first, col_first]), tilts, 2.0 / energies, phase, windows)


def solution(mesh):
    placed = (P(None, ("row", "illum"), "col"), P("illum", None), P(None, "illum", "row", "col"))
    return jax.shard_map(
        per_device,
        mesh=mesh,
        in_specs=placed,
        out_specs=P(None, ("row", "illum"), "col"),
        check_vma=False,
    )
```

```python
import functools
import math

import jax
import jax.numpy as jnp
from jax import lax
from jax.experimental import pallas as pl
from jax.experimental.pallas import tpu as pltpu
from jax.sharding import PartitionSpec as P

EPS_ENERGY = 1e-06
RIM = 8
REACH = 4
LANES = 128
F32 = jnp.float32


def sine_cosine(x):
    y = x * x
    s = -2.5052108385441718e-08
    for c in (2.7557319223985893e-06, -1.9841269841269841e-04, 8.333333333333333e-03, -1.6666666666666666e-01):
        s = s * y + c
    c_ = -2.7557319223985888e-07
    for c in (2.48015873015873e-05, -1.3888888888888889e-03, 4.1666666666666664e-02, -0.5, 1.0):
        c_ = c_ * y + c
    return x + x * y * s, c_


def sine_cosine_of_turns(turns):
    quarters = 4.0 * (turns - jnp.floor(turns))
    nearest = jnp.floor(quarters + 0.5)
    s, c = sine_cosine((quarters - nearest) * (0.5 * math.pi))
    odd = (nearest == 1.0) | (nearest == 3.0)
    s, c = jnp.where(odd, c, s), jnp.where(odd, s, c)
    s = jnp.where((nearest == 2.0) | (nearest == 3.0), -s, s)
    c = jnp.where((nearest == 1.0) | (nearest == 2.0), -c, c)
    return s, c


def lane_ids(shape):
    return lax.broadcasted_iota(jnp.int32, shape, len(shape) - 1)


class Tile:
    def __init__(self, stripe, tiles, top, bottom, lanes=None, rim=None):
        self.stripe, self.tiles = stripe, tiles
        self.rows = stripe + 2 * RIM
        self.top, self.bottom, self.lanes, self.rim = top, bottom, lanes, rim
        self.owned = tiles - 1 if rim else tiles
        step = 32 if stripe % 32 == 0 else 8
        self.inner = [(2 * RIM + r, step, None) for r in range(0, stripe, step)]
        self.blocks = [(RIM, RIM, top)] + self.inner + [(2 * RIM + stripe, RIM, bottom)]

    def sweep(self, body, blocks):
        for t in range(self.tiles):
            for first, count, factor in blocks:

                def mask(x, factor=factor, lanes=self.lanes if t == self.rim else None):
                    x = x if factor is None else x * factor
                    return x if lanes is None else x * lanes

                body(t, (t - 1) % self.tiles, (t + 1) % self.tiles, pl.ds(first, count), mask)


def beside(ref, t, left, right, rows):
    above = pl.ds(rows.start - 1, rows.size)
    below = pl.ds(rows.start + 1, rows.size)
    here = ref[t, rows, :]
    lane = lane_ids(here.shape)
    west = pltpu.roll(here if left == t else jnp.where(lane == LANES - 1, ref[left, rows, :], here), 1, 1)
    east = pltpu.roll(here if right == t else jnp.where(lane == 0, ref[right, rows, :], here), LANES - 1, 1)
    return here, (ref[t, above, :] + ref[t, below, :]) + (west + east)


def first_half(tile, field, half, sign, blocks):
    fr, fi = field
    hr, hi = half

    def body(t, left, right, rows, mask):
        real, beside_real = beside(fr, t, left, right, rows)
        imag, beside_imag = beside(fi, t, left, right, rows)
        hr[t, rows, :] = mask(beside_real + (2.0 * sign) * imag)
        hi[t, rows, :] = mask(beside_imag - (2.0 * sign) * real)

    tile.sweep(body, blocks)


def second_half(tile, field, half, blocks, use):
    fr, fi = field
    hr, hi = half

    def body(t, left, right, rows, mask):
        _, beside_real = beside(hr, t, left, right, rows)
        _, beside_imag = beside(hi, t, left, right, rows)
        use(t, rows, mask, 0.1 * beside_real - fr[t, rows, :], 0.1 * beside_imag - fi[t, rows, :])

    tile.sweep(body, blocks)


def blank_rims(refs, tile):
    for ref in refs:
        for first in (0, tile.rows + RIM):
            ref[:, first : first + RIM, :] = jnp.zeros((tile.tiles, RIM, LANES), F32)


def rim_columns(tile, col_first, shape):
    at, on = lax.broadcasted_iota(jnp.int32, shape, 0), lane_ids(shape)
    return col_first + jnp.where((at >= tile.owned) & (on >= LANES // 2), on - LANES, at * LANES + on)


def incident_tables(tile, tilts, row_first, columns, total_rows, total_cols, tables):
    row_r, row_i, col_r, col_i = tables
    ids = lax.broadcasted_iota(jnp.int32, (tile.rows, LANES), 0) + (row_first - RIM)
    s, c = sine_cosine_of_turns(ids.astype(F32) * tilts[0] / total_rows)
    row_r[...] = (-7.0 * c - 24.0 * s) * 0.04
    row_i[...] = (-7.0 * s + 24.0 * c) * 0.04
    col_i[...], col_r[...] = sine_cosine_of_turns(columns.astype(F32) * tilts[1] / total_cols)


def enter(tile, tables, trig, field):
    row_r, row_i, col_r, col_i = tables
    fr, fi = field

    def start(t, left, right, rows, mask):
        at = pl.ds(rows.start - RIM, rows.size)
        ar, ai = row_r[at, :], row_i[at, :]
        br, bi = col_r[t : t + 1, :], col_i[t : t + 1, :]
        ur, ui = ar * br - ai * bi, ar * bi + ai * br
        c, s = trig[0][t, rows, :], trig[1][t, rows, :]
        fr[t, rows, :] = mask(ur * c - ui * s)
        fi[t, rows, :] = mask(ur * s + ui * c)

    tile.sweep(start, tile.blocks)


def modulate_into(trig, field):
    def use(t, rows, mask, ur, ui):
        c, s = trig[0][t, rows, :], trig[1][t, rows, :]
        field[0][t, rows, :] = mask(ur * c - ui * s)
        field[1][t, rows, :] = mask(ur * s + ui * c)

    return use


def backward(tile, adjoint, half, w0, w1, trig1, put):
    gr, gi = adjoint
    inner = [first for first, _, _ in tile.inner]

    def back(t, rows, mask, ur, ui):
        if t < tile.owned and rows.start in inner:
            put(1, t, rows, ui * w1[0][t, rows, :] - ur * w1[1][t, rows, :])
        c, s = trig1[0][t, rows, :], trig1[1][t, rows, :]
        gr[t, rows, :] = mask(ur * c + ui * s)
        gi[t, rows, :] = mask(ui * c - ur * s)

    def last(t, rows, mask, ur, ui):
        if t < tile.owned:
            put(0, t, rows, ui * w0[0][t, rows, :] - ur * w0[1][t, rows, :])

    first_half(tile, adjoint, half, -1.0, tile.blocks)
    second_half(tile, adjoint, half, tile.blocks, back)
    first_half(tile, adjoint, half, -1.0, tile.blocks)
    second_half(tile, adjoint, half, tile.inner, last)


def own_columns(t):
    return slice(t * LANES, (t + 1) * LANES)


def own_rows(rows):
    return slice(rows.start - 2 * RIM, rows.start - 2 * RIM + rows.size)


def gradient_kernel(sizes, place_ref, angles_ref, scale_ref, phase_ref, target_ref, out_ref,
                    c0, s0, c1, s1, w0r, w0i, w1r, w1i, gr, gi, hr, hi, row_r, row_i, col_r, col_i):
    stripe, tiles, illums, total_rows, total_cols = sizes
    row_first, col_first = place_ref[0], place_ref[1]
    edges = edges_of(row_first, col_first, stripe, tiles, total_rows, total_cols)
    tile = Tile(stripe, tiles, *edges, rim=tiles - 1)
    blank_rims((w0r, w0i, w1r, w1i, gr, gi, hr, hi), tile)
    out_ref[...] = jnp.zeros(out_ref.shape, F32)
    span = slice(RIM, RIM + tile.rows)
    for t in range(tiles):
        for k, (c, s) in enumerate(((c0, s0), (c1, s1))):
            s[t, span, :], c[t, span, :] = sine_cosine(phase_ref[k, :, own_columns(t)])
    tables, half = (row_r, row_i, col_r, col_i), (hr, hi)

    def illum(j, carry):
        tilts = angles_ref[j, 0].astype(F32), angles_ref[j, 1].astype(F32)
        incident_tables(tile, tilts, row_first, rim_columns(tile, col_first, col_r.shape), total_rows, total_cols, tables)
        enter(tile, tables, (c0, s0), (w0r, w0i))
        first_half(tile, (w0r, w0i), half, 1.0, tile.blocks)
        second_half(tile, (w0r, w0i), half, tile.blocks, modulate_into((c1, s1), (w1r, w1i)))
        first_half(tile, (w1r, w1i), half, 1.0, tile.blocks)

        def residual(t, rows, mask, ur, ui):
            at = slice(rows.start - RIM, rows.start - RIM + rows.size)
            gr[t, rows, :] = mask(ur - target_ref[j, 0, at, own_columns(t)])
            gi[t, rows, :] = mask(ui - target_ref[j, 1, at, own_columns(t)])

        second_half(tile, (w1r, w1i), half, tile.blocks, residual)

        def put(k, t, rows, value):
            at = (k, own_rows(rows), own_columns(t))
            out_ref[at] = out_ref[at] + scale_ref[j] * value

        backward(tile, (gr, gi), half, (w0r, w0i), (w1r, w1i), (c1, s1), put)
        return carry

    lax.fori_loop(0, illums, illum, 0)


def edges_of(row_first, col_first, stripe, tiles, total_rows, total_cols):
    width = (tiles - 1) * LANES
    top = jnp.where(row_first == 0, 0.0, 1.0).astype(F32)
    bottom = jnp.where(row_first + stripe == total_rows, 0.0, 1.0).astype(F32)
    lane = lane_ids((1, LANES))
    in_west = (lane >= LANES - RIM) & (col_first > 0)
    in_east = (lane < RIM) & (col_first + width < total_cols)
    return top, bottom, jnp.where(in_west | in_east, 1.0, 0.0).astype(F32)


def place():
    return lax.axis_index("illum"), lax.axis_index("row"), lax.axis_index("col")


def pack_rows(real, imag, low):
    first = lax.broadcasted_iota(jnp.int32, real.shape, 0) < 4
    if low:
        return jnp.where(first, real, pltpu.roll(imag, 4, 0))
    return jnp.where(first, pltpu.roll(real, 4, 0), imag)


def unpack_rows(packed, low):
    turned = pltpu.roll(packed, 4, 0)
    return (packed, turned) if low else (turned, packed)


def edge_blocks(measured_ref, first):
    base = first // 16 * 16
    at = first - base
    return [measured_ref[p, 0, base : base + 16, :].astype(F32)[at : at + 8] for p in range(2)]


def open_kernel(phase_ref, measured_ref, note_ref, along_ref, same_ref, held, edge, sems):
    stripe, width = phase_ref.shape[1:]
    rows = 2 * stripe
    illum, row, _ = place()
    first = pl.multiple_of(illum * (stripe - 8), 8)
    field_copy = pltpu.make_async_copy(measured_ref, held, sems.at[0])
    edge_copy = pltpu.make_async_copy(phase_ref.at[:, pl.ds(first, 8), :], edge, sems.at[1])
    edge_copy.start()
    field_copy.start()
    edge_copy.wait()
    for k in range(2):
        along_ref[:, k * width : (k + 1) * width] = edge[k]
    field_copy.wait()
    top, bottom = pack_rows(*edge_blocks(held, 0), True), pack_rows(*edge_blocks(held, rows - 8), False)
    along_ref[:, 2 * width :] = jnp.where(illum == 0, top, bottom)
    same_ref[...] = jnp.where(illum == 0, bottom, top)
    total = jnp.zeros((8, width), F32)
    for p in range(2):
        for r in range(0, rows, 16):
            x = held[p, 0, r : r + 16, :].astype(F32)
            x = x * x
            total = total + (x[:8] + x[8:])
    energy = jnp.sum(jnp.sum(total, axis=1, keepdims=True), axis=0, keepdims=True)
    note_ref[...] = jnp.where(lane_ids((8, LANES)) == illum * 4 + row, energy, 0.0)


def partner_kernel(phase_ref, angles_ref, note_ref, core_note_ref, partner_ref, known_ref):
    stripe, width = phase_ref.shape[1:]
    illum, _, _ = place()
    first = pl.multiple_of((1 - illum) * (stripe - 8), 8)
    for k in range(2):
        partner_ref[:, k * width : (k + 1) * width] = phase_ref[k, pl.ds(first, 8), :]
    lane = lane_ids((8, LANES))
    known = jnp.maximum(note_ref[...], core_note_ref[...])
    for n in range(2):
        known = jnp.where(lane == 16 + n, angles_ref[:, n : n + 1].astype(F32), known)
    partner_ref[:, 2 * width :] = known
    known_ref[...] = known


def swap_kernel(measured_ref, known_ref, swap_ref):
    stripe = measured_ref.shape[2] // 2
    illum, _, _ = place()
    other = pl.multiple_of((1 - illum) * stripe, 16)
    for p in range(2):
        for r in range(0, stripe, 16):
            at = pl.ds(pl.multiple_of(other + r, 16), 16)
            swap_ref[p * stripe + r : p * stripe + r + 16, :] = measured_ref[p, 0, at, :].astype(F32)
    above = pack_rows(*edge_blocks(measured_ref, stripe - 8), False)
    below = pack_rows(*edge_blocks(measured_ref, stripe), True)
    swap_ref[2 * stripe :, :] = jnp.where(illum == 0, above, below)


def same_kernel(packed_ref, known_ref, partner_ref, same_ref):
    width = packed_ref.shape[1]
    same_ref[:, :width] = packed_ref[...]
    same_ref[:, width:] = jnp.maximum(known_ref[...], partner_ref[:, 2 * width :])


def rim_pack_kernel(phase_ref, measured_ref, known_ref, partner_ref, along_ref, same_ref, out_ref):
    stripe, width = phase_ref.shape[1:]
    rows = 2 * stripe
    illum, _, col = place()
    low_illum = illum == 0
    cols = out_ref.shape[0]
    lane = lane_ids((8, LANES))
    known = jnp.maximum(jnp.maximum(known_ref[...], partner_ref[:, 2 * width :]), same_ref[:, width:])
    for c in range(cols):
        out_ref[c, out_ref.shape[1] - 8 :, :] = known

    for east in (True, False):
        edge = slice(width - LANES, width) if east else slice(0, LANES)
        base = LANES - RIM if east else 0

        @pl.when(col < cols - 1 if east else col > 0)
        def _():
            to = col + 1 if east else col - 1
            groups = []
            for j in range(stripe // 8 + 2):
                items = []
                for k in range(2):
                    tile = slice(k * width + edge.start, k * width + edge.stop)
                    if j == 0:
                        items.append(jnp.where(low_illum, along_ref[:, tile], partner_ref[:, tile]))
                    elif j == stripe // 8 + 1:
                        items.append(jnp.where(low_illum, partner_ref[:, tile], along_ref[:, tile]))
                    else:
                        items.append(phase_ref[k, 8 * (j - 1) : 8 * j, edge])
                groups.append(items)
            while len(groups) < rows // 8 + 1:
                groups.append([None, None])
            for r in range(0, rows, 16):
                both = [measured_ref[p, 0, r : r + 16, edge].astype(F32) for p in range(2)]
                for h in range(2):
                    groups[r // 8 + h] += [b[8 * h : 8 * h + 8] for b in both]
            groups[rows // 8] += [same_ref[:, edge], along_ref[:, 2 * width + edge.start : 2 * width + edge.stop]]
            for g in range(0, len(groups), 4):
                acc = jnp.zeros((8, LANES), F32)
                for q, items in enumerate(groups[g : g + 4]):
                    for k, item in enumerate(items):
                        if item is not None:
                            slot = 4 * q + k
                            shift = (8 * slot - base) % LANES
                            moved = pltpu.roll(item, shift, 1) if shift else item
                            acc = jnp.where((lane >= 8 * slot) & (lane < 8 * slot + 8), moved, acc)
                out_ref[to, 2 * g : 2 * g + 8, :] = acc


def rim_unpack_kernel(got_ref, phase_rim_ref, rim_ref, relay_ref):
    cols, depth = got_ref.shape[:2]
    stripe = phase_rim_ref.shape[1] - 2 * RIM
    rows = 2 * stripe
    illum, _, col = place()
    west, east = jnp.maximum(col - 1, 0), jnp.minimum(col + 1, cols - 1)
    lane = lane_ids((8, LANES))
    in_west = (lane >= LANES - RIM) & (col > 0)
    in_east = (lane < RIM) & (col < cols - 1)
    for g in range(0, rows // 8 + 1, 4):
        a, b = got_ref[west, 2 * g : 2 * g + 8, :], got_ref[east, 2 * g : 2 * g + 8, :]
        for j in range(g, min(g + 4, rows // 8 + 1)):
            for k in range(4):
                if k < 2 and j >= stripe // 8 + 2:
                    continue
                slot = 4 * (j - g) + k
                from_west = pltpu.roll(a, (LANES - RIM - 8 * slot) % LANES, 1)
                from_east = pltpu.roll(b, (-8 * slot) % LANES, 1) if slot else b
                item = jnp.where(in_west, from_west, jnp.where(in_east, from_east, 0.0))
                (phase_rim_ref if k < 2 else rim_ref)[k % 2, 8 * j : 8 * j + 8, :] = item
    other = pl.multiple_of((1 - illum) * stripe, 8)
    near = pl.multiple_of(stripe - 8 + 8 * illum, 8)
    for r in range(0, stripe + 8, 8):
        at = pl.ds(pl.multiple_of(other + r, 8) if r < stripe else near, 8)
        relay_ref[r : r + 8, :] = rim_ref[0, at, :] + pltpu.roll(rim_ref[1, at, :], LANES // 2, 1)
    total = got_ref[0, depth - 8 :, :]
    for c in range(1, cols):
        total = total + got_ref[c, depth - 8 :, :]
    relay_ref[stripe + 8 :, :] = total


def fill_target(tile, target, low_illum, middle, near, far):
    end = 2 * RIM + tile.stripe
    for t in range(tile.tiles):
        beside_rows, packed = near(t), far(t)
        for part, ref in enumerate(target):
            for r in range(0, tile.stripe, 16):
                ref[t, 2 * RIM + r : 2 * RIM + r + 16, :] = middle(part, t, r)
            ref[t, RIM : 2 * RIM, :] = jnp.where(low_illum, unpack_rows(packed, False)[part], beside_rows[part])
            ref[t, end : end + RIM, :] = jnp.where(low_illum, beside_rows[part], unpack_rows(packed, True)[part])


def fill_trig(tile, trig, low_illum, middle, near, far):
    for t in range(tile.tiles):
        for k, (c, s) in enumerate(trig):
            above, below = far(k, t), near(k, t)
            here = [(RIM, jnp.where(low_illum, above, below)), (2 * RIM + tile.stripe, jnp.where(low_illum, below, above))]
            here += [(2 * RIM + r, middle(k, t, r)) for r in range(0, tile.stripe, 16)]
            for first, x in here:
                s[t, first : first + x.shape[0], :], c[t, first : first + x.shape[0], :] = sine_cosine(x)


def tilts_of(note):
    lane = lane_ids(note.shape)
    return [jnp.sum(jnp.where(lane == n, note, 0.0)[:1], axis=1, keepdims=True) for n in (16, 17)]


def forward_both(tile, notes, columns, row_first, totals, trig, half, tables, fields, uses):
    for note, columns_of, (w0, w1), use in zip(notes, (columns, columns), fields, uses):
        incident_tables(tile, tilts_of(note), row_first, columns_of, *totals, tables)
        enter(tile, tables, trig[0], w0)
        first_half(tile, w0, half, 1.0, tile.blocks)
        second_half(tile, w0, half, tile.blocks, modulate_into(trig[1], w1))
        first_half(tile, w1, half, 1.0, tile.blocks)
        second_half(tile, w1, half, tile.blocks, use)


def keep_in(field):
    def use(t, rows, mask, ur, ui):
        field[0][t, rows, :] = ur
        field[1][t, rows, :] = ui

    return use


def residual_in(field, target):
    def use(t, rows, mask, ur, ui):
        field[0][t, rows, :] = mask(ur - target[0][t, rows, :])
        field[1][t, rows, :] = mask(ui - target[1][t, rows, :])

    return use


def residual_of(tile, field, exit_field, target):
    def body(t, left, right, rows, mask):
        for g, u, m in zip(field, exit_field, target):
            g[t, rows, :] = mask(u[t, rows, :] - m[t, rows, :])

    tile.sweep(body, tile.blocks)


def put_in(ref):
    def put(k, t, rows, value):
        ref[k, own_rows(rows), own_columns(t)] = value

    return put


def main_tile(sizes):
    stripe, tiles, total_rows, total_cols = sizes
    illum, row, col = place()
    row_first = (row * 2 + illum) * stripe
    top, bottom, _ = edges_of(row_first, 0, stripe, tiles + 1, total_rows, total_cols)
    return Tile(stripe, tiles, top, bottom), row_first, col * tiles * LANES


def patch_tile(sizes):
    stripe, tiles, total_rows, total_cols = sizes
    _, row_first, col_first = main_tile(sizes)
    width = tiles * LANES
    top, bottom, _ = edges_of(row_first, 0, stripe, tiles + 1, total_rows, total_cols)
    lane = lane_ids((1, LANES))
    held = (lane < 16) | ((lane >= 56) & (lane < 72))
    held = held | ((lane >= 72) & (lane < 80) & (col_first + width < total_cols))
    held = held | ((lane >= LANES - RIM) & (col_first > 0))
    columns = jnp.where(lane < 16, lane, jnp.where(lane < 80, lane - 72 + width, lane - LANES)) + col_first
    tile = Tile(stripe, 1, top, bottom, jnp.where(held, 1.0, 0.0).astype(F32), 0)
    return tile, row_first, jnp.broadcast_to(columns, (8, LANES))


def join_edges(west, east, rim):
    lane = lane_ids(west.shape)
    moved = pltpu.roll(jnp.where(lane < RIM, rim, east), 72, 1)
    return jnp.where(lane < 16, west, jnp.where(lane >= LANES - RIM, rim, moved))


def forward_kernel(sizes, phase_ref, measured_ref, known_ref, partner_ref, along_ref, same_ref,
                   own_ref, o0r, o0i, o1r, o1i, o2r, o2i, c1, s1,
                   c0, s0, w0r, w0i, w1r, w1i, gr, gi, hr, hi, mr, mi, row_r, row_i, col_r, col_i):
    stripe, tiles, total_rows, total_cols = sizes
    tile, row_first, col_first = main_tile(sizes)
    illum, _, _ = place()
    low_illum = illum == 0
    blank_rims((w0r, w0i, w1r, w1i, gr, gi, hr, hi, o0r, o0i, o1r, o1i), tile)
    trig = (c0, s0), (c1, s1)
    fill_trig(
        tile, trig, low_illum,
        lambda k, t, r: phase_ref[k, r : r + 16, own_columns(t)],
        lambda k, t: partner_ref[:, own_columns(t + k * tiles)],
        lambda k, t: along_ref[:, own_columns(t + k * tiles)],
    )
    mine = illum * stripe
    near_base = pl.multiple_of(stripe - 16 * illum, 16)

    def middle(part, t, r):
        return measured_ref[part, 0, pl.ds(pl.multiple_of(mine + r, 16), 16), own_columns(t)].astype(F32)

    def near(t):
        both = [measured_ref[part, 0, pl.ds(near_base, 16), own_columns(t)].astype(F32) for part in range(2)]
        return [jnp.where(low_illum, x[:8], x[8:]) for x in both]

    fill_target(tile, (mr, mi), low_illum, middle, near, lambda t: same_ref[:, own_columns(t)])
    half = hr, hi
    forward_both(
        tile, (partner_ref[:, 2 * tiles * LANES :], known_ref[...]), rim_columns(tile, col_first, col_r.shape), row_first,
        (total_rows, total_cols), trig, half, (row_r, row_i, col_r, col_i),
        (((o0r, o0i), (o1r, o1i)), ((w0r, w0i), (w1r, w1i))),
        (keep_in((o2r, o2i)), residual_in((gr, gi), (mr, mi))),
    )
    backward(tile, (gr, gi), half, (w0r, w0i), (w1r, w1i), trig[1], put_in(own_ref))


def other_near(swap_ref, stripe, low_illum, columns):
    packed = swap_ref[2 * stripe :, columns]
    high, low = unpack_rows(packed, False), unpack_rows(packed, True)
    return [jnp.where(low_illum, low[part], high[part]) for part in range(2)]


def other_kernel(sizes, swap_ref, along_ref, w0r, w0i, w1r, w1i, ur_ref, ui_ref, c1, s1, out_ref, gr, gi, hr, hi, mr, mi):
    stripe, tiles, _, _ = sizes
    tile, _, _ = main_tile(sizes)
    illum, _, _ = place()
    blank_rims((gr, gi, hr, hi), tile)
    fill_target(
        tile, (mr, mi), illum == 0,
        lambda part, t, r: swap_ref[part * stripe + r : part * stripe + r + 16, own_columns(t)],
        lambda t: other_near(swap_ref, stripe, illum == 0, own_columns(t)),
        lambda t: along_ref[:, own_columns(t + 2 * tiles)],
    )
    residual_of(tile, (gr, gi), (ur_ref, ui_ref), (mr, mi))
    backward(tile, (gr, gi), (hr, hi), (w0r, w0i), (w1r, w1i), (c1, s1), put_in(out_ref))


def patch_kernel(sizes, phase_ref, measured_ref, known_ref, partner_ref, along_ref, same_ref, phase_rim_ref, rim_ref,
                 own_ref, o0r, o0i, o1r, o1i, o2r, o2i, c1, s1,
                 c0, s0, w0r, w0i, w1r, w1i, gr, gi, hr, hi, mr, mi, row_r, row_i, col_r, col_i):
    stripe, tiles, total_rows, total_cols = sizes
    tile, row_first, columns = patch_tile(sizes)
    illum, _, _ = place()
    low_illum = illum == 0
    blank_rims((w0r, w0i, w1r, w1i, gr, gi, hr, hi, o0r, o0i, o1r, o1i), tile)
    trig = (c0, s0), (c1, s1)
    first, last = 0, tiles - 1

    def joined(get, rim):
        return join_edges(get(first), get(last), rim)

    end = stripe + RIM
    fill_trig(
        tile, trig, low_illum,
        lambda k, t, r: joined(lambda e: phase_ref[k, r : r + 16, own_columns(e)], phase_rim_ref[k, RIM + r : RIM + r + 16, :]),
        lambda k, t: joined(
            lambda e: partner_ref[:, own_columns(e + k * tiles)],
            jnp.where(low_illum, phase_rim_ref[k, end:, :], phase_rim_ref[k, :RIM, :]),
        ),
        lambda k, t: joined(
            lambda e: along_ref[:, own_columns(e + k * tiles)],
            jnp.where(low_illum, phase_rim_ref[k, :RIM, :], phase_rim_ref[k, end:, :]),
        ),
    )
    mine = illum * stripe
    near_base = pl.multiple_of(stripe - 16 * illum, 16)
    near_rim = pl.multiple_of(stripe - 8 * illum, 8)

    def middle(part, t, r):
        at = pl.ds(pl.multiple_of(mine + r, 16), 16)
        return joined(lambda e: measured_ref[part, 0, at, own_columns(e)].astype(F32), rim_ref[part, at, :])

    def near(t):
        def rows(part, e):
            x = measured_ref[part, 0, pl.ds(near_base, 16), own_columns(e)].astype(F32)
            return jnp.where(low_illum, x[:8], x[8:])

        return [joined(lambda e: rows(part, e), rim_ref[part, pl.ds(near_rim, 8), :]) for part in range(2)]

    def far(t):
        return joined(lambda e: same_ref[:, own_columns(e)], rim_ref[0, 2 * stripe :, :])

    fill_target(tile, (mr, mi), low_illum, middle, near, far)
    half = hr, hi
    forward_both(
        tile, (partner_ref[:, 2 * tiles * LANES :], known_ref[...]), columns, row_first,
        (total_rows, total_cols), trig, half, (row_r, row_i, col_r, col_i),
        (((o0r, o0i), (o1r, o1i)), ((w0r, w0i), (w1r, w1i))),
        (keep_in((o2r, o2i)), residual_in((gr, gi), (mr, mi))),
    )
    backward(tile, (gr, gi), half, (w0r, w0i), (w1r, w1i), trig[1], put_in(own_ref))


def finish_kernel(sizes, own_ref, other_ref, own_patch_ref, swap_ref, along_ref, rim_ref, relay_ref, partner_relay_ref,
                  w0r, w0i, w1r, w1i, ur_ref, ui_ref, c1, s1, out_ref, other_patch, gr, gi, hr, hi, mr, mi):
    stripe, tiles, total_rows, total_cols = sizes
    tile, _, _ = patch_tile(sizes)
    illum, _, _ = place()
    low_illum = illum == 0
    blank_rims((gr, gi, hr, hi), tile)

    lane = lane_ids((8, LANES))
    sums = jnp.maximum(relay_ref[stripe + 8 :, :], partner_relay_ref[stripe + 8 :, :])
    scales = []
    for which in range(2):
        here = jnp.where((lane >= 4 * which) & (lane < 4 * which + 4), sums, 0.0)
        energy = jnp.sum(here[:1], axis=1, keepdims=True) / (total_rows * total_cols) + EPS_ENERGY
        scales.append(2.0 / energy)
    mine = jnp.where(low_illum, scales[0], scales[1])
    others = jnp.where(low_illum, scales[1], scales[0])
    first, last = own_columns(0), own_columns(tiles - 1)

    def middle(part, t, r):
        rim = partner_relay_ref[r : r + 16, :]
        at = slice(part * stripe + r, part * stripe + r + 16)
        return join_edges(swap_ref[at, first], swap_ref[at, last], pltpu.roll(rim, LANES // 2, 1) if part else rim)

    def near(t):
        rim = partner_relay_ref[stripe : stripe + 8, :]
        rims = [rim, pltpu.roll(rim, LANES // 2, 1)]
        west, east = [other_near(swap_ref, stripe, low_illum, at) for at in (first, last)]
        return [join_edges(*x) for x in zip(west, east, rims)]

    def far(t):
        west, east = [along_ref[:, own_columns(e + 2 * tiles)] for e in (0, tiles - 1)]
        return join_edges(west, east, rim_ref[1, 2 * stripe :, :])

    fill_target(tile, (mr, mi), low_illum, middle, near, far)
    residual_of(tile, (gr, gi), (ur_ref, ui_ref), (mr, mi))
    backward(tile, (gr, gi), (hr, hi), (w0r, w0i), (w1r, w1i), (c1, s1), put_in(other_patch))

    for k in range(2):
        for t in range(tiles):
            out_ref[k, :, own_columns(t)] = own_ref[k, :, own_columns(t)] * mine + other_ref[k, :, own_columns(t)] * others
        patch = own_patch_ref[k] * mine + other_patch[k] * others
        on = lane_ids(patch.shape)
        out_ref[k, :, first] = jnp.where(on < RIM, patch, out_ref[k, :, first])
        out_ref[k, :, last] = jnp.where(on >= LANES - RIM, pltpu.roll(patch, 56, 1), out_ref[k, :, last])


def call(kernel, outs, *args, scratch=(), in_place=0, flops=0):
    return pl.pallas_call(
        kernel,
        out_shape=[jax.ShapeDtypeStruct(shape, F32) for shape in outs],
        in_specs=[pl.BlockSpec(memory_space=pl.ANY)] * in_place
        + [pl.BlockSpec(memory_space=pltpu.VMEM)] * (len(args) - in_place),
        out_specs=[pl.BlockSpec(memory_space=pltpu.VMEM)] * len(outs),
        scratch_shapes=[pltpu.VMEM(s, F32) if isinstance(s, tuple) else s for s in scratch],
        compiler_params=pltpu.CompilerParams(vmem_limit_bytes=24 * 2**20),
        cost_estimate=pl.CostEstimate(flops=flops, bytes_accessed=2**18, transcendentals=0),
    )(*args)


def paired(phase_delay, angles, measured):
    slices, stripe, width = phase_delay.shape
    rows, cols = lax.axis_size("row"), lax.axis_size("col")
    tiles = width // LANES
    sizes = (stripe, tiles, 2 * stripe * rows, width * cols)
    swap = [(0, 1), (1, 0)]
    along = []
    for r in range(rows - 1):
        along += [(rows + r, r + 1), (r + 1, rows + r)]
    same = [(r, (r + 1) % rows) for r in range(rows)] + [(rows + (r + 1) % rows, rows + r) for r in range(rows)]

    note, along_out, same_packed = call(
        open_kernel, [(8, LANES), (8, 3 * width), (8, width)], phase_delay, measured,
        scratch=[pltpu.VMEM(measured.shape, measured.dtype), (slices, 8, width), pltpu.SemaphoreType.DMA((2,))], in_place=2,
    )
    core_note = lax.ppermute(note, "row", [(r, r ^ 1) for r in range(rows)])
    along_in = lax.ppermute(along_out, ("illum", "row"), along)
    partner_out, known = call(partner_kernel, [(8, 2 * width + LANES), (8, LANES)], phase_delay, angles, note, core_note)
    partner_in = lax.ppermute(partner_out, "illum", swap)
    (swap_out,) = call(swap_kernel, [(2 * stripe + 8, width)], measured, known)
    swap_in = lax.ppermute(swap_out, "illum", swap)
    (same_out,) = call(same_kernel, [(8, width + LANES)], same_packed, known, partner_in)
    same_in = lax.ppermute(same_out, ("illum", "row"), same)
    depth = 8 * (-(-(stripe // 4 + 1) // 4)) + 8
    (rims_out,) = call(rim_pack_kernel, [(cols, depth, LANES)], phase_delay, measured, known, partner_in, along_in, same_in)
    rims_in = lax.all_to_all(rims_out, "col", 0, 0, tiled=True)

    def fields(count):
        return [(count, stripe + 4 * RIM, LANES)]

    def tables(count):
        return [(stripe + 2 * RIM, LANES)] * 2 + [(-(-count // 8) * 8, LANES)] * 2

    rows_in = phase_delay, measured, known, partner_in, along_in, same_in
    own, *kept = call(
        functools.partial(forward_kernel, sizes), [phase_delay.shape] + fields(tiles) * 8, *rows_in,
        scratch=fields(tiles) * 12 + tables(tiles), flops=6 * 10**9,
    )
    (other,) = call(
        functools.partial(other_kernel, sizes), [phase_delay.shape], swap_in, along_in, *kept,
        scratch=fields(tiles) * 6, flops=2 * 10**9,
    )
    phase_rim, rim, relay = call(
        rim_unpack_kernel, [(2, stripe + 2 * RIM, LANES), (2, 2 * stripe + 8, LANES), (stripe + 16, LANES)], rims_in
    )
    partner_relay = lax.ppermute(relay, "illum", swap)
    own_patch, *patch_kept = call(
        functools.partial(patch_kernel, sizes), [(slices, stripe, LANES)] + fields(1) * 8, *rows_in, phase_rim, rim,
        scratch=fields(1) * 12 + tables(1), flops=10**9,
    )
    (out,) = call(
        functools.partial(finish_kernel, sizes), [phase_delay.shape],
        own, other, own_patch, swap_in, along_in, rim, relay, partner_relay, *patch_kept,
        scratch=[(slices, stripe, LANES)] + fields(1) * 6,
    )
    return out


def halo(x, axis, dim, width, index_of=None):
    peers = lax.axis_size(axis)
    up = [(i, i + 1) for i in range(peers - 1)]
    before = lax.ppermute(lax.slice_in_dim(x, x.shape[dim] - width, x.shape[dim], axis=dim), axis, up)
    after = lax.ppermute(lax.slice_in_dim(x, 0, width, axis=dim), axis, [(j, i) for i, j in up])
    return before, after


def with_column_rims(x, width):
    before, after = halo(x, "col", x.ndim - 1, width)
    gap = jnp.zeros(x.shape[:-1] + (LANES - 2 * width,), x.dtype)
    return jnp.concatenate([x, after, gap, before], axis=-1)


def stripe_halo(x, width):
    illums, rows = lax.axis_size("illum"), lax.axis_size("row")
    where = [(s % illums) * rows + s // illums for s in range(illums * rows)]
    up = [(where[s], where[s + 1]) for s in range(illums * rows - 1)]
    before = lax.ppermute(x[:, -width:], ("illum", "row"), up)
    after = lax.ppermute(x[:, :width], ("illum", "row"), [(b, a) for a, b in up])
    return jnp.concatenate([before, x, after], axis=1)


def per_device(phase_delay, angles, measured):
    illums = lax.axis_size("illum")
    if illums == 2 and lax.axis_size("row") == 4:
        return paired(phase_delay, angles, measured)
    slices, stripe, width = phase_delay.shape
    tile_rows = measured.shape[2]
    total_rows, total_cols = tile_rows * lax.axis_size("row"), width * lax.axis_size("col")
    tiles = width // LANES + 1
    row_first = lax.axis_index("row") * tile_rows + lax.axis_index("illum") * stripe
    col_first = lax.axis_index("col") * width

    target = measured[:, 0].astype(F32)
    energy = lax.psum(jnp.sum(target * target).reshape(1), ("row", "col"))
    energies = lax.all_gather(energy, "illum", tiled=True) / (total_rows * total_cols) + EPS_ENERGY
    tilts = lax.all_gather(angles, "illum", tiled=True)

    phase = with_column_rims(stripe_halo(phase_delay, RIM), RIM)
    above, below = halo(target, "row", 1, REACH)
    target = with_column_rims(jnp.concatenate([above, target, below], axis=1), REACH)
    windows = jnp.stack([target[:, i * stripe : (i + 1) * stripe + 2 * REACH] for i in range(illums)])
    windows = lax.all_to_all(windows, "illum", 0, 0, tiled=True)
    windows = jnp.pad(windows, ((0, 0), (0, 0), (RIM - REACH, RIM - REACH), (0, 0)))

    field = pltpu.VMEM((tiles, stripe + 4 * RIM, LANES), F32)
    rows_all = stripe + 2 * RIM
    return pl.pallas_call(
        functools.partial(gradient_kernel, (stripe, tiles, illums, total_rows, total_cols)),
        out_shape=jax.ShapeDtypeStruct(phase_delay.shape, F32),
        in_specs=[pl.BlockSpec(memory_space=pltpu.SMEM)] * 3 + [pl.BlockSpec(memory_space=pltpu.VMEM)] * 2,
        out_specs=pl.BlockSpec(memory_space=pltpu.VMEM),
        scratch_shapes=[field] * 12
        + [pltpu.VMEM((rows_all, LANES), F32)] * 2
        + [pltpu.VMEM((-(-tiles // 8) * 8, LANES), F32)] * 2,
        compiler_params=pltpu.CompilerParams(vmem_limit_bytes=48 * 2**20),
    )(jnp.stack([row_first, col_first]), tilts, 2.0 / energies, phase, windows)


def solution(mesh):
    placed = (P(None, ("row", "illum"), "col"), P("illum", None), P(None, "illum", "row", "col"))
    return jax.shard_map(
        per_device,
        mesh=mesh,
        in_specs=placed,
        out_specs=P(None, ("row", "illum"), "col"),
        check_vma=False,
    )
```

```python
import functools
import math

import jax
import jax.numpy as jnp
from jax import lax
from jax.experimental import pallas as pl
from jax.experimental.pallas import tpu as pltpu
from jax.sharding import PartitionSpec as P

EPS_ENERGY = 1e-06
RIM = 8
REACH = 4
LANES = 128
F32 = jnp.float32


def sine_cosine(x):
    y = x * x
    s = -2.5052108385441718e-08
    for c in (2.7557319223985893e-06, -1.9841269841269841e-04, 8.333333333333333e-03, -1.6666666666666666e-01):
        s = s * y + c
    c_ = -2.7557319223985888e-07
    for c in (2.48015873015873e-05, -1.3888888888888889e-03, 4.1666666666666664e-02, -0.5, 1.0):
        c_ = c_ * y + c
    return x + x * y * s, c_


def sine_cosine_of_turns(turns):
    quarters = 4.0 * (turns - jnp.floor(turns))
    nearest = jnp.floor(quarters + 0.5)
    s, c = sine_cosine((quarters - nearest) * (0.5 * math.pi))
    odd = (nearest == 1.0) | (nearest == 3.0)
    s, c = jnp.where(odd, c, s), jnp.where(odd, s, c)
    s = jnp.where((nearest == 2.0) | (nearest == 3.0), -s, s)
    c = jnp.where((nearest == 1.0) | (nearest == 2.0), -c, c)
    return s, c


def lane_ids(shape):
    return lax.broadcasted_iota(jnp.int32, shape, len(shape) - 1)


class Tile:
    def __init__(self, stripe, tiles, top, bottom, lanes=None, rim=None):
        self.stripe, self.tiles = stripe, tiles
        self.rows = stripe + 2 * RIM
        self.top, self.bottom, self.lanes, self.rim = top, bottom, lanes, rim
        self.owned = tiles - 1 if rim else tiles
        step = 32 if stripe % 32 == 0 else 8
        self.inner = [(2 * RIM + r, step, None) for r in range(0, stripe, step)]
        self.blocks = [(RIM, RIM, top)] + self.inner + [(2 * RIM + stripe, RIM, bottom)]

    def sweep(self, body, blocks, fields=()):
        for first, count, factor in blocks:
            rows = pl.ds(first, count)
            held = {}

            def load(ref, t, rows=rows, held=held):
                key = id(ref), t % self.tiles
                if key not in held:
                    held[key] = ref[t % self.tiles, rows, :]
                return held[key]

            for t in range(self.tiles):

                def mask(x, factor=factor, lanes=self.lanes if t == self.rim else None):
                    x = x if factor is None else x * factor
                    return x if lanes is None else x * lanes

                body(t, rows, mask, [self.beside(ref, t, rows, load) for ref in fields])

    def beside(self, ref, t, rows, load):
        above = pl.ds(rows.start - 1, rows.size)
        below = pl.ds(rows.start + 1, rows.size)
        here = load(ref, t)
        west = east = here
        if self.tiles > 1:
            lane = lane_ids(here.shape)
            west = jnp.where(lane == LANES - 1, load(ref, t - 1), here)
            east = jnp.where(lane == 0, load(ref, t + 1), here)
        west, east = pltpu.roll(west, 1, 1), pltpu.roll(east, LANES - 1, 1)
        return here, (ref[t, above, :] + ref[t, below, :]) + (west + east)


def first_half(tile, field, half, sign, blocks):
    def body(t, rows, mask, sums):
        (real, beside_real), (imag, beside_imag) = sums
        half[0][t, rows, :] = mask(beside_real + (2.0 * sign) * imag)
        half[1][t, rows, :] = mask(beside_imag - (2.0 * sign) * real)

    tile.sweep(body, blocks, field)


def second_half(tile, field, half, blocks, use):
    def body(t, rows, mask, sums):
        (_, beside_real), (_, beside_imag) = sums
        use(t, rows, mask, 0.1 * beside_real - field[0][t, rows, :], 0.1 * beside_imag - field[1][t, rows, :])

    tile.sweep(body, blocks, half)


def blank_rims(refs, tile):
    for ref in refs:
        for first in (0, tile.rows + RIM):
            ref[:, first : first + RIM, :] = jnp.zeros((tile.tiles, RIM, LANES), F32)


def rim_columns(tile, col_first, shape):
    at, on = lax.broadcasted_iota(jnp.int32, shape, 0), lane_ids(shape)
    return col_first + jnp.where((at >= tile.owned) & (on >= LANES // 2), on - LANES, at * LANES + on)


def incident_tables(tile, tilts, row_first, columns, total_rows, total_cols, tables):
    row_r, row_i, col_r, col_i = tables
    ids = lax.broadcasted_iota(jnp.int32, (tile.rows, LANES), 0) + (row_first - RIM)
    s, c = sine_cosine_of_turns(ids.astype(F32) * tilts[0] / total_rows)
    row_r[...] = (-7.0 * c - 24.0 * s) * 0.04
    row_i[...] = (-7.0 * s + 24.0 * c) * 0.04
    col_i[...], col_r[...] = sine_cosine_of_turns(columns.astype(F32) * tilts[1] / total_cols)


def enter(tile, tables, trig, field):
    row_r, row_i, col_r, col_i = tables
    fr, fi = field

    def start(t, rows, mask, _):
        at = pl.ds(rows.start - RIM, rows.size)
        ar, ai = row_r[at, :], row_i[at, :]
        br, bi = col_r[t : t + 1, :], col_i[t : t + 1, :]
        ur, ui = ar * br - ai * bi, ar * bi + ai * br
        c, s = trig[0][t, rows, :], trig[1][t, rows, :]
        fr[t, rows, :] = mask(ur * c - ui * s)
        fi[t, rows, :] = mask(ur * s + ui * c)

    tile.sweep(start, tile.blocks)


def modulate_into(trig, field):
    def use(t, rows, mask, ur, ui):
        c, s = trig[0][t, rows, :], trig[1][t, rows, :]
        field[0][t, rows, :] = mask(ur * c - ui * s)
        field[1][t, rows, :] = mask(ur * s + ui * c)

    return use


def backward(tile, adjoint, half, w0, w1, trig1, put):
    gr, gi = adjoint
    inner = [first for first, _, _ in tile.inner]

    def back(t, rows, mask, ur, ui):
        if t < tile.owned and rows.start in inner:
            put(1, t, rows, ui * w1[0][t, rows, :] - ur * w1[1][t, rows, :])
        c, s = trig1[0][t, rows, :], trig1[1][t, rows, :]
        gr[t, rows, :] = mask(ur * c + ui * s)
        gi[t, rows, :] = mask(ui * c - ur * s)

    def last(t, rows, mask, ur, ui):
        if t < tile.owned:
            put(0, t, rows, ui * w0[0][t, rows, :] - ur * w0[1][t, rows, :])

    first_half(tile, adjoint, half, -1.0, tile.blocks)
    second_half(tile, adjoint, half, tile.blocks, back)
    first_half(tile, adjoint, half, -1.0, tile.blocks)
    second_half(tile, adjoint, half, tile.inner, last)


def own_columns(t):
    return slice(t * LANES, (t + 1) * LANES)


def own_rows(rows):
    return slice(rows.start - 2 * RIM, rows.start - 2 * RIM + rows.size)


def gradient_kernel(sizes, place_ref, angles_ref, scale_ref, phase_ref, target_ref, out_ref,
                    c0, s0, c1, s1, w0r, w0i, w1r, w1i, gr, gi, hr, hi, row_r, row_i, col_r, col_i):
    stripe, tiles, illums, total_rows, total_cols = sizes
    row_first, col_first = place_ref[0], place_ref[1]
    edges = edges_of(row_first, col_first, stripe, tiles, total_rows, total_cols)
    tile = Tile(stripe, tiles, *edges, rim=tiles - 1)
    blank_rims((w0r, w0i, w1r, w1i, gr, gi, hr, hi), tile)
    out_ref[...] = jnp.zeros(out_ref.shape, F32)
    span = slice(RIM, RIM + tile.rows)
    for t in range(tiles):
        for k, (c, s) in enumerate(((c0, s0), (c1, s1))):
            s[t, span, :], c[t, span, :] = sine_cosine(phase_ref[k, :, own_columns(t)])
    tables, half = (row_r, row_i, col_r, col_i), (hr, hi)

    def illum(j, carry):
        tilts = angles_ref[j, 0].astype(F32), angles_ref[j, 1].astype(F32)
        incident_tables(tile, tilts, row_first, rim_columns(tile, col_first, col_r.shape), total_rows, total_cols, tables)
        enter(tile, tables, (c0, s0), (w0r, w0i))
        first_half(tile, (w0r, w0i), half, 1.0, tile.blocks)
        second_half(tile, (w0r, w0i), half, tile.blocks, modulate_into((c1, s1), (w1r, w1i)))
        first_half(tile, (w1r, w1i), half, 1.0, tile.blocks)

        def residual(t, rows, mask, ur, ui):
            at = slice(rows.start - RIM, rows.start - RIM + rows.size)
            gr[t, rows, :] = mask(ur - target_ref[j, 0, at, own_columns(t)])
            gi[t, rows, :] = mask(ui - target_ref[j, 1, at, own_columns(t)])

        second_half(tile, (w1r, w1i), half, tile.blocks, residual)

        def put(k, t, rows, value):
            at = (k, own_rows(rows), own_columns(t))
            out_ref[at] = out_ref[at] + scale_ref[j] * value

        backward(tile, (gr, gi), half, (w0r, w0i), (w1r, w1i), (c1, s1), put)
        return carry

    lax.fori_loop(0, illums, illum, 0)


def edges_of(row_first, col_first, stripe, tiles, total_rows, total_cols):
    width = (tiles - 1) * LANES
    top = jnp.where(row_first == 0, 0.0, 1.0).astype(F32)
    bottom = jnp.where(row_first + stripe == total_rows, 0.0, 1.0).astype(F32)
    lane = lane_ids((1, LANES))
    in_west = (lane >= LANES - RIM) & (col_first > 0)
    in_east = (lane < RIM) & (col_first + width < total_cols)
    return top, bottom, jnp.where(in_west | in_east, 1.0, 0.0).astype(F32)


def place():
    return lax.axis_index("illum"), lax.axis_index("row"), lax.axis_index("col")


def pack_rows(real, imag, low):
    first = lax.broadcasted_iota(jnp.int32, real.shape, 0) < 4
    if low:
        return jnp.where(first, real, pltpu.roll(imag, 4, 0))
    return jnp.where(first, pltpu.roll(real, 4, 0), imag)


def unpack_rows(packed, low):
    turned = pltpu.roll(packed, 4, 0)
    return (packed, turned) if low else (turned, packed)


def edge_blocks(measured_ref, first):
    base = first // 16 * 16
    at = first - base
    return [measured_ref[p, 0, base : base + 16, :].astype(F32)[at : at + 8] for p in range(2)]


def open_kernel(phase_ref, measured_ref, tilt_ref, partner_ref, along_ref, same_ref, known_ref, held, edge, tilt, sems):
    stripe, width = phase_ref.shape[1:]
    rows = 2 * stripe
    illum, row, _ = place()
    field_copy = pltpu.make_async_copy(measured_ref, held, sems.at[0])
    tilt_copy = pltpu.make_async_copy(tilt_ref, tilt, sems.at[3])
    edge_copies = [
        pltpu.make_async_copy(phase_ref.at[:, pl.ds(first, 8), :], edge.at[e], sems.at[1 + e])
        for e, first in enumerate((0, stripe - 8))
    ]
    for copy in edge_copies:
        copy.start()
    field_copy.start()
    tilt_copy.start()
    for copy in edge_copies:
        copy.wait()
    for k in range(2):
        top, bottom = edge[0, k], edge[1, k]
        along_ref[:, k * width : (k + 1) * width] = jnp.where(illum == 0, top, bottom)
        partner_ref[:, k * width : (k + 1) * width] = jnp.where(illum == 0, bottom, top)
    field_copy.wait()
    top, bottom = pack_rows(*edge_blocks(held, 0), True), pack_rows(*edge_blocks(held, rows - 8), False)
    along_ref[:, 2 * width : 3 * width] = jnp.where(illum == 0, top, bottom)
    same_ref[:, :width] = jnp.where(illum == 0, bottom, top)
    total = jnp.zeros((8, width), F32)
    for p in range(2):
        for r in range(0, rows, 16):
            x = held[p, 0, r : r + 16, :].astype(F32)
            x = x * x
            total = total + (x[:8] + x[8:])
    energy = jnp.sum(jnp.sum(total, axis=1, keepdims=True), axis=0, keepdims=True)
    lane = lane_ids((8, LANES))
    note = jnp.where(lane == illum * 4 + row, energy, 0.0)
    along_ref[:, 3 * width :] = note
    same_ref[:, width:] = note
    tilt_copy.wait()
    for n in range(2):
        note = jnp.where(lane == 16 + n, tilt[:, n : n + 1].astype(F32), note)
    partner_ref[:, 2 * width :] = note
    known_ref[...] = note


def swap_kernel(measured_ref, partner_ref, swap_ref):
    stripe = measured_ref.shape[2] // 2
    illum, _, _ = place()
    other = pl.multiple_of((1 - illum) * stripe, 16)
    for p in range(2):
        for r in range(0, stripe, 16):
            at = pl.ds(pl.multiple_of(other + r, 16), 16)
            swap_ref[p * stripe + r : p * stripe + r + 16, :] = measured_ref[p, 0, at, :].astype(F32)
    above = pack_rows(*edge_blocks(measured_ref, stripe - 8), False)
    below = pack_rows(*edge_blocks(measured_ref, stripe), True)
    swap_ref[2 * stripe :, :] = jnp.where(illum == 0, above, below)


def rim_pack_kernel(phase_ref, measured_ref, known_ref, partner_ref, along_ref, same_ref, out_ref):
    stripe, width = phase_ref.shape[1:]
    rows = 2 * stripe
    illum, _, col = place()
    low_illum = illum == 0
    cols = out_ref.shape[0]
    lane = lane_ids((8, LANES))
    known = jnp.maximum(known_ref[...], partner_ref[:, 2 * width :])
    known = jnp.maximum(jnp.maximum(known, same_ref[:, width:]), along_ref[:, 3 * width :])
    for c in range(cols):
        out_ref[c, out_ref.shape[1] - 8 :, :] = known

    for east in (True, False):
        edge = slice(width - LANES, width) if east else slice(0, LANES)
        base = LANES - RIM if east else 0

        @pl.when(col < cols - 1 if east else col > 0)
        def _():
            to = col + 1 if east else col - 1
            groups = []
            for j in range(stripe // 8 + 2):
                items = []
                for k in range(2):
                    tile = slice(k * width + edge.start, k * width + edge.stop)
                    if j == 0:
                        items.append(jnp.where(low_illum, along_ref[:, tile], partner_ref[:, tile]))
                    elif j == stripe // 8 + 1:
                        items.append(jnp.where(low_illum, partner_ref[:, tile], along_ref[:, tile]))
                    else:
                        items.append(phase_ref[k, 8 * (j - 1) : 8 * j, edge])
                groups.append(items)
            while len(groups) < rows // 8 + 1:
                groups.append([None, None])
            for r in range(0, rows, 16):
                both = [measured_ref[p, 0, r : r + 16, edge].astype(F32) for p in range(2)]
                for h in range(2):
                    groups[r // 8 + h] += [b[8 * h : 8 * h + 8] for b in both]
            groups[rows // 8] += [same_ref[:, edge], along_ref[:, 2 * width + edge.start : 2 * width + edge.stop]]
            for g in range(0, len(groups), 4):
                acc = jnp.zeros((8, LANES), F32)
                for q, items in enumerate(groups[g : g + 4]):
                    for k, item in enumerate(items):
                        if item is not None:
                            slot = 4 * q + k
                            shift = (8 * slot - base) % LANES
                            moved = pltpu.roll(item, shift, 1) if shift else item
                            acc = jnp.where((lane >= 8 * slot) & (lane < 8 * slot + 8), moved, acc)
                out_ref[to, 2 * g : 2 * g + 8, :] = acc


def rim_unpack_kernel(got_ref, phase_rim_ref, rim_ref, relay_ref, sums_ref):
    cols, depth = got_ref.shape[:2]
    stripe = phase_rim_ref.shape[1] - 2 * RIM
    rows = 2 * stripe
    illum, _, col = place()
    west, east = jnp.maximum(col - 1, 0), jnp.minimum(col + 1, cols - 1)
    lane = lane_ids((8, LANES))
    in_west = (lane >= LANES - RIM) & (col > 0)
    in_east = (lane < RIM) & (col < cols - 1)
    for g in range(0, rows // 8 + 1, 4):
        a, b = got_ref[west, 2 * g : 2 * g + 8, :], got_ref[east, 2 * g : 2 * g + 8, :]
        for j in range(g, min(g + 4, rows // 8 + 1)):
            for k in range(4):
                if k < 2 and j >= stripe // 8 + 2:
                    continue
                slot = 4 * (j - g) + k
                from_west = pltpu.roll(a, (LANES - RIM - 8 * slot) % LANES, 1)
                from_east = pltpu.roll(b, (-8 * slot) % LANES, 1) if slot else b
                item = jnp.where(in_west, from_west, jnp.where(in_east, from_east, 0.0))
                (phase_rim_ref if k < 2 else rim_ref)[k % 2, 8 * j : 8 * j + 8, :] = item
    other = pl.multiple_of((1 - illum) * stripe, 8)
    near = pl.multiple_of(stripe - 8 + 8 * illum, 8)
    for r in range(0, stripe + 8, 8):
        at = pl.ds(pl.multiple_of(other + r, 8) if r < stripe else near, 8)
        relay_ref[r : r + 8, :] = rim_ref[0, at, :] + pltpu.roll(rim_ref[1, at, :], LANES // 2, 1)
    total = got_ref[0, depth - 8 :, :]
    for c in range(1, cols):
        total = total + got_ref[c, depth - 8 :, :]
    sums_ref[...] = total


def relay_kernel(relay_ref, sums_ref, core_sums_ref, out_ref):
    out_ref[: relay_ref.shape[0], :] = relay_ref[...]
    out_ref[relay_ref.shape[0] :, :] = jnp.maximum(sums_ref[...], core_sums_ref[...])


def fill_target(tile, target, low_illum, middle, near, far):
    end = 2 * RIM + tile.stripe
    for t in range(tile.tiles):
        beside_rows, packed = near(t), far(t)
        for part, ref in enumerate(target):
            for r in range(0, tile.stripe, 16):
                ref[t, 2 * RIM + r : 2 * RIM + r + 16, :] = middle(part, t, r)
            ref[t, RIM : 2 * RIM, :] = jnp.where(low_illum, unpack_rows(packed, False)[part], beside_rows[part])
            ref[t, end : end + RIM, :] = jnp.where(low_illum, beside_rows[part], unpack_rows(packed, True)[part])


def fill_trig(tile, trig, low_illum, middle, near, far):
    for t in range(tile.tiles):
        for k, (c, s) in enumerate(trig):
            above, below = far(k, t), near(k, t)
            here = [(RIM, jnp.where(low_illum, above, below)), (2 * RIM + tile.stripe, jnp.where(low_illum, below, above))]
            here += [(2 * RIM + r, middle(k, t, r)) for r in range(0, tile.stripe, 16)]
            for first, x in here:
                s[t, first : first + x.shape[0], :], c[t, first : first + x.shape[0], :] = sine_cosine(x)


def tilts_of(note):
    lane = lane_ids(note.shape)
    return [jnp.sum(jnp.where(lane == n, note, 0.0)[:1], axis=1, keepdims=True) for n in (16, 17)]


def forward_both(tile, notes, columns, row_first, totals, trig, half, tables, fields, uses):
    for note, columns_of, (w0, w1), use in zip(notes, (columns, columns), fields, uses):
        incident_tables(tile, tilts_of(note), row_first, columns_of, *totals, tables)
        enter(tile, tables, trig[0], w0)
        first_half(tile, w0, half, 1.0, tile.blocks)
        second_half(tile, w0, half, tile.blocks, modulate_into(trig[1], w1))
        first_half(tile, w1, half, 1.0, tile.blocks)
        second_half(tile, w1, half, tile.blocks, use)


def keep_in(field):
    def use(t, rows, mask, ur, ui):
        field[0][t, rows, :] = ur
        field[1][t, rows, :] = ui

    return use


def residual_in(field, target):
    def use(t, rows, mask, ur, ui):
        field[0][t, rows, :] = mask(ur - target[0][t, rows, :])
        field[1][t, rows, :] = mask(ui - target[1][t, rows, :])

    return use


def residual_of(tile, field, exit_field, target):
    def body(t, rows, mask, _):
        for g, u, m in zip(field, exit_field, target):
            g[t, rows, :] = mask(u[t, rows, :] - m[t, rows, :])

    tile.sweep(body, tile.blocks)


def put_in(ref):
    def put(k, t, rows, value):
        ref[k, own_rows(rows), own_columns(t)] = value

    return put


def main_tile(sizes):
    stripe, tiles, total_rows, total_cols = sizes
    illum, row, col = place()
    row_first = (row * 2 + illum) * stripe
    top, bottom, _ = edges_of(row_first, 0, stripe, tiles + 1, total_rows, total_cols)
    return Tile(stripe, tiles, top, bottom), row_first, col * tiles * LANES


def patch_tile(sizes):
    stripe, tiles, total_rows, total_cols = sizes
    _, row_first, col_first = main_tile(sizes)
    width = tiles * LANES
    top, bottom, _ = edges_of(row_first, 0, stripe, tiles + 1, total_rows, total_cols)
    lane = lane_ids((1, LANES))
    held = (lane < 16) | ((lane >= 56) & (lane < 72))
    held = held | ((lane >= 72) & (lane < 80) & (col_first + width < total_cols))
    held = held | ((lane >= LANES - RIM) & (col_first > 0))
    columns = jnp.where(lane < 16, lane, jnp.where(lane < 80, lane - 72 + width, lane - LANES)) + col_first
    tile = Tile(stripe, 1, top, bottom, jnp.where(held, 1.0, 0.0).astype(F32), 0)
    return tile, row_first, jnp.broadcast_to(columns, (8, LANES))


def join_edges(west, east, rim):
    lane = lane_ids(west.shape)
    moved = pltpu.roll(jnp.where(lane < RIM, rim, east), 72, 1)
    return jnp.where(lane < 16, west, jnp.where(lane >= LANES - RIM, rim, moved))


def forward_kernel(sizes, phase_ref, measured_ref, known_ref, partner_ref, along_ref, same_ref,
                   own_ref, o0r, o0i, o1r, o1i, o2r, o2i, c1, s1,
                   c0, s0, w0r, w0i, w1r, w1i, gr, gi, hr, hi, mr, mi, row_r, row_i, col_r, col_i):
    stripe, tiles, total_rows, total_cols = sizes
    tile, row_first, col_first = main_tile(sizes)
    illum, _, _ = place()
    low_illum = illum == 0
    blank_rims((w0r, w0i, w1r, w1i, gr, gi, hr, hi, o0r, o0i, o1r, o1i), tile)
    trig = (c0, s0), (c1, s1)
    fill_trig(
        tile, trig, low_illum,
        lambda k, t, r: phase_ref[k, r : r + 16, own_columns(t)],
        lambda k, t: partner_ref[:, own_columns(t + k * tiles)],
        lambda k, t: along_ref[:, own_columns(t + k * tiles)],
    )
    mine = illum * stripe
    near_base = pl.multiple_of(stripe - 16 * illum, 16)

    def middle(part, t, r):
        return measured_ref[part, 0, pl.ds(pl.multiple_of(mine + r, 16), 16), own_columns(t)].astype(F32)

    def near(t):
        both = [measured_ref[part, 0, pl.ds(near_base, 16), own_columns(t)].astype(F32) for part in range(2)]
        return [jnp.where(low_illum, x[:8], x[8:]) for x in both]

    fill_target(tile, (mr, mi), low_illum, middle, near, lambda t: same_ref[:, own_columns(t)])
    half = hr, hi
    forward_both(
        tile, (partner_ref[:, 2 * tiles * LANES :], known_ref[...]), rim_columns(tile, col_first, col_r.shape), row_first,
        (total_rows, total_cols), trig, half, (row_r, row_i, col_r, col_i),
        (((o0r, o0i), (o1r, o1i)), ((w0r, w0i), (w1r, w1i))),
        (keep_in((o2r, o2i)), residual_in((gr, gi), (mr, mi))),
    )
    backward(tile, (gr, gi), half, (w0r, w0i), (w1r, w1i), trig[1], put_in(own_ref))


def other_near(swap_ref, stripe, low_illum, columns):
    packed = swap_ref[2 * stripe :, columns]
    high, low = unpack_rows(packed, False), unpack_rows(packed, True)
    return [jnp.where(low_illum, low[part], high[part]) for part in range(2)]


def other_kernel(sizes, swap_ref, along_ref, sums_ref, w0r, w0i, w1r, w1i, ur_ref, ui_ref, c1, s1, out_ref, gr, gi, hr, hi, mr, mi):
    stripe, tiles, _, _ = sizes
    tile, _, _ = main_tile(sizes)
    illum, _, _ = place()
    blank_rims((gr, gi, hr, hi), tile)
    fill_target(
        tile, (mr, mi), illum == 0,
        lambda part, t, r: swap_ref[part * stripe + r : part * stripe + r + 16, own_columns(t)],
        lambda t: other_near(swap_ref, stripe, illum == 0, own_columns(t)),
        lambda t: along_ref[:, own_columns(t + 2 * tiles)],
    )
    residual_of(tile, (gr, gi), (ur_ref, ui_ref), (mr, mi))
    backward(tile, (gr, gi), (hr, hi), (w0r, w0i), (w1r, w1i), (c1, s1), put_in(out_ref))


def patch_kernel(sizes, phase_ref, measured_ref, known_ref, partner_ref, along_ref, same_ref, phase_rim_ref, rim_ref,
                 own_ref, o0r, o0i, o1r, o1i, o2r, o2i, c1, s1,
                 c0, s0, w0r, w0i, w1r, w1i, gr, gi, hr, hi, mr, mi, row_r, row_i, col_r, col_i):
    stripe, tiles, total_rows, total_cols = sizes
    tile, row_first, columns = patch_tile(sizes)
    illum, _, _ = place()
    low_illum = illum == 0
    blank_rims((w0r, w0i, w1r, w1i, gr, gi, hr, hi, o0r, o0i, o1r, o1i), tile)
    trig = (c0, s0), (c1, s1)
    first, last = 0, tiles - 1

    def joined(get, rim):
        return join_edges(get(first), get(last), rim)

    end = stripe + RIM
    fill_trig(
        tile, trig, low_illum,
        lambda k, t, r: joined(lambda e: phase_ref[k, r : r + 16, own_columns(e)], phase_rim_ref[k, RIM + r : RIM + r + 16, :]),
        lambda k, t: joined(
            lambda e: partner_ref[:, own_columns(e + k * tiles)],
            jnp.where(low_illum, phase_rim_ref[k, end:, :], phase_rim_ref[k, :RIM, :]),
        ),
        lambda k, t: joined(
            lambda e: along_ref[:, own_columns(e + k * tiles)],
            jnp.where(low_illum, phase_rim_ref[k, :RIM, :], phase_rim_ref[k, end:, :]),
        ),
    )
    mine = illum * stripe
    near_base = pl.multiple_of(stripe - 16 * illum, 16)
    near_rim = pl.multiple_of(stripe - 8 * illum, 8)

    def middle(part, t, r):
        at = pl.ds(pl.multiple_of(mine + r, 16), 16)
        return joined(lambda e: measured_ref[part, 0, at, own_columns(e)].astype(F32), rim_ref[part, at, :])

    def near(t):
        def rows(part, e):
            x = measured_ref[part, 0, pl.ds(near_base, 16), own_columns(e)].astype(F32)
            return jnp.where(low_illum, x[:8], x[8:])

        return [joined(lambda e: rows(part, e), rim_ref[part, pl.ds(near_rim, 8), :]) for part in range(2)]

    def far(t):
        return joined(lambda e: same_ref[:, own_columns(e)], rim_ref[0, 2 * stripe :, :])

    fill_target(tile, (mr, mi), low_illum, middle, near, far)
    half = hr, hi
    forward_both(
        tile, (partner_ref[:, 2 * tiles * LANES :], known_ref[...]), columns, row_first,
        (total_rows, total_cols), trig, half, (row_r, row_i, col_r, col_i),
        (((o0r, o0i), (o1r, o1i)), ((w0r, w0i), (w1r, w1i))),
        (keep_in((o2r, o2i)), residual_in((gr, gi), (mr, mi))),
    )
    backward(tile, (gr, gi), half, (w0r, w0i), (w1r, w1i), trig[1], put_in(own_ref))


def finish_kernel(sizes, own_ref, other_ref, own_patch_ref, swap_ref, along_ref, rim_ref, relay_ref, partner_relay_ref,
                  w0r, w0i, w1r, w1i, ur_ref, ui_ref, c1, s1, out_ref, other_patch, gr, gi, hr, hi, mr, mi):
    stripe, tiles, total_rows, total_cols = sizes
    tile, _, _ = patch_tile(sizes)
    illum, _, _ = place()
    low_illum = illum == 0
    blank_rims((gr, gi, hr, hi), tile)

    lane = lane_ids((8, LANES))
    sums = jnp.maximum(relay_ref[stripe + 8 :, :], partner_relay_ref[stripe + 8 :, :])
    scales = []
    for which in range(2):
        here = jnp.where((lane >= 4 * which) & (lane < 4 * which + 4), sums, 0.0)
        energy = jnp.sum(here[:1], axis=1, keepdims=True) / (total_rows * total_cols) + EPS_ENERGY
        scales.append(2.0 / energy)
    mine = jnp.where(low_illum, scales[0], scales[1])
    others = jnp.where(low_illum, scales[1], scales[0])
    first, last = own_columns(0), own_columns(tiles - 1)

    def middle(part, t, r):
        rim = partner_relay_ref[r : r + 16, :]
        at = slice(part * stripe + r, part * stripe + r + 16)
        return join_edges(swap_ref[at, first], swap_ref[at, last], pltpu.roll(rim, LANES // 2, 1) if part else rim)

    def near(t):
        rim = partner_relay_ref[stripe : stripe + 8, :]
        rims = [rim, pltpu.roll(rim, LANES // 2, 1)]
        west, east = [other_near(swap_ref, stripe, low_illum, at) for at in (first, last)]
        return [join_edges(*x) for x in zip(west, east, rims)]

    def far(t):
        west, east = [along_ref[:, own_columns(e + 2 * tiles)] for e in (0, tiles - 1)]
        return join_edges(west, east, rim_ref[1, 2 * stripe :, :])

    fill_target(tile, (mr, mi), low_illum, middle, near, far)
    residual_of(tile, (gr, gi), (ur_ref, ui_ref), (mr, mi))
    backward(tile, (gr, gi), (hr, hi), (w0r, w0i), (w1r, w1i), (c1, s1), put_in(other_patch))

    for k in range(2):
        for t in range(tiles):
            out_ref[k, :, own_columns(t)] = own_ref[k, :, own_columns(t)] * mine + other_ref[k, :, own_columns(t)] * others
        patch = own_patch_ref[k] * mine + other_patch[k] * others
        on = lane_ids(patch.shape)
        out_ref[k, :, first] = jnp.where(on < RIM, patch, out_ref[k, :, first])
        out_ref[k, :, last] = jnp.where(on >= LANES - RIM, pltpu.roll(patch, 56, 1), out_ref[k, :, last])


def call(kernel, outs, *args, scratch=(), in_place=0, flops=0, mib=8):
    return pl.pallas_call(
        kernel,
        out_shape=[jax.ShapeDtypeStruct(shape, F32) for shape in outs],
        in_specs=[pl.BlockSpec(memory_space=pltpu.HBM)] * in_place
        + [pl.BlockSpec(memory_space=pltpu.VMEM)] * (len(args) - in_place),
        out_specs=[pl.BlockSpec(memory_space=pltpu.VMEM)] * len(outs),
        scratch_shapes=[pltpu.VMEM(s, F32) if isinstance(s, tuple) else s for s in scratch],
        compiler_params=pltpu.CompilerParams(vmem_limit_bytes=int(mib * 2**20)),
        cost_estimate=pl.CostEstimate(flops=flops, bytes_accessed=2**18, transcendentals=0),
    )(*args)


def paired(phase_delay, angles, measured):
    slices, stripe, width = phase_delay.shape
    rows, cols = lax.axis_size("row"), lax.axis_size("col")
    tiles = width // LANES
    sizes = (stripe, tiles, 2 * stripe * rows, width * cols)
    swap = [(0, 1), (1, 0)]
    along = []
    for r in range(rows):
        along += [(rows + r, (r + 1) % rows), ((r + 1) % rows, rows + r)]
    same = [(r, (r + 1) % rows) for r in range(rows)] + [(rows + (r + 1) % rows, rows + r) for r in range(rows)]

    partner_out, along_out, same_out, known = call(
        open_kernel, [(8, 2 * width + LANES), (8, 3 * width + LANES), (8, width + LANES), (8, LANES)],
        phase_delay, measured, angles, in_place=3, mib=62,
        scratch=[
            pltpu.VMEM(measured.shape, measured.dtype), (2, slices, 8, width),
            pltpu.VMEM(angles.shape, angles.dtype), pltpu.SemaphoreType.DMA((4,)),
        ],
    )
    along_in = lax.ppermute(along_out, ("illum", "row"), along)
    partner_in = lax.ppermute(partner_out, "illum", swap)
    same_in = lax.ppermute(same_out, ("illum", "row"), same)
    (swap_out,) = call(swap_kernel, [(2 * stripe + 8, width)], measured, partner_in)
    swap_in = lax.ppermute(swap_out, "illum", swap)
    depth = 8 * (-(-(stripe // 4 + 1) // 4)) + 8
    (rims_out,) = call(rim_pack_kernel, [(cols, depth, LANES)], phase_delay, measured, known, partner_in, along_in, same_in)
    rims_in = lax.all_to_all(rims_out, "col", 0, 0, tiled=True)

    def fields(count):
        return [(count, stripe + 4 * RIM, LANES)]

    def tables(count):
        return [(stripe + 2 * RIM, LANES)] * 2 + [(-(-count // 8) * 8, LANES)] * 2

    rows_in = phase_delay, measured, known, partner_in, along_in, same_in
    own, *kept = call(
        functools.partial(forward_kernel, sizes), [phase_delay.shape] + fields(tiles) * 8, *rows_in,
        scratch=fields(tiles) * 12 + tables(tiles), flops=6 * 10**9, mib=16,
    )
    phase_rim, rim, relay, sums = call(
        rim_unpack_kernel, [(2, stripe + 2 * RIM, LANES), (2, 2 * stripe + 8, LANES), (stripe + 8, LANES), (8, LANES)], rims_in
    )
    core_sums = lax.ppermute(sums, "row", [(r, r ^ 1) for r in range(rows)])
    (other,) = call(
        functools.partial(other_kernel, sizes), [phase_delay.shape], swap_in, along_in, sums, *kept,
        scratch=fields(tiles) * 6, flops=2 * 10**9, mib=12,
    )
    (relay,) = call(relay_kernel, [(stripe + 16, LANES)], relay, sums, core_sums)
    partner_relay = lax.ppermute(relay, "illum", swap)
    own_patch, *patch_kept = call(
        functools.partial(patch_kernel, sizes), [(slices, stripe, LANES)] + fields(1) * 8, *rows_in, phase_rim, rim,
        scratch=fields(1) * 12 + tables(1), flops=10**9,
    )
    (out,) = call(
        functools.partial(finish_kernel, sizes), [phase_delay.shape],
        own, other, own_patch, swap_in, along_in, rim, relay, partner_relay, *patch_kept,
        scratch=[(slices, stripe, LANES)] + fields(1) * 6,
    )
    return out


def halo(x, axis, dim, width, index_of=None):
    peers = lax.axis_size(axis)
    up = [(i, i + 1) for i in range(peers - 1)]
    before = lax.ppermute(lax.slice_in_dim(x, x.shape[dim] - width, x.shape[dim], axis=dim), axis, up)
    after = lax.ppermute(lax.slice_in_dim(x, 0, width, axis=dim), axis, [(j, i) for i, j in up])
    return before, after


def with_column_rims(x, width):
    before, after = halo(x, "col", x.ndim - 1, width)
    gap = jnp.zeros(x.shape[:-1] + (LANES - 2 * width,), x.dtype)
    return jnp.concatenate([x, after, gap, before], axis=-1)


def stripe_halo(x, width):
    illums, rows = lax.axis_size("illum"), lax.axis_size("row")
    where = [(s % illums) * rows + s // illums for s in range(illums * rows)]
    up = [(where[s], where[s + 1]) for s in range(illums * rows - 1)]
    before = lax.ppermute(x[:, -width:], ("illum", "row"), up)
    after = lax.ppermute(x[:, :width], ("illum", "row"), [(b, a) for a, b in up])
    return jnp.concatenate([before, x, after], axis=1)


def per_device(phase_delay, angles, measured):
    illums = lax.axis_size("illum")
    if illums == 2 and lax.axis_size("row") == 4:
        return paired(phase_delay, angles, measured)
    slices, stripe, width = phase_delay.shape
    tile_rows = measured.shape[2]
    total_rows, total_cols = tile_rows * lax.axis_size("row"), width * lax.axis_size("col")
    tiles = width // LANES + 1
    row_first = lax.axis_index("row") * tile_rows + lax.axis_index("illum") * stripe
    col_first = lax.axis_index("col") * width

    target = measured[:, 0].astype(F32)
    energy = lax.psum(jnp.sum(target * target).reshape(1), ("row", "col"))
    energies = lax.all_gather(energy, "illum", tiled=True) / (total_rows * total_cols) + EPS_ENERGY
    tilts = lax.all_gather(angles, "illum", tiled=True)

    phase = with_column_rims(stripe_halo(phase_delay, RIM), RIM)
    above, below = halo(target, "row", 1, REACH)
    target = with_column_rims(jnp.concatenate([above, target, below], axis=1), REACH)
    windows = jnp.stack([target[:, i * stripe : (i + 1) * stripe + 2 * REACH] for i in range(illums)])
    windows = lax.all_to_all(windows, "illum", 0, 0, tiled=True)
    windows = jnp.pad(windows, ((0, 0), (0, 0), (RIM - REACH, RIM - REACH), (0, 0)))

    field = pltpu.VMEM((tiles, stripe + 4 * RIM, LANES), F32)
    rows_all = stripe + 2 * RIM
    return pl.pallas_call(
        functools.partial(gradient_kernel, (stripe, tiles, illums, total_rows, total_cols)),
        out_shape=jax.ShapeDtypeStruct(phase_delay.shape, F32),
        in_specs=[pl.BlockSpec(memory_space=pltpu.SMEM)] * 3 + [pl.BlockSpec(memory_space=pltpu.VMEM)] * 2,
        out_specs=pl.BlockSpec(memory_space=pltpu.VMEM),
        scratch_shapes=[field] * 12
        + [pltpu.VMEM((rows_all, LANES), F32)] * 2
        + [pltpu.VMEM((-(-tiles // 8) * 8, LANES), F32)] * 2,
        compiler_params=pltpu.CompilerParams(vmem_limit_bytes=48 * 2**20),
    )(jnp.stack([row_first, col_first]), tilts, 2.0 / energies, phase, windows)


def solution(mesh):
    placed = (P(None, ("row", "illum"), "col"), P("illum", None), P(None, "illum", "row", "col"))
    return jax.shard_map(
        per_device,
        mesh=mesh,
        in_specs=placed,
        out_specs=P(None, ("row", "illum"), "col"),
        check_vma=False,
    )
```

```python
import functools
import math

import jax
import jax.numpy as jnp
from jax import lax
from jax.experimental import pallas as pl
from jax.experimental.pallas import tpu as pltpu
from jax.sharding import PartitionSpec as P

EPS_ENERGY = 1e-06
RIM = 8
REACH = 4
LANES = 128
F32 = jnp.float32


def sine_cosine(x):
    y = x * x
    s = -2.5052108385441718e-08
    for c in (2.7557319223985893e-06, -1.9841269841269841e-04, 8.333333333333333e-03, -1.6666666666666666e-01):
        s = s * y + c
    c_ = -2.7557319223985888e-07
    for c in (2.48015873015873e-05, -1.3888888888888889e-03, 4.1666666666666664e-02, -0.5, 1.0):
        c_ = c_ * y + c
    return x + x * y * s, c_


def sine_cosine_of_turns(turns):
    quarters = 4.0 * (turns - jnp.floor(turns))
    nearest = jnp.floor(quarters + 0.5)
    s, c = sine_cosine((quarters - nearest) * (0.5 * math.pi))
    odd = (nearest == 1.0) | (nearest == 3.0)
    s, c = jnp.where(odd, c, s), jnp.where(odd, s, c)
    s = jnp.where((nearest == 2.0) | (nearest == 3.0), -s, s)
    c = jnp.where((nearest == 1.0) | (nearest == 2.0), -c, c)
    return s, c


def lane_ids(shape):
    return lax.broadcasted_iota(jnp.int32, shape, len(shape) - 1)


class Tile:
    def __init__(self, stripe, tiles, top, bottom, lanes=None, rim=None):
        self.stripe, self.tiles = stripe, tiles
        self.rows = stripe + 2 * RIM
        self.top, self.bottom, self.lanes, self.rim = top, bottom, lanes, rim
        self.owned = tiles - 1 if rim else tiles
        step = 32 if stripe % 32 == 0 else 8
        self.inner = [(2 * RIM + r, step, None) for r in range(0, stripe, step)]
        self.blocks = [(RIM, RIM, top)] + self.inner + [(2 * RIM + stripe, RIM, bottom)]

    def sweep(self, body, blocks, fields=()):
        for first, count, factor in blocks:
            rows = pl.ds(first, count)
            held = {}

            def load(ref, t, rows=rows, held=held):
                key = id(ref), t % self.tiles
                if key not in held:
                    held[key] = ref[t % self.tiles, rows, :]
                return held[key]

            for t in range(self.tiles):

                def mask(x, factor=factor, lanes=self.lanes if t == self.rim else None):
                    x = x if factor is None else x * factor
                    return x if lanes is None else x * lanes

                body(t, rows, mask, [self.beside(ref, t, rows, load) for ref in fields])

    def beside(self, ref, t, rows, load):
        above = pl.ds(rows.start - 1, rows.size)
        below = pl.ds(rows.start + 1, rows.size)
        here = load(ref, t)
        west = east = here
        if self.tiles > 1:
            lane = lane_ids(here.shape)
            west = jnp.where(lane == LANES - 1, load(ref, t - 1), here)
            east = jnp.where(lane == 0, load(ref, t + 1), here)
        west, east = pltpu.roll(west, 1, 1), pltpu.roll(east, LANES - 1, 1)
        return here, (ref[t, above, :] + ref[t, below, :]) + (west + east)


def first_half(tile, field, half, sign, blocks):
    def body(t, rows, mask, sums):
        (real, beside_real), (imag, beside_imag) = sums
        half[0][t, rows, :] = mask(beside_real + (2.0 * sign) * imag)
        half[1][t, rows, :] = mask(beside_imag - (2.0 * sign) * real)

    tile.sweep(body, blocks, field)


def second_half(tile, field, half, blocks, use):
    def body(t, rows, mask, sums):
        (_, beside_real), (_, beside_imag) = sums
        use(t, rows, mask, 0.1 * beside_real - field[0][t, rows, :], 0.1 * beside_imag - field[1][t, rows, :])

    tile.sweep(body, blocks, half)


def blank_rims(refs, tile):
    for ref in refs:
        for first in (0, tile.rows + RIM):
            ref[:, first : first + RIM, :] = jnp.zeros((tile.tiles, RIM, LANES), F32)


def rim_columns(tile, col_first, shape):
    at, on = lax.broadcasted_iota(jnp.int32, shape, 0), lane_ids(shape)
    return col_first + jnp.where((at >= tile.owned) & (on >= LANES // 2), on - LANES, at * LANES + on)


def incident_tables(tile, tilts, row_first, columns, total_rows, total_cols, tables):
    row_r, row_i, col_r, col_i = tables
    ids = lax.broadcasted_iota(jnp.int32, (tile.rows, LANES), 0) + (row_first - RIM)
    s, c = sine_cosine_of_turns(ids.astype(F32) * tilts[0] / total_rows)
    row_r[...] = (-7.0 * c - 24.0 * s) * 0.04
    row_i[...] = (-7.0 * s + 24.0 * c) * 0.04
    col_i[...], col_r[...] = sine_cosine_of_turns(columns.astype(F32) * tilts[1] / total_cols)


def enter(tile, tables, trig, field):
    row_r, row_i, col_r, col_i = tables
    fr, fi = field

    def start(t, rows, mask, _):
        at = pl.ds(rows.start - RIM, rows.size)
        ar, ai = row_r[at, :], row_i[at, :]
        br, bi = col_r[t : t + 1, :], col_i[t : t + 1, :]
        ur, ui = ar * br - ai * bi, ar * bi + ai * br
        c, s = trig[0][t, rows, :], trig[1][t, rows, :]
        fr[t, rows, :] = mask(ur * c - ui * s)
        fi[t, rows, :] = mask(ur * s + ui * c)

    tile.sweep(start, tile.blocks)


def modulate_into(trig, field):
    def use(t, rows, mask, ur, ui):
        c, s = trig[0][t, rows, :], trig[1][t, rows, :]
        field[0][t, rows, :] = mask(ur * c - ui * s)
        field[1][t, rows, :] = mask(ur * s + ui * c)

    return use


def backward(tile, adjoint, half, w0, w1, trig1, put):
    gr, gi = adjoint
    inner = [first for first, _, _ in tile.inner]

    def back(t, rows, mask, ur, ui):
        if t < tile.owned and rows.start in inner:
            put(1, t, rows, ui * w1[0][t, rows, :] - ur * w1[1][t, rows, :])
        c, s = trig1[0][t, rows, :], trig1[1][t, rows, :]
        gr[t, rows, :] = mask(ur * c + ui * s)
        gi[t, rows, :] = mask(ui * c - ur * s)

    def last(t, rows, mask, ur, ui):
        if t < tile.owned:
            put(0, t, rows, ui * w0[0][t, rows, :] - ur * w0[1][t, rows, :])

    first_half(tile, adjoint, half, -1.0, tile.blocks)
    second_half(tile, adjoint, half, tile.blocks, back)
    first_half(tile, adjoint, half, -1.0, tile.blocks)
    second_half(tile, adjoint, half, tile.inner, last)


def own_columns(t):
    return slice(t * LANES, (t + 1) * LANES)


def own_rows(rows):
    return slice(rows.start - 2 * RIM, rows.start - 2 * RIM + rows.size)


def gradient_kernel(sizes, place_ref, angles_ref, scale_ref, phase_ref, target_ref, out_ref,
                    c0, s0, c1, s1, w0r, w0i, w1r, w1i, gr, gi, hr, hi, row_r, row_i, col_r, col_i):
    stripe, tiles, illums, total_rows, total_cols = sizes
    row_first, col_first = place_ref[0], place_ref[1]
    edges = edges_of(row_first, col_first, stripe, tiles, total_rows, total_cols)
    tile = Tile(stripe, tiles, *edges, rim=tiles - 1)
    blank_rims((w0r, w0i, w1r, w1i, gr, gi, hr, hi), tile)
    out_ref[...] = jnp.zeros(out_ref.shape, F32)
    span = slice(RIM, RIM + tile.rows)
    for t in range(tiles):
        for k, (c, s) in enumerate(((c0, s0), (c1, s1))):
            s[t, span, :], c[t, span, :] = sine_cosine(phase_ref[k, :, own_columns(t)])
    tables, half = (row_r, row_i, col_r, col_i), (hr, hi)

    def illum(j, carry):
        tilts = angles_ref[j, 0].astype(F32), angles_ref[j, 1].astype(F32)
        incident_tables(tile, tilts, row_first, rim_columns(tile, col_first, col_r.shape), total_rows, total_cols, tables)
        enter(tile, tables, (c0, s0), (w0r, w0i))
        first_half(tile, (w0r, w0i), half, 1.0, tile.blocks)
        second_half(tile, (w0r, w0i), half, tile.blocks, modulate_into((c1, s1), (w1r, w1i)))
        first_half(tile, (w1r, w1i), half, 1.0, tile.blocks)

        def residual(t, rows, mask, ur, ui):
            at = slice(rows.start - RIM, rows.start - RIM + rows.size)
            gr[t, rows, :] = mask(ur - target_ref[j, 0, at, own_columns(t)])
            gi[t, rows, :] = mask(ui - target_ref[j, 1, at, own_columns(t)])

        second_half(tile, (w1r, w1i), half, tile.blocks, residual)

        def put(k, t, rows, value):
            at = (k, own_rows(rows), own_columns(t))
            out_ref[at] = out_ref[at] + scale_ref[j] * value

        backward(tile, (gr, gi), half, (w0r, w0i), (w1r, w1i), (c1, s1), put)
        return carry

    lax.fori_loop(0, illums, illum, 0)


def edges_of(row_first, col_first, stripe, tiles, total_rows, total_cols):
    width = (tiles - 1) * LANES
    top = jnp.where(row_first == 0, 0.0, 1.0).astype(F32)
    bottom = jnp.where(row_first + stripe == total_rows, 0.0, 1.0).astype(F32)
    lane = lane_ids((1, LANES))
    in_west = (lane >= LANES - RIM) & (col_first > 0)
    in_east = (lane < RIM) & (col_first + width < total_cols)
    return top, bottom, jnp.where(in_west | in_east, 1.0, 0.0).astype(F32)


def place():
    return lax.axis_index("illum"), lax.axis_index("row"), lax.axis_index("col")


def pack_rows(real, imag, low):
    first = lax.broadcasted_iota(jnp.int32, real.shape, 0) < 4
    if low:
        return jnp.where(first, real, pltpu.roll(imag, 4, 0))
    return jnp.where(first, pltpu.roll(real, 4, 0), imag)


def unpack_rows(packed, low):
    turned = pltpu.roll(packed, 4, 0)
    return (packed, turned) if low else (turned, packed)


def edge_blocks(measured_ref, first):
    base = first // 16 * 16
    at = first - base
    return [measured_ref[p, 0, base : base + 16, :].astype(F32)[at : at + 8] for p in range(2)]


def open_kernel(phase_ref, measured_ref, tilt_ref, partner_ref, along_ref, same_ref, known_ref, held, edge, tilt, sems):
    stripe, width = phase_ref.shape[1:]
    rows = 2 * stripe
    illum, row, _ = place()
    field_copy = pltpu.make_async_copy(measured_ref, held, sems.at[0])
    tilt_copy = pltpu.make_async_copy(tilt_ref, tilt, sems.at[3])
    edge_copies = [
        pltpu.make_async_copy(phase_ref.at[:, pl.ds(first, 8), :], edge.at[e], sems.at[1 + e])
        for e, first in enumerate((0, stripe - 8))
    ]
    for copy in edge_copies:
        copy.start()
    field_copy.start()
    tilt_copy.start()
    for copy in edge_copies:
        copy.wait()
    for k in range(2):
        top, bottom = edge[0, k], edge[1, k]
        along_ref[:, k * width : (k + 1) * width] = jnp.where(illum == 0, top, bottom)
        partner_ref[:, k * width : (k + 1) * width] = jnp.where(illum == 0, bottom, top)
    field_copy.wait()
    top, bottom = pack_rows(*edge_blocks(held, 0), True), pack_rows(*edge_blocks(held, rows - 8), False)
    along_ref[:, 2 * width : 3 * width] = jnp.where(illum == 0, top, bottom)
    same_ref[:, :width] = jnp.where(illum == 0, bottom, top)
    total = jnp.zeros((8, width), F32)
    for p in range(2):
        for r in range(0, rows, 16):
            x = held[p, 0, r : r + 16, :].astype(F32)
            x = x * x
            total = total + (x[:8] + x[8:])
    energy = jnp.sum(jnp.sum(total, axis=1, keepdims=True), axis=0, keepdims=True)
    lane = lane_ids((8, LANES))
    note = jnp.where(lane == illum * 4 + row, energy, 0.0)
    along_ref[:, 3 * width :] = note
    same_ref[:, width:] = note
    tilt_copy.wait()
    for n in range(2):
        note = jnp.where(lane == 16 + n, tilt[:, n : n + 1].astype(F32), note)
    partner_ref[:, 2 * width :] = note
    known_ref[...] = note


def swap_kernel(measured_ref, same_ref, swap_ref):
    stripe = measured_ref.shape[2] // 2
    illum, _, _ = place()
    other = pl.multiple_of((1 - illum) * stripe, 16)
    for p in range(2):
        for r in range(0, stripe, 16):
            at = pl.ds(pl.multiple_of(other + r, 16), 16)
            swap_ref[p * stripe + r : p * stripe + r + 16, :] = measured_ref[p, 0, at, :].astype(F32)
    above = pack_rows(*edge_blocks(measured_ref, stripe - 8), False)
    below = pack_rows(*edge_blocks(measured_ref, stripe), True)
    swap_ref[2 * stripe :, :] = jnp.where(illum == 0, above, below)


def rim_pack_kernel(phase_ref, measured_ref, known_ref, partner_ref, along_ref, same_ref, first_ref, second_ref, note_ref):
    stripe, width = phase_ref.shape[1:]
    rows = 2 * stripe
    illum, _, col = place()
    low_illum = illum == 0
    even = lax.rem(col, 2) == 0
    lane = lane_ids((8, LANES))
    known = jnp.maximum(known_ref[...], partner_ref[:, 2 * width :])
    known = jnp.maximum(jnp.maximum(known, same_ref[:, width:]), along_ref[:, 3 * width :])
    note_ref[...] = known
    first_ref[first_ref.shape[0] - 8 :, :] = known

    def packed(east):
        edge = slice(width - LANES, width) if east else slice(0, LANES)
        base = LANES - RIM if east else 0
        groups = []
        for j in range(stripe // 8 + 2):
            items = []
            for k in range(2):
                tile = slice(k * width + edge.start, k * width + edge.stop)
                if j == 0:
                    items.append(jnp.where(low_illum, along_ref[:, tile], partner_ref[:, tile]))
                elif j == stripe // 8 + 1:
                    items.append(jnp.where(low_illum, partner_ref[:, tile], along_ref[:, tile]))
                else:
                    items.append(phase_ref[k, 8 * (j - 1) : 8 * j, edge])
            groups.append(items)
        while len(groups) < rows // 8 + 1:
            groups.append([None, None])
        for r in range(0, rows, 16):
            both = [measured_ref[p, 0, r : r + 16, edge].astype(F32) for p in range(2)]
            for h in range(2):
                groups[r // 8 + h] += [b[8 * h : 8 * h + 8] for b in both]
        groups[rows // 8] += [same_ref[:, edge], along_ref[:, 2 * width + edge.start : 2 * width + edge.stop]]
        for g in range(0, len(groups), 4):
            acc = jnp.zeros((8, LANES), F32)
            for q, items in enumerate(groups[g : g + 4]):
                for k, item in enumerate(items):
                    if item is not None:
                        slot = 4 * q + k
                        shift = (8 * slot - base) % LANES
                        moved = pltpu.roll(item, shift, 1) if shift else item
                        acc = jnp.where((lane >= 8 * slot) & (lane < 8 * slot + 8), moved, acc)
            yield 2 * g, acc

    for (at, east), (_, west) in zip(packed(True), packed(False)):
        first_ref[at : at + 8, :] = jnp.where(even, east, west)
        second_ref[at : at + 8, :] = jnp.where(even, west, east)


def second_kernel(packed_ref, note_ref, first_ref, out_ref):
    rims = packed_ref.shape[0]
    out_ref[:rims, :] = packed_ref[...]
    out_ref[rims:, :] = note_ref[...] + first_ref[rims:, :]


def rim_unpack_kernel(first_ref, second_ref, note_ref, phase_rim_ref, rim_ref, relay_ref, sums_ref):
    stripe = phase_rim_ref.shape[1] - 2 * RIM
    rims, rows = first_ref.shape[0] - 8, 2 * stripe
    illum, _, col = place()
    even = lax.rem(col, 2) == 0
    lane = lane_ids((8, LANES))
    in_west = (lane >= LANES - RIM) & (col > 0)
    in_east = (lane < RIM) & (col < lax.axis_size("col") - 1)
    for g in range(0, rows // 8 + 1, 4):
        first, second = first_ref[2 * g : 2 * g + 8, :], second_ref[2 * g : 2 * g + 8, :]
        a, b = jnp.where(even, second, first), jnp.where(even, first, second)
        for j in range(g, min(g + 4, rows // 8 + 1)):
            for k in range(4):
                if k < 2 and j >= stripe // 8 + 2:
                    continue
                slot = 4 * (j - g) + k
                from_west = pltpu.roll(a, (LANES - RIM - 8 * slot) % LANES, 1)
                from_east = pltpu.roll(b, (-8 * slot) % LANES, 1) if slot else b
                item = jnp.where(in_west, from_west, jnp.where(in_east, from_east, 0.0))
                (phase_rim_ref if k < 2 else rim_ref)[k % 2, 8 * j : 8 * j + 8, :] = item
    other = pl.multiple_of((1 - illum) * stripe, 8)
    near = pl.multiple_of(stripe - 8 + 8 * illum, 8)
    for r in range(0, stripe + 8, 8):
        at = pl.ds(pl.multiple_of(other + r, 8) if r < stripe else near, 8)
        relay_ref[r : r + 8, :] = rim_ref[0, at, :] + pltpu.roll(rim_ref[1, at, :], LANES // 2, 1)
    sums_ref[...] = note_ref[...] + first_ref[rims:, :] + second_ref[rims:, :]


def fill_target(tile, target, low_illum, middle, near, far):
    end = 2 * RIM + tile.stripe
    for t in range(tile.tiles):
        beside_rows, packed = near(t), far(t)
        for part, ref in enumerate(target):
            for r in range(0, tile.stripe, 16):
                ref[t, 2 * RIM + r : 2 * RIM + r + 16, :] = middle(part, t, r)
            ref[t, RIM : 2 * RIM, :] = jnp.where(low_illum, unpack_rows(packed, False)[part], beside_rows[part])
            ref[t, end : end + RIM, :] = jnp.where(low_illum, beside_rows[part], unpack_rows(packed, True)[part])


def fill_trig(tile, trig, low_illum, middle, near, far):
    for t in range(tile.tiles):
        for k, (c, s) in enumerate(trig):
            above, below = far(k, t), near(k, t)
            here = [(RIM, jnp.where(low_illum, above, below)), (2 * RIM + tile.stripe, jnp.where(low_illum, below, above))]
            here += [(2 * RIM + r, middle(k, t, r)) for r in range(0, tile.stripe, 16)]
            for first, x in here:
                s[t, first : first + x.shape[0], :], c[t, first : first + x.shape[0], :] = sine_cosine(x)


def tilts_of(note):
    lane = lane_ids(note.shape)
    return [jnp.sum(jnp.where(lane == n, note, 0.0)[:1], axis=1, keepdims=True) for n in (16, 17)]


def forward(tile, note, columns, row_first, totals, trig, half, tables, w0, w1, use):
    incident_tables(tile, tilts_of(note), row_first, columns, *totals, tables)
    enter(tile, tables, trig[0], w0)
    first_half(tile, w0, half, 1.0, tile.blocks)
    second_half(tile, w0, half, tile.blocks, modulate_into(trig[1], w1))
    first_half(tile, w1, half, 1.0, tile.blocks)
    second_half(tile, w1, half, tile.blocks, use)


def keep_in(field):
    def use(t, rows, mask, ur, ui):
        field[0][t, rows, :] = ur
        field[1][t, rows, :] = ui

    return use


def residual_in(field, target):
    def use(t, rows, mask, ur, ui):
        field[0][t, rows, :] = mask(ur - target[0][t, rows, :])
        field[1][t, rows, :] = mask(ui - target[1][t, rows, :])

    return use


def residual_of(tile, field, exit_field, target):
    def body(t, rows, mask, _):
        for g, u, m in zip(field, exit_field, target):
            g[t, rows, :] = mask(u[t, rows, :] - m[t, rows, :])

    tile.sweep(body, tile.blocks)


def put_in(ref):
    def put(k, t, rows, value):
        ref[k, own_rows(rows), own_columns(t)] = value

    return put


def main_tile(sizes):
    stripe, tiles, total_rows, total_cols = sizes
    illum, row, col = place()
    row_first = (row * 2 + illum) * stripe
    top, bottom, _ = edges_of(row_first, 0, stripe, tiles + 1, total_rows, total_cols)
    return Tile(stripe, tiles, top, bottom), row_first, col * tiles * LANES


def patch_tile(sizes):
    stripe, tiles, total_rows, total_cols = sizes
    _, row_first, col_first = main_tile(sizes)
    width = tiles * LANES
    top, bottom, _ = edges_of(row_first, 0, stripe, tiles + 1, total_rows, total_cols)
    lane = lane_ids((1, LANES))
    held = (lane < 16) | ((lane >= 56) & (lane < 72))
    held = held | ((lane >= 72) & (lane < 80) & (col_first + width < total_cols))
    held = held | ((lane >= LANES - RIM) & (col_first > 0))
    columns = jnp.where(lane < 16, lane, jnp.where(lane < 80, lane - 72 + width, lane - LANES)) + col_first
    tile = Tile(stripe, 1, top, bottom, jnp.where(held, 1.0, 0.0).astype(F32), 0)
    return tile, row_first, jnp.broadcast_to(columns, (8, LANES))


def join_edges(west, east, rim):
    lane = lane_ids(west.shape)
    moved = pltpu.roll(jnp.where(lane < RIM, rim, east), 72, 1)
    return jnp.where(lane < 16, west, jnp.where(lane >= LANES - RIM, rim, moved))


def trig_kernel(phase_ref, c0, s0, c1, s1):
    for t in range(c0.shape[0]):
        for k, (c, s) in enumerate(((c0, s0), (c1, s1))):
            for r in range(0, c.shape[1], 16):
                s[t, r : r + 16, :], c[t, r : r + 16, :] = sine_cosine(phase_ref[k, r : r + 16, own_columns(t)])


def ahead_kernel(sizes, own_c0, own_s0, own_c1, own_s1, partner_ref, along_ref,
                 c0, s0, c1, s1, w0r, w0i, w1r, w1i, ur_ref, ui_ref, hr, hi, row_r, row_i, col_r, col_i):
    stripe, tiles, total_rows, total_cols = sizes
    tile, row_first, col_first = main_tile(sizes)
    illum, _, _ = place()
    low_illum = illum == 0
    blank_rims((w0r, w0i, w1r, w1i, hr, hi), tile)
    trig = (c0, s0), (c1, s1)
    end = 2 * RIM + stripe
    for t in range(tiles):
        for k, (mine, here) in enumerate((((own_c0, own_s0), trig[0]), ((own_c1, own_s1), trig[1]))):
            far, near = along_ref[:, own_columns(t + k * tiles)], partner_ref[:, own_columns(t + k * tiles)]
            above = sine_cosine(jnp.where(low_illum, far, near))
            below = sine_cosine(jnp.where(low_illum, near, far))
            for part in range(2):
                here[part][t, 2 * RIM : end, :] = mine[part][t]
                here[part][t, RIM : 2 * RIM, :] = above[1 - part]
                here[part][t, end : end + RIM, :] = below[1 - part]
    forward(
        tile, partner_ref[:, 2 * tiles * LANES :], rim_columns(tile, col_first, col_r.shape), row_first,
        (total_rows, total_cols), trig, (hr, hi), (row_r, row_i, col_r, col_i),
        (w0r, w0i), (w1r, w1i), keep_in((ur_ref, ui_ref)),
    )


def own_kernel(sizes, c0, s0, c1, s1, measured_ref, known_ref, same_ref,
               own_ref, w0r, w0i, w1r, w1i, gr, gi, hr, hi, mr, mi, row_r, row_i, col_r, col_i):
    stripe, tiles, total_rows, total_cols = sizes
    tile, row_first, col_first = main_tile(sizes)
    illum, _, _ = place()
    low_illum = illum == 0
    blank_rims((w0r, w0i, w1r, w1i, gr, gi, hr, hi), tile)
    trig = (c0, s0), (c1, s1)
    mine = illum * stripe
    near_base = pl.multiple_of(stripe - 16 * illum, 16)

    def middle(part, t, r):
        return measured_ref[part, 0, pl.ds(pl.multiple_of(mine + r, 16), 16), own_columns(t)].astype(F32)

    def near(t):
        both = [measured_ref[part, 0, pl.ds(near_base, 16), own_columns(t)].astype(F32) for part in range(2)]
        return [jnp.where(low_illum, x[:8], x[8:]) for x in both]

    fill_target(tile, (mr, mi), low_illum, middle, near, lambda t: same_ref[:, own_columns(t)])
    forward(
        tile, known_ref[...], rim_columns(tile, col_first, col_r.shape), row_first,
        (total_rows, total_cols), trig, (hr, hi), (row_r, row_i, col_r, col_i),
        (w0r, w0i), (w1r, w1i), residual_in((gr, gi), (mr, mi)),
    )
    backward(tile, (gr, gi), (hr, hi), (w0r, w0i), (w1r, w1i), trig[1], put_in(own_ref))


def other_near(swap_ref, stripe, low_illum, columns):
    packed = swap_ref[2 * stripe :, columns]
    high, low = unpack_rows(packed, False), unpack_rows(packed, True)
    return [jnp.where(low_illum, low[part], high[part]) for part in range(2)]


def other_kernel(sizes, swap_ref, along_ref, sums_ref, w0r, w0i, w1r, w1i, ur_ref, ui_ref, c1, s1, out_ref, gr, gi, hr, hi, mr, mi):
    stripe, tiles, _, _ = sizes
    tile, _, _ = main_tile(sizes)
    illum, _, _ = place()
    blank_rims((gr, gi, hr, hi), tile)
    fill_target(
        tile, (mr, mi), illum == 0,
        lambda part, t, r: swap_ref[part * stripe + r : part * stripe + r + 16, own_columns(t)],
        lambda t: other_near(swap_ref, stripe, illum == 0, own_columns(t)),
        lambda t: along_ref[:, own_columns(t + 2 * tiles)],
    )
    residual_of(tile, (gr, gi), (ur_ref, ui_ref), (mr, mi))
    backward(tile, (gr, gi), (hr, hi), (w0r, w0i), (w1r, w1i), (c1, s1), put_in(out_ref))


def patch_kernel(sizes, phase_ref, measured_ref, known_ref, partner_ref, along_ref, same_ref, phase_rim_ref, rim_ref,
                 own_ref, o0r, o0i, o1r, o1i, o2r, o2i, c1, s1,
                 c0, s0, w0r, w0i, w1r, w1i, gr, gi, hr, hi, mr, mi, row_r, row_i, col_r, col_i):
    stripe, tiles, total_rows, total_cols = sizes
    tile, row_first, columns = patch_tile(sizes)
    illum, _, _ = place()
    low_illum = illum == 0
    blank_rims((w0r, w0i, w1r, w1i, gr, gi, hr, hi, o0r, o0i, o1r, o1i), tile)
    trig = (c0, s0), (c1, s1)
    first, last = 0, tiles - 1

    def joined(get, rim):
        return join_edges(get(first), get(last), rim)

    end = stripe + RIM
    fill_trig(
        tile, trig, low_illum,
        lambda k, t, r: joined(lambda e: phase_ref[k, r : r + 16, own_columns(e)], phase_rim_ref[k, RIM + r : RIM + r + 16, :]),
        lambda k, t: joined(
            lambda e: partner_ref[:, own_columns(e + k * tiles)],
            jnp.where(low_illum, phase_rim_ref[k, end:, :], phase_rim_ref[k, :RIM, :]),
        ),
        lambda k, t: joined(
            lambda e: along_ref[:, own_columns(e + k * tiles)],
            jnp.where(low_illum, phase_rim_ref[k, :RIM, :], phase_rim_ref[k, end:, :]),
        ),
    )
    mine = illum * stripe
    near_base = pl.multiple_of(stripe - 16 * illum, 16)
    near_rim = pl.multiple_of(stripe - 8 * illum, 8)

    def middle(part, t, r):
        at = pl.ds(pl.multiple_of(mine + r, 16), 16)
        return joined(lambda e: measured_ref[part, 0, at, own_columns(e)].astype(F32), rim_ref[part, at, :])

    def near(t):
        def rows(part, e):
            x = measured_ref[part, 0, pl.ds(near_base, 16), own_columns(e)].astype(F32)
            return jnp.where(low_illum, x[:8], x[8:])

        return [joined(lambda e: rows(part, e), rim_ref[part, pl.ds(near_rim, 8), :]) for part in range(2)]

    def far(t):
        return joined(lambda e: same_ref[:, own_columns(e)], rim_ref[0, 2 * stripe :, :])

    fill_target(tile, (mr, mi), low_illum, middle, near, far)
    half = hr, hi
    totals, tables = (total_rows, total_cols), (row_r, row_i, col_r, col_i)
    forward(
        tile, partner_ref[:, 2 * tiles * LANES :], columns, row_first, totals, trig, half, tables,
        (o0r, o0i), (o1r, o1i), keep_in((o2r, o2i)),
    )
    forward(
        tile, known_ref[...], columns, row_first, totals, trig, half, tables,
        (w0r, w0i), (w1r, w1i), residual_in((gr, gi), (mr, mi)),
    )
    backward(tile, (gr, gi), half, (w0r, w0i), (w1r, w1i), trig[1], put_in(own_ref))


def finish_kernel(sizes, own_ref, other_ref, own_patch_ref, swap_ref, along_ref, rim_ref, sums_ref, far_sums_ref, partner_relay_ref,
                  w0r, w0i, w1r, w1i, ur_ref, ui_ref, c1, s1, out_ref, other_patch, gr, gi, hr, hi, mr, mi):
    stripe, tiles, total_rows, total_cols = sizes
    tile, _, _ = patch_tile(sizes)
    illum, _, _ = place()
    low_illum = illum == 0
    blank_rims((gr, gi, hr, hi), tile)

    lane = lane_ids((8, LANES))
    sums = jnp.maximum(sums_ref[...], far_sums_ref[...])
    scales = []
    for which in range(2):
        here = jnp.where((lane >= 4 * which) & (lane < 4 * which + 4), sums, 0.0)
        energy = jnp.sum(here[:1], axis=1, keepdims=True) / (total_rows * total_cols) + EPS_ENERGY
        scales.append(2.0 / energy)
    mine = jnp.where(low_illum, scales[0], scales[1])
    others = jnp.where(low_illum, scales[1], scales[0])
    first, last = own_columns(0), own_columns(tiles - 1)

    def middle(part, t, r):
        rim = partner_relay_ref[r : r + 16, :]
        at = slice(part * stripe + r, part * stripe + r + 16)
        return join_edges(swap_ref[at, first], swap_ref[at, last], pltpu.roll(rim, LANES // 2, 1) if part else rim)

    def near(t):
        rim = partner_relay_ref[stripe : stripe + 8, :]
        rims = [rim, pltpu.roll(rim, LANES // 2, 1)]
        west, east = [other_near(swap_ref, stripe, low_illum, at) for at in (first, last)]
        return [join_edges(*x) for x in zip(west, east, rims)]

    def far(t):
        west, east = [along_ref[:, own_columns(e + 2 * tiles)] for e in (0, tiles - 1)]
        return join_edges(west, east, rim_ref[1, 2 * stripe :, :])

    fill_target(tile, (mr, mi), low_illum, middle, near, far)
    residual_of(tile, (gr, gi), (ur_ref, ui_ref), (mr, mi))
    backward(tile, (gr, gi), (hr, hi), (w0r, w0i), (w1r, w1i), (c1, s1), put_in(other_patch))

    for k in range(2):
        for t in range(tiles):
            out_ref[k, :, own_columns(t)] = own_ref[k, :, own_columns(t)] * mine + other_ref[k, :, own_columns(t)] * others
        patch = own_patch_ref[k] * mine + other_patch[k] * others
        on = lane_ids(patch.shape)
        out_ref[k, :, first] = jnp.where(on < RIM, patch, out_ref[k, :, first])
        out_ref[k, :, last] = jnp.where(on >= LANES - RIM, pltpu.roll(patch, 56, 1), out_ref[k, :, last])


def like(x, held):
    shape, dtype = (x, F32) if isinstance(x, tuple) else (x.shape, x.dtype)
    return pltpu.VMEM(shape, dtype) if held else jax.ShapeDtypeStruct(shape, dtype)


def call(kernel, outs, *args, scratch=(), in_place=0, flops=0, mib=8, held=()):
    return pl.pallas_call(
        kernel,
        out_shape=[like(x, n in held) for n, x in enumerate(outs)],
        in_specs=[pl.BlockSpec(memory_space=pltpu.HBM)] * in_place
        + [pl.BlockSpec(memory_space=pltpu.VMEM)] * (len(args) - in_place),
        out_specs=[pl.BlockSpec(memory_space=pltpu.VMEM)] * len(outs),
        scratch_shapes=[pltpu.VMEM(s, F32) if isinstance(s, tuple) else s for s in scratch],
        compiler_params=pltpu.CompilerParams(vmem_limit_bytes=int(mib * 2**20)),
        cost_estimate=pl.CostEstimate(flops=flops, bytes_accessed=2**18, transcendentals=0),
    )(*args)


def paired(phase_delay, angles, measured):
    slices, stripe, width = phase_delay.shape
    rows, cols = lax.axis_size("row"), lax.axis_size("col")
    tiles = width // LANES
    sizes = (stripe, tiles, 2 * stripe * rows, width * cols)
    swap = [(0, 1), (1, 0)]
    along = []
    for r in range(rows):
        along += [(rows + r, (r + 1) % rows), ((r + 1) % rows, rows + r)]
    same = [(r, (r + 1) % rows) for r in range(rows)] + [(rows + (r + 1) % rows, rows + r) for r in range(rows)]

    partner_out, along_out, same_out, known, measured = call(
        open_kernel, [(8, 2 * width + LANES), (8, 3 * width + LANES), (8, width + LANES), (8, LANES), measured],
        phase_delay, measured, angles, in_place=3, mib=62, held=(4,),
        scratch=[
            (2, slices, 8, width),
            pltpu.VMEM(angles.shape, angles.dtype), pltpu.SemaphoreType.DMA((4,)),
        ],
    )
    along_in = lax.ppermute(along_out, ("illum", "row"), along)
    partner_in = lax.ppermute(partner_out, "illum", swap)
    same_in = lax.ppermute(same_out, ("illum", "row"), same)
    (swap_out,) = call(swap_kernel, [(2 * stripe + 8, width)], measured, same_in)
    swap_in = lax.ppermute(swap_out, "illum", swap)
    rims = 8 * (-(-(stripe // 4 + 1) // 4))
    first_out, second_packed, note = call(
        rim_pack_kernel, [(rims + 8, LANES), (rims, LANES), (8, LANES)], phase_delay, measured, known, partner_in, along_in, same_in
    )
    first_in = lax.ppermute(first_out, "col", [(c, c ^ 1) for c in range(cols)])
    (second_out,) = call(second_kernel, [(rims + 8, LANES)], second_packed, note, first_in)
    second_in = lax.ppermute(second_out, "col", [(c, cols - 1 - c) for c in range(cols)])

    def fields(count):
        return [(count, stripe + 4 * RIM, LANES)]

    def tables(count):
        return [(stripe + 2 * RIM, LANES)] * 2 + [(-(-count // 8) * 8, LANES)] * 2

    rows_in = phase_delay, measured, known, partner_in, along_in, same_in
    own_trig = call(trig_kernel, [(tiles, stripe, LANES)] * 4, phase_delay, flops=10**9)
    kept = call(
        functools.partial(ahead_kernel, sizes), fields(tiles) * 10, *own_trig, partner_in, along_in,
        scratch=fields(tiles) * 2 + tables(tiles), flops=15*10**8, mib=16,
    )
    (own,) = call(
        functools.partial(own_kernel, sizes), [phase_delay.shape], *kept[:4], measured, known, same_in,
        scratch=fields(tiles) * 10 + tables(tiles), flops=3*10**9, mib=16,
    )
    phase_rim, rim, relay, sums = call(
        rim_unpack_kernel, [(2, stripe + 2 * RIM, LANES), (2, 2 * stripe + 8, LANES), (stripe + 8, LANES), (8, LANES)], first_in, second_in, note
    )
    partner_relay = lax.ppermute(relay, "illum", swap)
    far_sums = lax.ppermute(sums, "row", [(r, r ^ 2) for r in range(rows)])
    (other,) = call(
        functools.partial(other_kernel, sizes), [phase_delay.shape], swap_in, along_in, sums, *kept[4:], *kept[2:4],
        scratch=fields(tiles) * 6, flops=10**9, mib=12,
    )
    own_patch, *patch_kept = call(
        functools.partial(patch_kernel, sizes), [(slices, stripe, LANES)] + fields(1) * 8, *rows_in, phase_rim, rim,
        scratch=fields(1) * 12 + tables(1), flops=10**9,
    )
    (out,) = call(
        functools.partial(finish_kernel, sizes), [phase_delay.shape],
        own, other, own_patch, swap_in, along_in, rim, sums, far_sums, partner_relay, *patch_kept,
        scratch=[(slices, stripe, LANES)] + fields(1) * 6,
    )
    return out


def halo(x, axis, dim, width, index_of=None):
    peers = lax.axis_size(axis)
    up = [(i, i + 1) for i in range(peers - 1)]
    before = lax.ppermute(lax.slice_in_dim(x, x.shape[dim] - width, x.shape[dim], axis=dim), axis, up)
    after = lax.ppermute(lax.slice_in_dim(x, 0, width, axis=dim), axis, [(j, i) for i, j in up])
    return before, after


def with_column_rims(x, width):
    before, after = halo(x, "col", x.ndim - 1, width)
    gap = jnp.zeros(x.shape[:-1] + (LANES - 2 * width,), x.dtype)
    return jnp.concatenate([x, after, gap, before], axis=-1)


def stripe_halo(x, width):
    illums, rows = lax.axis_size("illum"), lax.axis_size("row")
    where = [(s % illums) * rows + s // illums for s in range(illums * rows)]
    up = [(where[s], where[s + 1]) for s in range(illums * rows - 1)]
    before = lax.ppermute(x[:, -width:], ("illum", "row"), up)
    after = lax.ppermute(x[:, :width], ("illum", "row"), [(b, a) for a, b in up])
    return jnp.concatenate([before, x, after], axis=1)


def per_device(phase_delay, angles, measured):
    illums = lax.axis_size("illum")
    if (illums, lax.axis_size("row"), lax.axis_size("col")) == (2, 4, 4):
        return paired(phase_delay, angles, measured)
    slices, stripe, width = phase_delay.shape
    tile_rows = measured.shape[2]
    total_rows, total_cols = tile_rows * lax.axis_size("row"), width * lax.axis_size("col")
    tiles = width // LANES + 1
    row_first = lax.axis_index("row") * tile_rows + lax.axis_index("illum") * stripe
    col_first = lax.axis_index("col") * width

    target = measured[:, 0].astype(F32)
    energy = lax.psum(jnp.sum(target * target).reshape(1), ("row", "col"))
    energies = lax.all_gather(energy, "illum", tiled=True) / (total_rows * total_cols) + EPS_ENERGY
    tilts = lax.all_gather(angles, "illum", tiled=True)

    phase = with_column_rims(stripe_halo(phase_delay, RIM), RIM)
    above, below = halo(target, "row", 1, REACH)
    target = with_column_rims(jnp.concatenate([above, target, below], axis=1), REACH)
    windows = jnp.stack([target[:, i * stripe : (i + 1) * stripe + 2 * REACH] for i in range(illums)])
    windows = lax.all_to_all(windows, "illum", 0, 0, tiled=True)
    windows = jnp.pad(windows, ((0, 0), (0, 0), (RIM - REACH, RIM - REACH), (0, 0)))

    field = pltpu.VMEM((tiles, stripe + 4 * RIM, LANES), F32)
    rows_all = stripe + 2 * RIM
    return pl.pallas_call(
        functools.partial(gradient_kernel, (stripe, tiles, illums, total_rows, total_cols)),
        out_shape=jax.ShapeDtypeStruct(phase_delay.shape, F32),
        in_specs=[pl.BlockSpec(memory_space=pltpu.SMEM)] * 3 + [pl.BlockSpec(memory_space=pltpu.VMEM)] * 2,
        out_specs=pl.BlockSpec(memory_space=pltpu.VMEM),
        scratch_shapes=[field] * 12
        + [pltpu.VMEM((rows_all, LANES), F32)] * 2
        + [pltpu.VMEM((-(-tiles // 8) * 8, LANES), F32)] * 2,
        compiler_params=pltpu.CompilerParams(vmem_limit_bytes=48 * 2**20),
    )(jnp.stack([row_first, col_first]), tilts, 2.0 / energies, phase, windows)


def solution(mesh):
    placed = (P(None, ("row", "illum"), "col"), P("illum", None), P(None, "illum", "row", "col"))
    return jax.shard_map(
        per_device,
        mesh=mesh,
        in_specs=placed,
        out_specs=P(None, ("row", "illum"), "col"),
        check_vma=False,
    )
```

```python
import functools
import math

import jax
import jax.numpy as jnp
from jax import lax
from jax.experimental import pallas as pl
from jax.experimental.pallas import tpu as pltpu
from jax.sharding import PartitionSpec as P

EPS_ENERGY = 1e-06
RIM = 8
REACH = 4
LANES = 128
F32 = jnp.float32


def sine_cosine(x):
    y = x * x
    s = -2.5052108385441718e-08
    for c in (2.7557319223985893e-06, -1.9841269841269841e-04, 8.333333333333333e-03, -1.6666666666666666e-01):
        s = s * y + c
    c_ = -2.7557319223985888e-07
    for c in (2.48015873015873e-05, -1.3888888888888889e-03, 4.1666666666666664e-02, -0.5, 1.0):
        c_ = c_ * y + c
    return x + x * y * s, c_


def sine_cosine_of_turns(turns):
    quarters = 4.0 * (turns - jnp.floor(turns))
    nearest = jnp.floor(quarters + 0.5)
    s, c = sine_cosine((quarters - nearest) * (0.5 * math.pi))
    odd = (nearest == 1.0) | (nearest == 3.0)
    s, c = jnp.where(odd, c, s), jnp.where(odd, s, c)
    s = jnp.where((nearest == 2.0) | (nearest == 3.0), -s, s)
    c = jnp.where((nearest == 1.0) | (nearest == 2.0), -c, c)
    return s, c


def lane_ids(shape):
    return lax.broadcasted_iota(jnp.int32, shape, len(shape) - 1)


class Tile:
    def __init__(self, stripe, tiles, top, bottom, lanes=None, rim=None, alone=()):
        self.stripe, self.tiles = stripe, tiles
        self.rows = stripe + 2 * RIM
        self.top, self.bottom, self.lanes, self.rim = top, bottom, lanes, rim
        self.alone = alone
        self.owned = tiles if rim in alone or rim is None else tiles - 1
        step = 32 if stripe % 32 == 0 else 8
        self.inner = [(2 * RIM + r, step, None) for r in range(0, stripe, step)]
        self.blocks = [(RIM, RIM, top)] + self.inner + [(2 * RIM + stripe, RIM, bottom)]

    def sweep(self, body, blocks, fields=()):
        for first, count, factor in blocks:
            rows = pl.ds(first, count)
            held = {}

            def load(ref, t, rows=rows, held=held):
                key = id(ref), t
                if key not in held:
                    held[key] = ref[t, rows, :]
                return held[key]

            for t in [*self.alone, *range(self.tiles - len(self.alone))]:

                def mask(x, factor=factor, lanes=self.lanes if t == self.rim else None):
                    x = x if factor is None else x * factor
                    return x if lanes is None else x * lanes

                body(t, rows, mask, [self.beside(ref, t, rows, load) for ref in fields])

    def beside(self, ref, t, rows, load):
        above = pl.ds(rows.start - 1, rows.size)
        below = pl.ds(rows.start + 1, rows.size)
        here = load(ref, t)
        west = east = here
        if t not in self.alone:
            ring = self.tiles - len(self.alone)
            lane = lane_ids(here.shape)
            west = jnp.where(lane == LANES - 1, load(ref, (t - 1) % ring), here)
            east = jnp.where(lane == 0, load(ref, (t + 1) % ring), here)
        west, east = pltpu.roll(west, 1, 1), pltpu.roll(east, LANES - 1, 1)
        return here, (ref[t, above, :] + ref[t, below, :]) + (west + east)


def first_half(tile, field, half, sign, blocks):
    def body(t, rows, mask, sums):
        (real, beside_real), (imag, beside_imag) = sums
        half[0][t, rows, :] = mask(beside_real + (2.0 * sign) * imag)
        half[1][t, rows, :] = mask(beside_imag - (2.0 * sign) * real)

    tile.sweep(body, blocks, field)


def second_half(tile, field, half, blocks, use):
    def body(t, rows, mask, sums):
        (_, beside_real), (_, beside_imag) = sums
        use(t, rows, mask, 0.1 * beside_real - field[0][t, rows, :], 0.1 * beside_imag - field[1][t, rows, :])

    tile.sweep(body, blocks, half)


def blank_rims(refs, tile):
    for ref in refs:
        for first in (0, tile.rows + RIM):
            ref[:, first : first + RIM, :] = jnp.zeros((tile.tiles, RIM, LANES), F32)


def rim_columns(tile, col_first, shape):
    at, on = lax.broadcasted_iota(jnp.int32, shape, 0), lane_ids(shape)
    return col_first + jnp.where((at >= tile.owned) & (on >= LANES // 2), on - LANES, at * LANES + on)


def incident_tables(tile, tilts, row_first, columns, total_rows, total_cols, tables):
    row_r, row_i, col_r, col_i = tables
    ids = lax.broadcasted_iota(jnp.int32, (tile.rows, LANES), 0) + (row_first - RIM)
    s, c = sine_cosine_of_turns(ids.astype(F32) * tilts[0] / total_rows)
    row_r[...] = (-7.0 * c - 24.0 * s) * 0.04
    row_i[...] = (-7.0 * s + 24.0 * c) * 0.04
    col_i[...], col_r[...] = sine_cosine_of_turns(columns.astype(F32) * tilts[1] / total_cols)


def enter(tile, tables, trig, field):
    row_r, row_i, col_r, col_i = tables
    fr, fi = field

    def start(t, rows, mask, _):
        at = pl.ds(rows.start - RIM, rows.size)
        ar, ai = row_r[at, :], row_i[at, :]
        br, bi = col_r[t : t + 1, :], col_i[t : t + 1, :]
        ur, ui = ar * br - ai * bi, ar * bi + ai * br
        c, s = trig[0][t, rows, :], trig[1][t, rows, :]
        fr[t, rows, :] = mask(ur * c - ui * s)
        fi[t, rows, :] = mask(ur * s + ui * c)

    tile.sweep(start, tile.blocks)


def modulate_into(trig, field):
    def use(t, rows, mask, ur, ui):
        c, s = trig[0][t, rows, :], trig[1][t, rows, :]
        field[0][t, rows, :] = mask(ur * c - ui * s)
        field[1][t, rows, :] = mask(ur * s + ui * c)

    return use


def backward(tile, adjoint, half, w0, w1, trig1, put, between=None, on_middle=None):
    between = between or adjoint
    gr, gi = between
    inner = [first for first, _, _ in tile.inner]

    def back(t, rows, mask, ur, ui):
        if t < tile.owned and rows.start in inner:
            put(1, t, rows, ui * w1[0][t, rows, :] - ur * w1[1][t, rows, :])
        c, s = trig1[0][t, rows, :], trig1[1][t, rows, :]
        gr[t, rows, :] = mask(ur * c + ui * s)
        gi[t, rows, :] = mask(ui * c - ur * s)

    def last(t, rows, mask, ur, ui):
        if t < tile.owned:
            put(0, t, rows, ui * w0[0][t, rows, :] - ur * w0[1][t, rows, :])

    first_half(tile, adjoint, half, -1.0, tile.blocks)
    second_half(tile, adjoint, half, tile.blocks, back)
    if on_middle:
        on_middle()
    first_half(tile, between, half, -1.0, tile.blocks)
    second_half(tile, between, half, tile.inner, last)


def own_columns(t):
    return slice(t * LANES, (t + 1) * LANES)


def own_rows(rows):
    return slice(rows.start - 2 * RIM, rows.start - 2 * RIM + rows.size)


def gradient_kernel(sizes, place_ref, angles_ref, scale_ref, phase_ref, target_ref, out_ref,
                    c0, s0, c1, s1, w0r, w0i, w1r, w1i, gr, gi, hr, hi, row_r, row_i, col_r, col_i):
    stripe, tiles, illums, total_rows, total_cols = sizes
    row_first, col_first = place_ref[0], place_ref[1]
    edges = edges_of(row_first, col_first, stripe, tiles, total_rows, total_cols)
    tile = Tile(stripe, tiles, *edges, rim=tiles - 1)
    blank_rims((w0r, w0i, w1r, w1i, gr, gi, hr, hi), tile)
    out_ref[...] = jnp.zeros(out_ref.shape, F32)
    span = slice(RIM, RIM + tile.rows)
    for t in range(tiles):
        for k, (c, s) in enumerate(((c0, s0), (c1, s1))):
            s[t, span, :], c[t, span, :] = sine_cosine(phase_ref[k, :, own_columns(t)])
    tables, half = (row_r, row_i, col_r, col_i), (hr, hi)

    def illum(j, carry):
        tilts = angles_ref[j, 0].astype(F32), angles_ref[j, 1].astype(F32)
        incident_tables(tile, tilts, row_first, rim_columns(tile, col_first, col_r.shape), total_rows, total_cols, tables)
        enter(tile, tables, (c0, s0), (w0r, w0i))
        first_half(tile, (w0r, w0i), half, 1.0, tile.blocks)
        second_half(tile, (w0r, w0i), half, tile.blocks, modulate_into((c1, s1), (w1r, w1i)))
        first_half(tile, (w1r, w1i), half, 1.0, tile.blocks)

        def residual(t, rows, mask, ur, ui):
            at = slice(rows.start - RIM, rows.start - RIM + rows.size)
            gr[t, rows, :] = mask(ur - target_ref[j, 0, at, own_columns(t)])
            gi[t, rows, :] = mask(ui - target_ref[j, 1, at, own_columns(t)])

        second_half(tile, (w1r, w1i), half, tile.blocks, residual)

        def put(k, t, rows, value):
            at = (k, own_rows(rows), own_columns(t))
            out_ref[at] = out_ref[at] + scale_ref[j] * value

        backward(tile, (gr, gi), half, (w0r, w0i), (w1r, w1i), (c1, s1), put)
        return carry

    lax.fori_loop(0, illums, illum, 0)


def edges_of(row_first, col_first, stripe, tiles, total_rows, total_cols):
    width = (tiles - 1) * LANES
    top = jnp.where(row_first == 0, 0.0, 1.0).astype(F32)
    bottom = jnp.where(row_first + stripe == total_rows, 0.0, 1.0).astype(F32)
    lane = lane_ids((1, LANES))
    in_west = (lane >= LANES - RIM) & (col_first > 0)
    in_east = (lane < RIM) & (col_first + width < total_cols)
    return top, bottom, jnp.where(in_west | in_east, 1.0, 0.0).astype(F32)


def place():
    return lax.axis_index("illum"), lax.axis_index("row"), lax.axis_index("col")


def pack_rows(real, imag, low):
    first = lax.broadcasted_iota(jnp.int32, real.shape, 0) < 4
    if low:
        return jnp.where(first, real, pltpu.roll(imag, 4, 0))
    return jnp.where(first, pltpu.roll(real, 4, 0), imag)


def unpack_rows(packed, low):
    turned = pltpu.roll(packed, 4, 0)
    return (packed, turned) if low else (turned, packed)


def edge_blocks(measured_ref, first):
    base = first // 16 * 16
    at = first - base
    return [measured_ref[p, 0, base : base + 16, :].astype(F32)[at : at + 8] for p in range(2)]


def open_kernel(phase_ref, measured_ref, tilt_ref, partner_ref, along_ref, same_ref, known_ref, note_ref, held, edge, tilt, sems):
    stripe, width = phase_ref.shape[1:]
    rows = 2 * stripe
    illum, _, _ = place()
    field_copy = pltpu.make_async_copy(measured_ref, held, sems.at[0])
    tilt_copy = pltpu.make_async_copy(tilt_ref, tilt, sems.at[3])
    edge_copies = [
        pltpu.make_async_copy(phase_ref.at[:, pl.ds(first, 8), :], edge.at[e], sems.at[1 + e])
        for e, first in enumerate((0, stripe - 8))
    ]
    for copy in edge_copies:
        copy.start()
    field_copy.start()
    tilt_copy.start()
    for copy in edge_copies:
        copy.wait()
    for k in range(2):
        top, bottom = edge[0, k], edge[1, k]
        along_ref[:, k * width : (k + 1) * width] = jnp.where(illum == 0, top, bottom)
        partner_ref[:, k * width : (k + 1) * width] = jnp.where(illum == 0, bottom, top)
    field_copy.wait()
    top, bottom = pack_rows(*edge_blocks(held, 0), True), pack_rows(*edge_blocks(held, rows - 8), False)
    along_ref[:, 2 * width :] = jnp.where(illum == 0, top, bottom)
    same_ref[...] = jnp.where(illum == 0, bottom, top)
    total = jnp.zeros((8, width), F32)
    for p in range(2):
        for r in range(0, rows, 16):
            x = held[p, 0, r : r + 16, :].astype(F32)
            x = x * x
            total = total + (x[:8] + x[8:])
    energy = jnp.sum(jnp.sum(total, axis=1, keepdims=True), axis=0, keepdims=True)
    lane = lane_ids((8, LANES))
    note_ref[...] = jnp.where(lane == illum, energy, 0.0)
    note = jnp.zeros((8, LANES), F32)
    tilt_copy.wait()
    for n in range(2):
        note = jnp.where(lane == 16 + n, tilt[:, n : n + 1].astype(F32), note)
    partner_ref[:, 2 * width :] = note
    known_ref[...] = note


def swap_kernel(measured_ref, same_ref, swap_ref):
    stripe = measured_ref.shape[2] // 2
    illum, _, _ = place()
    other = pl.multiple_of((1 - illum) * stripe, 16)
    for p in range(2):
        for r in range(0, stripe, 16):
            at = pl.ds(pl.multiple_of(other + r, 16), 16)
            swap_ref[p * stripe + r : p * stripe + r + 16, :] = measured_ref[p, 0, at, :].astype(F32)
    above = pack_rows(*edge_blocks(measured_ref, stripe - 8), False)
    below = pack_rows(*edge_blocks(measured_ref, stripe), True)
    swap_ref[2 * stripe :, :] = jnp.where(illum == 0, above, below)


def rim_pack_kernel(phase_ref, measured_ref, pair_ref, far_ref, partner_ref, along_ref, same_ref, first_ref, second_ref, note_ref):
    stripe, width = phase_ref.shape[1:]
    rows = 2 * stripe
    illum, _, col = place()
    low_illum = illum == 0
    even = lax.rem(col, 2) == 0
    lane = lane_ids((8, LANES))
    note = pair_ref[...] + far_ref[...]
    note_ref[...] = note
    first_ref[first_ref.shape[0] - 8 :, :] = note

    def packed(east):
        edge = slice(width - LANES, width) if east else slice(0, LANES)
        base = LANES - RIM if east else 0
        groups = []
        for j in range(stripe // 8 + 2):
            items = []
            for k in range(2):
                tile = slice(k * width + edge.start, k * width + edge.stop)
                if j == 0:
                    items.append(jnp.where(low_illum, along_ref[:, tile], partner_ref[:, tile]))
                elif j == stripe // 8 + 1:
                    items.append(jnp.where(low_illum, partner_ref[:, tile], along_ref[:, tile]))
                else:
                    items.append(phase_ref[k, 8 * (j - 1) : 8 * j, edge])
            groups.append(items)
        while len(groups) < rows // 8 + 1:
            groups.append([None, None])
        for r in range(0, rows, 16):
            both = [measured_ref[p, 0, r : r + 16, edge].astype(F32) for p in range(2)]
            for h in range(2):
                groups[r // 8 + h] += [b[8 * h : 8 * h + 8] for b in both]
        groups[rows // 8] += [same_ref[:, edge], along_ref[:, 2 * width + edge.start : 2 * width + edge.stop]]
        for g in range(0, len(groups), 4):
            acc = jnp.zeros((8, LANES), F32)
            for q, items in enumerate(groups[g : g + 4]):
                for k, item in enumerate(items):
                    if item is not None:
                        slot = 4 * q + k
                        shift = (8 * slot - base) % LANES
                        moved = pltpu.roll(item, shift, 1) if shift else item
                        acc = jnp.where((lane >= 8 * slot) & (lane < 8 * slot + 8), moved, acc)
            yield 2 * g, acc

    for (at, east), (_, west) in zip(packed(True), packed(False)):
        first_ref[at : at + 8, :] = jnp.where(even, east, west)
        second_ref[at : at + 8, :] = jnp.where(even, west, east)


def second_kernel(packed_ref, note_ref, first_ref, out_ref):
    rims = packed_ref.shape[0]
    out_ref[:rims, :] = packed_ref[...]
    out_ref[rims:, :] = note_ref[...] + first_ref[rims:, :]


def rim_unpack_kernel(first_ref, second_ref, note_ref, phase_rim_ref, rim_ref, relay_ref):
    stripe = phase_rim_ref.shape[1] - 2 * RIM
    rims, rows = first_ref.shape[0] - 8, 2 * stripe
    illum, _, col = place()
    even = lax.rem(col, 2) == 0
    lane = lane_ids((8, LANES))
    in_west = (lane >= LANES - RIM) & (col > 0)
    in_east = (lane < RIM) & (col < lax.axis_size("col") - 1)
    for g in range(0, rows // 8 + 1, 4):
        first, second = first_ref[2 * g : 2 * g + 8, :], second_ref[2 * g : 2 * g + 8, :]
        a, b = jnp.where(even, second, first), jnp.where(even, first, second)
        for j in range(g, min(g + 4, rows // 8 + 1)):
            for k in range(4):
                if k < 2 and j >= stripe // 8 + 2:
                    continue
                slot = 4 * (j - g) + k
                from_west = pltpu.roll(a, (LANES - RIM - 8 * slot) % LANES, 1)
                from_east = pltpu.roll(b, (-8 * slot) % LANES, 1) if slot else b
                item = jnp.where(in_west, from_west, jnp.where(in_east, from_east, 0.0))
                (phase_rim_ref if k < 2 else rim_ref)[k % 2, 8 * j : 8 * j + 8, :] = item
    other = pl.multiple_of((1 - illum) * stripe, 8)
    near = pl.multiple_of(stripe - 8 + 8 * illum, 8)
    for r in range(0, stripe + 8, 8):
        at = pl.ds(pl.multiple_of(other + r, 8) if r < stripe else near, 8)
        relay_ref[r : r + 8, :] = rim_ref[0, at, :] + pltpu.roll(rim_ref[1, at, :], LANES // 2, 1)
    relay_ref[stripe + 8 :, :] = note_ref[...] + first_ref[rims:, :] + second_ref[rims:, :]


def fill_target(tile, target, low_illum, middle, near, far):
    end = 2 * RIM + tile.stripe
    for t in range(tile.tiles):
        beside_rows, packed = near(t), far(t)
        for part, ref in enumerate(target):
            for r in range(0, tile.stripe, 16):
                ref[t, 2 * RIM + r : 2 * RIM + r + 16, :] = middle(part, t, r)
            ref[t, RIM : 2 * RIM, :] = jnp.where(low_illum, unpack_rows(packed, False)[part], beside_rows[part])
            ref[t, end : end + RIM, :] = jnp.where(low_illum, beside_rows[part], unpack_rows(packed, True)[part])


def fill_trig(tile, trig, low_illum, middle, near, far):
    for t in range(tile.tiles):
        for k, (c, s) in enumerate(trig):
            above, below = far(k, t), near(k, t)
            here = [(RIM, jnp.where(low_illum, above, below)), (2 * RIM + tile.stripe, jnp.where(low_illum, below, above))]
            here += [(2 * RIM + r, middle(k, t, r)) for r in range(0, tile.stripe, 16)]
            for first, x in here:
                s[t, first : first + x.shape[0], :], c[t, first : first + x.shape[0], :] = sine_cosine(x)


def tilts_of(note):
    lane = lane_ids(note.shape)
    return [jnp.sum(jnp.where(lane == n, note, 0.0)[:1], axis=1, keepdims=True) for n in (16, 17)]


def forward(tile, tilts, columns, row_first, totals, trig, half, tables, w0, w1, use):
    incident_tables(tile, tilts, row_first, columns, *totals, tables)
    enter(tile, tables, trig[0], w0)
    first_half(tile, w0, half, 1.0, tile.blocks)
    second_half(tile, w0, half, tile.blocks, modulate_into(trig[1], w1))
    first_half(tile, w1, half, 1.0, tile.blocks)
    second_half(tile, w1, half, tile.blocks, use)


def keep_in(field):
    def use(t, rows, mask, ur, ui):
        field[0][t, rows, :] = ur
        field[1][t, rows, :] = ui

    return use


def residual_in(field, target):
    def use(t, rows, mask, ur, ui):
        field[0][t, rows, :] = mask(ur - target[0][t, rows, :])
        field[1][t, rows, :] = mask(ui - target[1][t, rows, :])

    return use


def residual_of(tile, field, exit_field, target):
    def body(t, rows, mask, _):
        for g, u, m in zip(field, exit_field, target):
            g[t, rows, :] = mask(u[t, rows, :] - m[t, rows, :])

    tile.sweep(body, tile.blocks)


def put_in(ref):
    def put(k, t, rows, value):
        ref[k, own_rows(rows), own_columns(t)] = value

    return put


def main_tile(sizes):
    stripe, tiles, total_rows, total_cols = sizes
    illum, row, col = place()
    row_first = (row * 2 + illum) * stripe
    top, bottom, _ = edges_of(row_first, 0, stripe, tiles + 1, total_rows, total_cols)
    return Tile(stripe, tiles, top, bottom), row_first, col * tiles * LANES


OTHER = 28


def patch_lanes():
    lane = lane_ids((1, LANES))
    other = ((lane >= OTHER - RIM) & (lane < OTHER + 16)) | ((lane >= 56 + OTHER) & (lane < 80 + OTHER))
    return other, jnp.where(other, (lane + (LANES - OTHER)) % LANES, lane)


def patch_held(sizes):
    stripe, tiles, total_rows, total_cols = sizes
    _, _, col_first = main_tile(sizes)
    width = tiles * LANES
    _, at = patch_lanes()
    held = (at < 16) | ((at >= 56) & (at < 72))
    held = held | ((at >= 72) & (at < 80) & (col_first + width < total_cols))
    held = held | ((at >= LANES - RIM) & (col_first > 0))
    columns = jnp.where(at < 16, at, jnp.where(at < 80, at - 72 + width, at - LANES)) + col_first
    return jnp.where(held, 1.0, 0.0).astype(F32), jnp.broadcast_to(columns, (8, LANES))


def join_edges(west, east, rim):
    lane = lane_ids(west.shape)
    moved = pltpu.roll(jnp.where(lane < RIM, rim, east), 72, 1)
    return jnp.where(lane < 16, west, jnp.where(lane >= LANES - RIM, rim, moved))


def join_illums(own, other):
    return jnp.where(patch_lanes()[0], pltpu.roll(other, OTHER, 1), own)


def trig_kernel(phase_ref, c0, s0, c1, s1):
    for t in range(c0.shape[0]):
        for k, (c, s) in enumerate(((c0, s0), (c1, s1))):
            for r in range(0, c.shape[1], 16):
                s[t, r : r + 16, :], c[t, r : r + 16, :] = sine_cosine(phase_ref[k, r : r + 16, own_columns(t)])


def ahead_kernel(sizes, own_c0, own_s0, own_c1, own_s1, partner_ref, along_ref,
                 c0, s0, c1, s1, w0r, w0i, w1r, w1i, ur_ref, ui_ref, hr, hi, row_r, row_i, col_r, col_i):
    stripe, tiles, total_rows, total_cols = sizes
    tile, row_first, col_first = main_tile(sizes)
    illum, _, _ = place()
    low_illum = illum == 0
    blank_rims((w0r, w0i, w1r, w1i, hr, hi), tile)
    trig = (c0, s0), (c1, s1)
    end = 2 * RIM + stripe
    for t in range(tiles):
        for k, (mine, here) in enumerate((((own_c0, own_s0), trig[0]), ((own_c1, own_s1), trig[1]))):
            far, near = along_ref[:, own_columns(t + k * tiles)], partner_ref[:, own_columns(t + k * tiles)]
            above = sine_cosine(jnp.where(low_illum, far, near))
            below = sine_cosine(jnp.where(low_illum, near, far))
            for part in range(2):
                here[part][t, 2 * RIM : end, :] = mine[part][t]
                here[part][t, RIM : 2 * RIM, :] = above[1 - part]
                here[part][t, end : end + RIM, :] = below[1 - part]
    forward(
        tile, tilts_of(partner_ref[:, 2 * tiles * LANES :]), rim_columns(tile, col_first, col_r.shape), row_first,
        (total_rows, total_cols), trig, (hr, hi), (row_r, row_i, col_r, col_i),
        (w0r, w0i), (w1r, w1i), keep_in((ur_ref, ui_ref)),
    )


def own_kernel(sizes, c0, s0, c1, s1, measured_ref, known_ref, same_ref,
               w0r, w0i, w1r, w1i, gr, gi, hr, hi, mr, mi, row_r, row_i, col_r, col_i):
    stripe, tiles, total_rows, total_cols = sizes
    tile, row_first, col_first = main_tile(sizes)
    illum, _, _ = place()
    low_illum = illum == 0
    blank_rims((w0r, w0i, w1r, w1i, gr, gi, hr, hi), tile)
    trig = (c0, s0), (c1, s1)
    mine = illum * stripe
    near_base = pl.multiple_of(stripe - 16 * illum, 16)

    def middle(part, t, r):
        return measured_ref[part, 0, pl.ds(pl.multiple_of(mine + r, 16), 16), own_columns(t)].astype(F32)

    def near(t):
        both = [measured_ref[part, 0, pl.ds(near_base, 16), own_columns(t)].astype(F32) for part in range(2)]
        return [jnp.where(low_illum, x[:8], x[8:]) for x in both]

    fill_target(tile, (mr, mi), low_illum, middle, near, lambda t: same_ref[:, own_columns(t)])
    forward(
        tile, tilts_of(known_ref[...]), rim_columns(tile, col_first, col_r.shape), row_first,
        (total_rows, total_cols), trig, (hr, hi), (row_r, row_i, col_r, col_i),
        (w0r, w0i), (w1r, w1i), residual_in((gr, gi), (mr, mi)),
    )


def back_kernel(sizes, c1, s1, w0r, w0i, w1r, w1i, gr, gi, own_ref, ar, ai, hr, hi):
    tile, _, _ = main_tile(sizes)
    blank_rims((ar, ai, hr, hi), tile)
    backward(tile, (gr, gi), (hr, hi), (w0r, w0i), (w1r, w1i), (c1, s1), put_in(own_ref), (ar, ai))


def other_near(swap_ref, stripe, low_illum, columns):
    packed = swap_ref[2 * stripe :, columns]
    high, low = unpack_rows(packed, False), unpack_rows(packed, True)
    return [jnp.where(low_illum, low[part], high[part]) for part in range(2)]


def patch_kernel(sizes, phase_ref, known_ref, partner_ref, along_ref, phase_rim_ref,
                 w0r, w0i, w1r, w1i, ur_ref, ui_ref, c1, s1, c0, s0, hr, hi, row_r, row_i, col_r, col_i):
    stripe, tiles, total_rows, total_cols = sizes
    main, row_first, _ = main_tile(sizes)
    held, columns = patch_held(sizes)
    tile = Tile(stripe, 1, main.top, main.bottom, held, 0, (0,))
    low_illum = place()[0] == 0
    blank_rims((w0r, w0i, w1r, w1i, hr, hi), tile)
    trig = (c0, s0), (c1, s1)
    end = stripe + RIM

    def joined(get, rim):
        x = join_edges(get(0), get(tiles - 1), rim)
        return join_illums(x, x)

    fill_trig(
        tile, trig, low_illum,
        lambda k, t, r: joined(lambda e: phase_ref[k, r : r + 16, own_columns(e)], phase_rim_ref[k, RIM + r : RIM + r + 16, :]),
        lambda k, t: joined(
            lambda e: partner_ref[:, own_columns(e + k * tiles)],
            jnp.where(low_illum, phase_rim_ref[k, end:, :], phase_rim_ref[k, :RIM, :]),
        ),
        lambda k, t: joined(
            lambda e: along_ref[:, own_columns(e + k * tiles)],
            jnp.where(low_illum, phase_rim_ref[k, :RIM, :], phase_rim_ref[k, end:, :]),
        ),
    )
    note = jnp.where(patch_lanes()[0], 0.0, 1.0)
    tilts = [a * note + b * (1.0 - note) for a, b in zip(tilts_of(known_ref[...]), tilts_of(partner_ref[:, 2 * tiles * LANES :]))]
    forward(
        tile, tilts, columns, row_first, (total_rows, total_cols), trig, (hr, hi), (row_r, row_i, col_r, col_i),
        (w0r, w0i), (w1r, w1i), keep_in((ur_ref, ui_ref)),
    )


def sum_kernel(a_ref, b_ref, out_ref):
    out_ref[...] = a_ref[...] + b_ref[...]


class Joined:
    def __init__(self, main, patch):
        self.main, self.patch, self.tiles = main, patch, main.shape[0]

    def __getitem__(self, at):
        return self.main[at] if at[0] < self.tiles else self.patch[(0,) + at[1:]]


def finish_kernel(sizes, own_ref, measured_ref, swap_ref, along_ref, same_ref, rim_ref, relay_ref, partner_relay_ref,
                  *rest):
    main_fields, patch_fields, rest = rest[:8], rest[8:16], rest[16:]
    out_ref, patch, gr, gi, hr, hi, mr, mi, full, sems = rest
    w0r, w0i, w1r, w1i, ur, ui, c1, s1 = [Joined(a, b) for a, b in zip(main_fields, patch_fields)]
    stripe, tiles, total_rows, total_cols = sizes
    main, _, _ = main_tile(sizes)
    tile = Tile(stripe, tiles + 1, main.top, main.bottom, patch_held(sizes)[0], tiles, (tiles,))
    illum, _, _ = place()
    low_illum = illum == 0
    blank_rims((gr, gi, hr, hi), tile)

    lane = lane_ids((8, LANES))
    sums = jnp.maximum(relay_ref[stripe + 8 :, :], partner_relay_ref[stripe + 8 :, :])
    scales = []
    for which in range(2):
        here = jnp.where(lane == which, sums, 0.0)
        energy = jnp.sum(here[:1], axis=1, keepdims=True) / (total_rows * total_cols) + EPS_ENERGY
        scales.append(2.0 / energy)
    mine = jnp.where(low_illum, scales[0], scales[1])
    others = jnp.where(low_illum, scales[1], scales[0])

    first, last = own_columns(0), own_columns(tiles - 1)
    own_first = illum * stripe
    near_base = pl.multiple_of(stripe - 16 * illum, 16)
    near_rim = pl.multiple_of(stripe - 8 * illum, 8)

    def middle(part, t, r):
        at = slice(part * stripe + r, part * stripe + r + 16)
        if t < tiles:
            return swap_ref[at, own_columns(t)]
        rim = partner_relay_ref[r : r + 16, :]
        other = join_edges(swap_ref[at, first], swap_ref[at, last], pltpu.roll(rim, LANES // 2, 1) if part else rim)
        at = pl.ds(pl.multiple_of(own_first + r, 16), 16)
        own = join_edges(*[measured_ref[part, 0, at, e].astype(F32) for e in (first, last)], rim_ref[part, at, :])
        return join_illums(own, other)

    def near(t):
        if t < tiles:
            return other_near(swap_ref, stripe, low_illum, own_columns(t))
        rim = partner_relay_ref[stripe : stripe + 8, :]
        rims = [rim, pltpu.roll(rim, LANES // 2, 1)]
        west, east = [other_near(swap_ref, stripe, low_illum, at) for at in (first, last)]
        other = [join_edges(*x) for x in zip(west, east, rims)]

        def rows(part, at):
            x = measured_ref[part, 0, pl.ds(near_base, 16), at].astype(F32)
            return jnp.where(low_illum, x[:8], x[8:])

        own = [join_edges(rows(part, first), rows(part, last), rim_ref[part, pl.ds(near_rim, 8), :]) for part in range(2)]
        return [join_illums(*x) for x in zip(own, other)]

    def far(t):
        if t < tiles:
            return along_ref[:, own_columns(t + 2 * tiles)]
        other = join_edges(*[along_ref[:, own_columns(e + 2 * tiles)] for e in (0, tiles - 1)], rim_ref[1, 2 * stripe :, :])
        own = join_edges(same_ref[:, first], same_ref[:, last], rim_ref[0, 2 * stripe :, :])
        return join_illums(own, other)

    fill_target(tile, (mr, mi), low_illum, middle, near, far)
    residual_of(tile, (gr, gi), (ur, ui), (mr, mi))

    def put(k, t, rows, value):
        rows = own_rows(rows)
        if t == tiles:
            patch[k, rows, :] = value * mine + pltpu.roll(value, LANES - OTHER, 1) * others
            return
        value = own_ref[k, rows, own_columns(t)] * mine + value * others
        on = lane_ids(value.shape)
        if t == 0:
            value = jnp.where(on < RIM, patch[k, rows, :], value)
        if t == tiles - 1:
            value = jnp.where(on >= LANES - RIM, pltpu.roll(patch[k, rows, :], 56, 1), value)
        full[k, rows, own_columns(t)] = value

    copies = [pltpu.make_async_copy(full.at[k], out_ref.at[k], sems.at[k]) for k in range(2)]
    backward(tile, (gr, gi), (hr, hi), (w0r, w0i), (w1r, w1i), (c1, s1), put, on_middle=copies[1].start)
    copies[0].start()
    for copy in copies:
        copy.wait()


def like(x, held):
    shape, dtype = (x, F32) if isinstance(x, tuple) else (x.shape, x.dtype)
    return pltpu.VMEM(shape, dtype) if held else jax.ShapeDtypeStruct(shape, dtype)


def after(kernel, *refs):
    count = len(refs)

    def ordered(*args):
        return kernel(*args[count:])

    return ordered


def call(kernel, outs, *args, behind=(), scratch=(), in_place=0, flops=0, mib=8, held=(), far=0):
    kernel, args = after(kernel, *behind), (*behind, *args)
    in_place_specs = [pl.BlockSpec(memory_space=pltpu.HBM)] * in_place
    return pl.pallas_call(
        kernel,
        out_shape=[like(x, n in held) for n, x in enumerate(outs)],
        in_specs=in_place_specs
        + [pl.BlockSpec(memory_space=pltpu.VMEM)] * (len(args) - in_place),
        out_specs=[pl.BlockSpec(memory_space=pltpu.VMEM)] * (len(outs) - far) + [pl.BlockSpec(memory_space=pltpu.HBM)] * far,
        scratch_shapes=[pltpu.VMEM(s, F32) if isinstance(s, tuple) else s for s in scratch],
        compiler_params=pltpu.CompilerParams(vmem_limit_bytes=int(mib * 2**20)),
        cost_estimate=pl.CostEstimate(flops=flops, bytes_accessed=2**18, transcendentals=0),
    )(*args)


def paired(phase_delay, angles, measured):
    slices, stripe, width = phase_delay.shape
    rows, cols = lax.axis_size("row"), lax.axis_size("col")
    tiles = width // LANES
    sizes = (stripe, tiles, 2 * stripe * rows, width * cols)
    swap = [(0, 1), (1, 0)]
    along = []
    for r in range(rows):
        along += [(rows + r, (r + 1) % rows), ((r + 1) % rows, rows + r)]
    same = [(r, (r + 1) % rows) for r in range(rows)] + [(rows + (r + 1) % rows, rows + r) for r in range(rows)]

    partner_out, along_out, same_out, known, note, measured = call(
        open_kernel, [(8, 2 * width + LANES), (8, 3 * width), (8, width), (8, LANES), (8, LANES), measured],
        phase_delay, measured, angles, in_place=3, mib=62, held=(5,),
        scratch=[
            (2, slices, 8, width), pltpu.VMEM(angles.shape, angles.dtype), pltpu.SemaphoreType.DMA((4,)),
        ],
    )
    along_in = lax.ppermute(along_out, ("illum", "row"), along)
    partner_in = lax.ppermute(partner_out, "illum", swap)
    same_in = lax.ppermute(same_out, ("illum", "row"), same)
    core_note = lax.ppermute(note, "row", [(r, r ^ 1) for r in range(rows)])
    (pair,) = call(sum_kernel, [(8, LANES)], note, core_note)
    far = lax.ppermute(pair, "row", [(r, r ^ 2) for r in range(rows)])
    (swap_out,) = call(swap_kernel, [(2 * stripe + 8, width)], measured, core_note)
    swap_in = lax.ppermute(swap_out, "illum", swap)
    def fields(count):
        return [(count, stripe + 4 * RIM, LANES)]

    def tables(count):
        return [(stripe + 2 * RIM, LANES)] * 2 + [(-(-count // 8) * 8, LANES)] * 2

    own_trig = call(trig_kernel, [(tiles, stripe, LANES)] * 4, phase_delay, flops=10**9)
    rims = 8 * (-(-(stripe // 4 + 1) // 4))
    first_out, second_packed, note = call(
        rim_pack_kernel, [(rims + 8, LANES), (rims, LANES), (8, LANES)], phase_delay, measured, pair, far, partner_in, along_in, same_in,
        behind=own_trig[:1],
    )
    first_in = lax.ppermute(first_out, "col", [(c, c ^ 1) for c in range(cols)])
    kept = call(
        functools.partial(ahead_kernel, sizes), fields(tiles) * 10, *own_trig, partner_in, along_in,
        scratch=fields(tiles) * 2 + tables(tiles), flops=15*10**8, mib=16,
    )
    (second_out,) = call(second_kernel, [(rims + 8, LANES)], second_packed, note, first_in, behind=kept[:1])
    second_in = lax.ppermute(second_out, "col", [(c, cols - 1 - c) for c in range(cols)])

    own_kept = call(
        functools.partial(own_kernel, sizes), fields(tiles) * 6, *kept[:4], measured, known, same_in,
        scratch=fields(tiles) * 4 + tables(tiles), flops=15*10**8, mib=16,
    )
    phase_rim, rim, relay = call(
        rim_unpack_kernel, [(2, stripe + 2 * RIM, LANES), (2, 2 * stripe + 8, LANES), (stripe + 16, LANES)],
        first_in, second_in, note,
        behind=own_kept[:1],
    )
    partner_relay = lax.ppermute(relay, "illum", swap)
    (own,) = call(
        functools.partial(back_kernel, sizes), [phase_delay.shape], *kept[2:4], *own_kept,
        scratch=fields(tiles) * 4, flops=10**9, mib=12, behind=[relay],
    )
    patch_kept = call(
        functools.partial(patch_kernel, sizes), fields(1) * 8, phase_delay, known, partner_in, along_in, phase_rim,
        scratch=fields(1) * 4 + tables(1), flops=10**9, behind=[own],
    )
    (out,) = call(
        functools.partial(finish_kernel, sizes), [phase_delay.shape],
        own, measured, swap_in, along_in, same_in, rim, relay, partner_relay, *kept[4:], *kept[2:4], *patch_kept,
        scratch=[(slices, stripe, LANES)] + fields(tiles + 1) * 6 + [phase_delay.shape, pltpu.SemaphoreType.DMA((slices,))], mib=12, flops=0, far=1,
    )
    return out


def halo(x, axis, dim, width, index_of=None):
    peers = lax.axis_size(axis)
    up = [(i, i + 1) for i in range(peers - 1)]
    before = lax.ppermute(lax.slice_in_dim(x, x.shape[dim] - width, x.shape[dim], axis=dim), axis, up)
    after = lax.ppermute(lax.slice_in_dim(x, 0, width, axis=dim), axis, [(j, i) for i, j in up])
    return before, after


def with_column_rims(x, width):
    before, after = halo(x, "col", x.ndim - 1, width)
    gap = jnp.zeros(x.shape[:-1] + (LANES - 2 * width,), x.dtype)
    return jnp.concatenate([x, after, gap, before], axis=-1)


def stripe_halo(x, width):
    illums, rows = lax.axis_size("illum"), lax.axis_size("row")
    where = [(s % illums) * rows + s // illums for s in range(illums * rows)]
    up = [(where[s], where[s + 1]) for s in range(illums * rows - 1)]
    before = lax.ppermute(x[:, -width:], ("illum", "row"), up)
    after = lax.ppermute(x[:, :width], ("illum", "row"), [(b, a) for a, b in up])
    return jnp.concatenate([before, x, after], axis=1)


def per_device(phase_delay, angles, measured):
    illums = lax.axis_size("illum")
    if (illums, lax.axis_size("row"), lax.axis_size("col")) == (2, 4, 4):
        return paired(phase_delay, angles, measured)
    slices, stripe, width = phase_delay.shape
    tile_rows = measured.shape[2]
    total_rows, total_cols = tile_rows * lax.axis_size("row"), width * lax.axis_size("col")
    tiles = width // LANES + 1
    row_first = lax.axis_index("row") * tile_rows + lax.axis_index("illum") * stripe
    col_first = lax.axis_index("col") * width

    target = measured[:, 0].astype(F32)
    energy = lax.psum(jnp.sum(target * target).reshape(1), ("row", "col"))
    energies = lax.all_gather(energy, "illum", tiled=True) / (total_rows * total_cols) + EPS_ENERGY
    tilts = lax.all_gather(angles, "illum", tiled=True)

    phase = with_column_rims(stripe_halo(phase_delay, RIM), RIM)
    above, below = halo(target, "row", 1, REACH)
    target = with_column_rims(jnp.concatenate([above, target, below], axis=1), REACH)
    windows = jnp.stack([target[:, i * stripe : (i + 1) * stripe + 2 * REACH] for i in range(illums)])
    windows = lax.all_to_all(windows, "illum", 0, 0, tiled=True)
    windows = jnp.pad(windows, ((0, 0), (0, 0), (RIM - REACH, RIM - REACH), (0, 0)))

    field = pltpu.VMEM((tiles, stripe + 4 * RIM, LANES), F32)
    rows_all = stripe + 2 * RIM
    return pl.pallas_call(
        functools.partial(gradient_kernel, (stripe, tiles, illums, total_rows, total_cols)),
        out_shape=jax.ShapeDtypeStruct(phase_delay.shape, F32),
        in_specs=[pl.BlockSpec(memory_space=pltpu.SMEM)] * 3 + [pl.BlockSpec(memory_space=pltpu.VMEM)] * 2,
        out_specs=pl.BlockSpec(memory_space=pltpu.VMEM),
        scratch_shapes=[field] * 12
        + [pltpu.VMEM((rows_all, LANES), F32)] * 2
        + [pltpu.VMEM((-(-tiles // 8) * 8, LANES), F32)] * 2,
        compiler_params=pltpu.CompilerParams(vmem_limit_bytes=48 * 2**20),
    )(jnp.stack([row_first, col_first]), tilts, 2.0 / energies, phase, windows)


def solution(mesh):
    placed = (P(None, ("row", "illum"), "col"), P("illum", None), P(None, "illum", "row", "col"))
    return jax.shard_map(
        per_device,
        mesh=mesh,
        in_specs=placed,
        out_specs=P(None, ("row", "illum"), "col"),
        check_vma=False,
    )
```

```python
import functools
import math

import jax
import jax.numpy as jnp
from jax import lax
from jax.experimental import pallas as pl
from jax.experimental.pallas import tpu as pltpu
from jax.sharding import PartitionSpec as P

EPS_ENERGY = 1e-06
RIM = 8
REACH = 4
LANES = 128
F32 = jnp.float32


def sine_cosine(x):
    y = x * x
    s = -2.5052108385441718e-08
    for c in (2.7557319223985893e-06, -1.9841269841269841e-04, 8.333333333333333e-03, -1.6666666666666666e-01):
        s = s * y + c
    c_ = -2.7557319223985888e-07
    for c in (2.48015873015873e-05, -1.3888888888888889e-03, 4.1666666666666664e-02, -0.5, 1.0):
        c_ = c_ * y + c
    return x + x * y * s, c_


def sine_cosine_of_turns(turns):
    quarters = 4.0 * (turns - jnp.floor(turns))
    nearest = jnp.floor(quarters + 0.5)
    s, c = sine_cosine((quarters - nearest) * (0.5 * math.pi))
    odd = (nearest == 1.0) | (nearest == 3.0)
    s, c = jnp.where(odd, c, s), jnp.where(odd, s, c)
    s = jnp.where((nearest == 2.0) | (nearest == 3.0), -s, s)
    c = jnp.where((nearest == 1.0) | (nearest == 2.0), -c, c)
    return s, c


def lane_ids(shape):
    return lax.broadcasted_iota(jnp.int32, shape, len(shape) - 1)


class Tile:
    def __init__(self, stripe, tiles, top, bottom, lanes=None, rim=None, alone=()):
        self.stripe, self.tiles = stripe, tiles
        self.rows = stripe + 2 * RIM
        self.top, self.bottom, self.lanes, self.rim = top, bottom, lanes, rim
        self.alone = alone
        self.order = [*alone, *range(1, tiles - len(alone)), *([0] if tiles > len(alone) else [])]
        self.owned = tiles if rim in alone or rim is None else tiles - 1
        step = 32 if stripe % 32 == 0 else 8
        self.inner = [(2 * RIM + r, step, None) for r in range(0, stripe, step)]
        self.blocks = [(RIM, RIM, top)] + self.inner + [(2 * RIM + stripe, RIM, bottom)]

    def sweep(self, body, blocks, fields=()):
        for first, count, factor in blocks:
            rows = pl.ds(first, count)
            held = {}

            def load(ref, t, rows=rows, held=held):
                key = id(ref), t
                if key not in held:
                    held[key] = ref[t, rows, :]
                return held[key]

            for t in self.order:

                def mask(x, factor=factor, lanes=self.lanes if t == self.rim else None):
                    x = x if factor is None else x * factor
                    return x if lanes is None else x * lanes

                body(t, rows, mask, [self.beside(ref, t, rows, load) for ref in fields])

    def beside(self, ref, t, rows, load):
        above = pl.ds(rows.start - 1, rows.size)
        below = pl.ds(rows.start + 1, rows.size)
        here = load(ref, t)
        west = east = here
        if t not in self.alone:
            ring = self.tiles - len(self.alone)
            lane = lane_ids(here.shape)
            west = jnp.where(lane == LANES - 1, load(ref, (t - 1) % ring), here)
            east = jnp.where(lane == 0, load(ref, (t + 1) % ring), here)
        west, east = pltpu.roll(west, 1, 1), pltpu.roll(east, LANES - 1, 1)
        return here, (ref[t, above, :] + ref[t, below, :]) + (west + east)


def first_half(tile, field, half, sign, blocks):
    def body(t, rows, mask, sums):
        (real, beside_real), (imag, beside_imag) = sums
        half[0][t, rows, :] = mask(beside_real + (2.0 * sign) * imag)
        half[1][t, rows, :] = mask(beside_imag - (2.0 * sign) * real)

    tile.sweep(body, blocks, field)


def second_half(tile, field, half, blocks, use):
    def body(t, rows, mask, sums):
        (_, beside_real), (_, beside_imag) = sums
        use(t, rows, mask, 0.1 * beside_real - field[0][t, rows, :], 0.1 * beside_imag - field[1][t, rows, :])

    tile.sweep(body, blocks, half)


def blank_rims(refs, tile):
    for ref in refs:
        for first in (0, tile.rows + RIM):
            ref[:, first : first + RIM, :] = jnp.zeros((tile.tiles, RIM, LANES), F32)


def rim_columns(tile, col_first, shape):
    at, on = lax.broadcasted_iota(jnp.int32, shape, 0), lane_ids(shape)
    return col_first + jnp.where((at >= tile.owned) & (on >= LANES // 2), on - LANES, at * LANES + on)


def incident_tables(tile, tilts, row_first, columns, total_rows, total_cols, tables):
    row_r, row_i, col_r, col_i = tables
    ids = lax.broadcasted_iota(jnp.int32, (tile.rows, LANES), 0) + (row_first - RIM)
    s, c = sine_cosine_of_turns(ids.astype(F32) * tilts[0] / total_rows)
    row_r[...] = (-7.0 * c - 24.0 * s) * 0.04
    row_i[...] = (-7.0 * s + 24.0 * c) * 0.04
    col_i[...], col_r[...] = sine_cosine_of_turns(columns.astype(F32) * tilts[1] / total_cols)


def enter(tile, tables, trig, field):
    row_r, row_i, col_r, col_i = tables
    fr, fi = field

    def start(t, rows, mask, _):
        at = pl.ds(rows.start - RIM, rows.size)
        ar, ai = row_r[at, :], row_i[at, :]
        br, bi = col_r[t : t + 1, :], col_i[t : t + 1, :]
        ur, ui = ar * br - ai * bi, ar * bi + ai * br
        c, s = trig[0][t, rows, :], trig[1][t, rows, :]
        fr[t, rows, :] = mask(ur * c - ui * s)
        fi[t, rows, :] = mask(ur * s + ui * c)

    tile.sweep(start, tile.blocks)


def modulate_into(trig, field):
    def use(t, rows, mask, ur, ui):
        c, s = trig[0][t, rows, :], trig[1][t, rows, :]
        field[0][t, rows, :] = mask(ur * c - ui * s)
        field[1][t, rows, :] = mask(ur * s + ui * c)

    return use


def backward(tile, adjoint, half, w0, w1, trig1, put, between=None, on_middle=None, on_rows=None):
    between = between or adjoint
    gr, gi = between
    inner = [first for first, _, _ in tile.inner]

    def back(t, rows, mask, ur, ui):
        if t < tile.owned and rows.start in inner:
            put(1, t, rows, ui * w1[0][t, rows, :] - ur * w1[1][t, rows, :])
        c, s = trig1[0][t, rows, :], trig1[1][t, rows, :]
        gr[t, rows, :] = mask(ur * c + ui * s)
        gi[t, rows, :] = mask(ui * c - ur * s)

    def last(t, rows, mask, ur, ui):
        if t < tile.owned:
            put(0, t, rows, ui * w0[0][t, rows, :] - ur * w0[1][t, rows, :])

    first_half(tile, adjoint, half, -1.0, tile.blocks)
    second_half(tile, adjoint, half, tile.blocks, back)
    if on_middle:
        on_middle()
    first_half(tile, between, half, -1.0, tile.blocks)
    for block in tile.inner if on_rows is None else [(r, 16, None) for r in range(2 * RIM, 2 * RIM + tile.stripe, 16)]:
        second_half(tile, between, half, [block], last)
        if on_rows:
            on_rows(block[0] - 2 * RIM)


def own_columns(t):
    return slice(t * LANES, (t + 1) * LANES)


def own_rows(rows):
    return slice(rows.start - 2 * RIM, rows.start - 2 * RIM + rows.size)


def gradient_kernel(sizes, place_ref, angles_ref, scale_ref, phase_ref, target_ref, out_ref,
                    c0, s0, c1, s1, w0r, w0i, w1r, w1i, gr, gi, hr, hi, row_r, row_i, col_r, col_i):
    stripe, tiles, illums, total_rows, total_cols = sizes
    row_first, col_first = place_ref[0], place_ref[1]
    edges = edges_of(row_first, col_first, stripe, tiles, total_rows, total_cols)
    tile = Tile(stripe, tiles, *edges, rim=tiles - 1)
    blank_rims((w0r, w0i, w1r, w1i, gr, gi, hr, hi), tile)
    out_ref[...] = jnp.zeros(out_ref.shape, F32)
    span = slice(RIM, RIM + tile.rows)
    for t in range(tiles):
        for k, (c, s) in enumerate(((c0, s0), (c1, s1))):
            s[t, span, :], c[t, span, :] = sine_cosine(phase_ref[k, :, own_columns(t)])
    tables, half = (row_r, row_i, col_r, col_i), (hr, hi)

    def illum(j, carry):
        tilts = angles_ref[j, 0].astype(F32), angles_ref[j, 1].astype(F32)
        incident_tables(tile, tilts, row_first, rim_columns(tile, col_first, col_r.shape), total_rows, total_cols, tables)
        enter(tile, tables, (c0, s0), (w0r, w0i))
        first_half(tile, (w0r, w0i), half, 1.0, tile.blocks)
        second_half(tile, (w0r, w0i), half, tile.blocks, modulate_into((c1, s1), (w1r, w1i)))
        first_half(tile, (w1r, w1i), half, 1.0, tile.blocks)

        def residual(t, rows, mask, ur, ui):
            at = slice(rows.start - RIM, rows.start - RIM + rows.size)
            gr[t, rows, :] = mask(ur - target_ref[j, 0, at, own_columns(t)])
            gi[t, rows, :] = mask(ui - target_ref[j, 1, at, own_columns(t)])

        second_half(tile, (w1r, w1i), half, tile.blocks, residual)

        def put(k, t, rows, value):
            at = (k, own_rows(rows), own_columns(t))
            out_ref[at] = out_ref[at] + scale_ref[j] * value

        backward(tile, (gr, gi), half, (w0r, w0i), (w1r, w1i), (c1, s1), put)
        return carry

    lax.fori_loop(0, illums, illum, 0)


def edges_of(row_first, col_first, stripe, tiles, total_rows, total_cols):
    width = (tiles - 1) * LANES
    top = jnp.where(row_first == 0, 0.0, 1.0).astype(F32)
    bottom = jnp.where(row_first + stripe == total_rows, 0.0, 1.0).astype(F32)
    lane = lane_ids((1, LANES))
    in_west = (lane >= LANES - RIM) & (col_first > 0)
    in_east = (lane < RIM) & (col_first + width < total_cols)
    return top, bottom, jnp.where(in_west | in_east, 1.0, 0.0).astype(F32)


def place():
    return lax.axis_index("illum"), lax.axis_index("row"), lax.axis_index("col")


def pack_rows(real, imag, low):
    first = lax.broadcasted_iota(jnp.int32, real.shape, 0) < 4
    if low:
        return jnp.where(first, real, pltpu.roll(imag, 4, 0))
    return jnp.where(first, pltpu.roll(real, 4, 0), imag)


def unpack_rows(packed, low):
    turned = pltpu.roll(packed, 4, 0)
    return (packed, turned) if low else (turned, packed)


def edge_blocks(measured_ref, first):
    base = first // 16 * 16
    at = first - base
    return [measured_ref[p, 0, base : base + 16, :].astype(F32)[at : at + 8] for p in range(2)]


def open_kernel(phase_ref, measured_ref, tilt_ref, partner_ref, along_ref, same_ref, known_ref, note_ref, held, edge, tilt, sems):
    stripe, width = phase_ref.shape[1:]
    rows = 2 * stripe
    illum, _, _ = place()
    field_copy = pltpu.make_async_copy(measured_ref, held, sems.at[0])
    tilt_copy = pltpu.make_async_copy(tilt_ref, tilt, sems.at[3])
    edge_copies = [
        pltpu.make_async_copy(phase_ref.at[:, pl.ds(first, 8), :], edge.at[e], sems.at[1 + e])
        for e, first in enumerate((0, stripe - 8))
    ]
    for copy in edge_copies:
        copy.start()
    field_copy.start()
    tilt_copy.start()
    for copy in edge_copies:
        copy.wait()
    for k in range(2):
        top, bottom = edge[0, k], edge[1, k]
        along_ref[:, k * width : (k + 1) * width] = jnp.where(illum == 0, top, bottom)
        partner_ref[:, k * width : (k + 1) * width] = jnp.where(illum == 0, bottom, top)
    field_copy.wait()
    top, bottom = pack_rows(*edge_blocks(held, 0), True), pack_rows(*edge_blocks(held, rows - 8), False)
    along_ref[:, 2 * width :] = jnp.where(illum == 0, top, bottom)
    same_ref[...] = jnp.where(illum == 0, bottom, top)
    total = jnp.zeros((8, width), F32)
    for p in range(2):
        for r in range(0, rows, 16):
            x = held[p, 0, r : r + 16, :].astype(F32)
            x = x * x
            total = total + (x[:8] + x[8:])
    energy = jnp.sum(jnp.sum(total, axis=1, keepdims=True), axis=0, keepdims=True)
    lane = lane_ids((8, LANES))
    note_ref[...] = jnp.where(lane == illum, energy, 0.0)
    note = jnp.zeros((8, LANES), F32)
    tilt_copy.wait()
    for n in range(2):
        note = jnp.where(lane == 16 + n, tilt[:, n : n + 1].astype(F32), note)
    partner_ref[:, 2 * width :] = note
    known_ref[...] = note


def swap_kernel(columns, measured_ref, swap_ref):
    stripe = measured_ref.shape[2] // 2
    illum, _, _ = place()
    other = pl.multiple_of((1 - illum) * stripe, 16)
    for p in range(2):
        for r in range(0, stripe, 16):
            at = pl.ds(pl.multiple_of(other + r, 16), 16)
            swap_ref[p * stripe + r : p * stripe + r + 16, :] = measured_ref[p, 0, at, columns].astype(F32)
    above = pack_rows(*[x[:, columns] for x in edge_blocks(measured_ref, stripe - 8)], False)
    below = pack_rows(*[x[:, columns] for x in edge_blocks(measured_ref, stripe)], True)
    swap_ref[2 * stripe :, :] = jnp.where(illum == 0, above, below)


def rim_pack_kernel(phase_ref, measured_ref, pair_ref, far_ref, partner_ref, along_ref, same_ref, first_ref, second_ref, note_ref):
    stripe, width = phase_ref.shape[1:]
    rows = 2 * stripe
    illum, _, col = place()
    low_illum = illum == 0
    even = lax.rem(col, 2) == 0
    lane = lane_ids((8, LANES))
    note = pair_ref[...] + far_ref[...]
    note_ref[...] = note
    first_ref[first_ref.shape[0] - 8 :, :] = note

    def packed(east):
        edge = slice(width - LANES, width) if east else slice(0, LANES)
        base = LANES - RIM if east else 0
        groups = []
        for j in range(stripe // 8 + 2):
            items = []
            for k in range(2):
                tile = slice(k * width + edge.start, k * width + edge.stop)
                if j == 0:
                    items.append(jnp.where(low_illum, along_ref[:, tile], partner_ref[:, tile]))
                elif j == stripe // 8 + 1:
                    items.append(jnp.where(low_illum, partner_ref[:, tile], along_ref[:, tile]))
                else:
                    items.append(phase_ref[k, 8 * (j - 1) : 8 * j, edge])
            groups.append(items)
        while len(groups) < rows // 8 + 1:
            groups.append([None, None])
        for r in range(0, rows, 16):
            both = [measured_ref[p, 0, r : r + 16, edge].astype(F32) for p in range(2)]
            for h in range(2):
                groups[r // 8 + h] += [b[8 * h : 8 * h + 8] for b in both]
        groups[rows // 8] += [same_ref[:, edge], along_ref[:, 2 * width + edge.start : 2 * width + edge.stop]]
        for g in range(0, len(groups), 4):
            acc = jnp.zeros((8, LANES), F32)
            for q, items in enumerate(groups[g : g + 4]):
                for k, item in enumerate(items):
                    if item is not None:
                        slot = 4 * q + k
                        shift = (8 * slot - base) % LANES
                        moved = pltpu.roll(item, shift, 1) if shift else item
                        acc = jnp.where((lane >= 8 * slot) & (lane < 8 * slot + 8), moved, acc)
            yield 2 * g, acc

    for (at, east), (_, west) in zip(packed(True), packed(False)):
        first_ref[at : at + 8, :] = jnp.where(even, west, east)
        second_ref[at : at + 8, :] = jnp.where(even, east, west)


def second_kernel(packed_ref, note_ref, first_ref, out_ref):
    rims = packed_ref.shape[0]
    out_ref[:rims, :] = packed_ref[...]
    out_ref[rims:, :] = note_ref[...] + first_ref[rims:, :]


def rim_unpack_kernel(first_ref, second_ref, note_ref, phase_rim_ref, rim_ref, relay_ref):
    stripe = phase_rim_ref.shape[1] - 2 * RIM
    rims, rows = first_ref.shape[0] - 8, 2 * stripe
    illum, _, col = place()
    even = lax.rem(col, 2) == 0
    lane = lane_ids((8, LANES))
    in_west = (lane >= LANES - RIM) & (col > 0)
    in_east = (lane < RIM) & (col < lax.axis_size("col") - 1)
    for g in range(0, rows // 8 + 1, 4):
        first, second = first_ref[2 * g : 2 * g + 8, :], second_ref[2 * g : 2 * g + 8, :]
        a, b = jnp.where(even, first, second), jnp.where(even, second, first)
        for j in range(g, min(g + 4, rows // 8 + 1)):
            for k in range(4):
                if k < 2 and j >= stripe // 8 + 2:
                    continue
                slot = 4 * (j - g) + k
                from_west = pltpu.roll(a, (LANES - RIM - 8 * slot) % LANES, 1)
                from_east = pltpu.roll(b, (-8 * slot) % LANES, 1) if slot else b
                item = jnp.where(in_west, from_west, jnp.where(in_east, from_east, 0.0))
                (phase_rim_ref if k < 2 else rim_ref)[k % 2, 8 * j : 8 * j + 8, :] = item
    other = pl.multiple_of((1 - illum) * stripe, 8)
    near = pl.multiple_of(stripe - 8 + 8 * illum, 8)
    blocks = [pl.multiple_of(other + r, 8) for r in range(0, stripe, 8)] + [near]
    for g in range(0, len(blocks), 4):
        packed = jnp.zeros((8, LANES), F32)
        for q, first in enumerate(blocks[g : g + 4]):
            at = pl.ds(first, 8)
            x = rim_ref[0, at, :] + pltpu.roll(rim_ref[1, at, :], LANES // 2, 1)
            packed = packed + (pltpu.roll(x, 2 * RIM * q, 1) if q else x)
        relay_ref[2 * g : 2 * g + 8, :] = packed
    relay_ref[relay_ref.shape[0] - 8 :, :] = note_ref[...] + first_ref[rims:, :] + second_ref[rims:, :]


def fill_target(tile, target, low_illum, middle, near, far, plain=()):
    end = 2 * RIM + tile.stripe
    for t in range(tile.tiles):
        beside_rows, packed = near(t), far(t)
        for part, ref in enumerate(target):
            for r in range(0, tile.stripe, 16) if t not in plain else ():
                ref[t, 2 * RIM + r : 2 * RIM + r + 16, :] = middle(part, t, r)
            ref[t, RIM : 2 * RIM, :] = jnp.where(low_illum, unpack_rows(packed, False)[part], beside_rows[part])
            ref[t, end : end + RIM, :] = jnp.where(low_illum, beside_rows[part], unpack_rows(packed, True)[part])


def fill_trig(tile, trig, low_illum, middle, near, far):
    for t in range(tile.tiles):
        for k, (c, s) in enumerate(trig):
            above, below = far(k, t), near(k, t)
            here = [(RIM, jnp.where(low_illum, above, below)), (2 * RIM + tile.stripe, jnp.where(low_illum, below, above))]
            here += [(2 * RIM + r, middle(k, t, r)) for r in range(0, tile.stripe, 16)]
            for first, x in here:
                s[t, first : first + x.shape[0], :], c[t, first : first + x.shape[0], :] = sine_cosine(x)


def tilts_of(note):
    lane = lane_ids(note.shape)
    return [jnp.sum(jnp.where(lane == n, note, 0.0)[:1], axis=1, keepdims=True) for n in (16, 17)]


def forward(tile, tilts, columns, row_first, totals, trig, half, tables, w0, w1, use):
    incident_tables(tile, tilts, row_first, columns, *totals, tables)
    propagate(tile, tables, trig, half, w0, w1, use)


def propagate(tile, tables, trig, half, w0, w1, use):
    enter(tile, tables, trig[0], w0)
    first_half(tile, w0, half, 1.0, tile.blocks)
    second_half(tile, w0, half, tile.blocks, modulate_into(trig[1], w1))
    first_half(tile, w1, half, 1.0, tile.blocks)
    second_half(tile, w1, half, tile.blocks, use)


def keep_in(field):
    def use(t, rows, mask, ur, ui):
        field[0][t, rows, :] = ur
        field[1][t, rows, :] = ui

    return use


def residual_in(field, target):
    def use(t, rows, mask, ur, ui):
        field[0][t, rows, :] = mask(ur - target[0][t, rows, :])
        field[1][t, rows, :] = mask(ui - target[1][t, rows, :])

    return use


def residual_of(tile, field, exit_field, target):
    def body(t, rows, mask, _):
        for part, (g, u) in enumerate(zip(field, exit_field)):
            g[t, rows, :] = mask(u[t, rows, :] - target(part, t, rows))

    tile.sweep(body, tile.blocks)


def put_in(ref):
    def put(k, t, rows, value):
        ref[k, own_rows(rows), own_columns(t)] = value

    return put


def main_tile(sizes):
    stripe, tiles, total_rows, total_cols = sizes
    illum, row, col = place()
    row_first = (row * 2 + illum) * stripe
    top, bottom, _ = edges_of(row_first, 0, stripe, tiles + 1, total_rows, total_cols)
    return Tile(stripe, tiles, top, bottom), row_first, col * tiles * LANES


OTHER = 28


def patch_lanes():
    lane = lane_ids((1, LANES))
    other = ((lane >= OTHER - RIM) & (lane < OTHER + 16)) | ((lane >= 56 + OTHER) & (lane < 80 + OTHER))
    return other, jnp.where(other, (lane + (LANES - OTHER)) % LANES, lane)


def patch_held(sizes):
    stripe, tiles, total_rows, total_cols = sizes
    _, _, col_first = main_tile(sizes)
    width = tiles * LANES
    _, at = patch_lanes()
    held = (at < 16) | ((at >= 56) & (at < 72))
    held = held | ((at >= 72) & (at < 80) & (col_first + width < total_cols))
    held = held | ((at >= LANES - RIM) & (col_first > 0))
    columns = jnp.where(at < 16, at, jnp.where(at < 80, at - 72 + width, at - LANES)) + col_first
    return jnp.where(held, 1.0, 0.0).astype(F32), jnp.broadcast_to(columns, (8, LANES))


def join_edges(west, east, rim):
    lane = lane_ids(west.shape)
    moved = pltpu.roll(jnp.where(lane < RIM, rim, east), 72, 1)
    return jnp.where(lane < 16, west, jnp.where(lane >= LANES - RIM, rim, moved))


def join_illums(own, other):
    return jnp.where(patch_lanes()[0], pltpu.roll(other, OTHER, 1), own)


def trig_kernel(sizes, phase_ref, measured_ref, known_ref, c0, s0, c1, s1, mr, mi, row_r, row_i, col_r, col_i):
    stripe, tiles, total_rows, total_cols = sizes
    tile, row_first, col_first = main_tile(sizes)
    illum, _, _ = place()
    columns = rim_columns(tile, col_first, col_r.shape)
    tables = (row_r, row_i, col_r, col_i)
    incident_tables(tile, tilts_of(known_ref[...]), row_first, columns, total_rows, total_cols, tables)
    for part, m in enumerate((mr, mi)):
        for t in range(tiles):
            for r in range(0, stripe, 16):
                at = pl.ds(pl.multiple_of(illum * stripe + r, 16), 16)
                m[t, r : r + 16, :] = measured_ref[part, 0, at, own_columns(t)].astype(F32)
    for t in range(c0.shape[0]):
        for k, (c, s) in enumerate(((c0, s0), (c1, s1))):
            for r in range(0, c.shape[1], 16):
                s[t, r : r + 16, :], c[t, r : r + 16, :] = sine_cosine(phase_ref[k, r : r + 16, own_columns(t)])


def ahead_kernel(sizes, own_c0, own_s0, own_c1, own_s1, partner_ref, along_ref,
                 c0, s0, c1, s1, w0r, w0i, w1r, w1i, ur_ref, ui_ref, hr, hi, row_r, row_i, col_r, col_i):
    stripe, tiles, total_rows, total_cols = sizes
    tile, row_first, col_first = main_tile(sizes)
    illum, _, _ = place()
    low_illum = illum == 0
    blank_rims((w0r, w0i, w1r, w1i, hr, hi), tile)
    trig = (c0, s0), (c1, s1)
    end = 2 * RIM + stripe
    for t in range(tiles):
        for k, (mine, here) in enumerate((((own_c0, own_s0), trig[0]), ((own_c1, own_s1), trig[1]))):
            far, near = along_ref[:, own_columns(t + k * tiles)], partner_ref[:, own_columns(t + k * tiles)]
            above = sine_cosine(jnp.where(low_illum, far, near))
            below = sine_cosine(jnp.where(low_illum, near, far))
            for part in range(2):
                here[part][t, 2 * RIM : end, :] = mine[part][t]
                here[part][t, RIM : 2 * RIM, :] = above[1 - part]
                here[part][t, end : end + RIM, :] = below[1 - part]
    forward(
        tile, tilts_of(partner_ref[:, 2 * tiles * LANES :]), rim_columns(tile, col_first, col_r.shape), row_first,
        (total_rows, total_cols), trig, (hr, hi), (row_r, row_i, col_r, col_i),
        (w0r, w0i), (w1r, w1i), keep_in((ur_ref, ui_ref)),
    )


def own_kernel(sizes, c0, s0, c1, s1, mr, mi, row_r, row_i, col_r, col_i, measured_ref, same_ref,
               w0r, w0i, w1r, w1i, gr, gi, hr, hi, above, below):
    stripe, tiles, total_rows, total_cols = sizes
    tile, row_first, col_first = main_tile(sizes)
    illum, _, _ = place()
    low_illum = illum == 0
    blank_rims((w0r, w0i, w1r, w1i, gr, gi, hr, hi), tile)
    trig = (c0, s0), (c1, s1)
    near_base = pl.multiple_of(stripe - 16 * illum, 16)
    for t in range(tiles):
        both = [measured_ref[part, 0, pl.ds(near_base, 16), own_columns(t)].astype(F32) for part in range(2)]
        near = [jnp.where(low_illum, x[:8], x[8:]) for x in both]
        far = same_ref[:, own_columns(t)]
        for part in range(2):
            above[part, t] = jnp.where(low_illum, unpack_rows(far, False)[part], near[part])
            below[part, t] = jnp.where(low_illum, near[part], unpack_rows(far, True)[part])

    def residual(t, rows, mask, ur, ui):
        for part, (g, u, m) in enumerate(((gr, ur, mr), (gi, ui, mi))):
            if rows.start == RIM:
                target = above[part, t]
            elif rows.start == 2 * RIM + stripe:
                target = below[part, t]
            else:
                target = m[t, own_rows(rows), :]
            g[t, rows, :] = mask(u - target)

    propagate(tile, (row_r, row_i, col_r, col_i), trig, (hr, hi), (w0r, w0i), (w1r, w1i), residual)


def back_kernel(sizes, c1, s1, w0r, w0i, w1r, w1i, gr, gi, own_ref, ar, ai, hr, hi):
    tile, _, _ = main_tile(sizes)
    blank_rims((ar, ai, hr, hi), tile)
    backward(tile, (gr, gi), (hr, hi), (w0r, w0i), (w1r, w1i), (c1, s1), put_in(own_ref), (ar, ai))


def other_near(swap_ref, stripe, low_illum, columns):
    packed = swap_ref[2 * stripe :, columns]
    high, low = unpack_rows(packed, False), unpack_rows(packed, True)
    return [jnp.where(low_illum, low[part], high[part]) for part in range(2)]


def patch_kernel(sizes, phase_ref, known_ref, partner_ref, along_ref, phase_rim_ref,
                 w0r, w0i, w1r, w1i, ur_ref, ui_ref, c1, s1, c0, s0, hr, hi, row_r, row_i, col_r, col_i):
    stripe, tiles, total_rows, total_cols = sizes
    main, row_first, _ = main_tile(sizes)
    held, columns = patch_held(sizes)
    tile = Tile(stripe, 1, main.top, main.bottom, held, 0, (0,))
    low_illum = place()[0] == 0
    blank_rims((w0r, w0i, w1r, w1i, hr, hi), tile)
    trig = (c0, s0), (c1, s1)
    end = stripe + RIM

    def joined(get, rim):
        x = join_edges(get(0), get(tiles - 1), rim)
        return join_illums(x, x)

    fill_trig(
        tile, trig, low_illum,
        lambda k, t, r: joined(lambda e: phase_ref[k, r : r + 16, own_columns(e)], phase_rim_ref[k, RIM + r : RIM + r + 16, :]),
        lambda k, t: joined(
            lambda e: partner_ref[:, own_columns(e + k * tiles)],
            jnp.where(low_illum, phase_rim_ref[k, end:, :], phase_rim_ref[k, :RIM, :]),
        ),
        lambda k, t: joined(
            lambda e: along_ref[:, own_columns(e + k * tiles)],
            jnp.where(low_illum, phase_rim_ref[k, :RIM, :], phase_rim_ref[k, end:, :]),
        ),
    )
    note = jnp.where(patch_lanes()[0], 0.0, 1.0)
    tilts = [a * note + b * (1.0 - note) for a, b in zip(tilts_of(known_ref[...]), tilts_of(partner_ref[:, 2 * tiles * LANES :]))]
    forward(
        tile, tilts, columns, row_first, (total_rows, total_cols), trig, (hr, hi), (row_r, row_i, col_r, col_i),
        (w0r, w0i), (w1r, w1i), keep_in((ur_ref, ui_ref)),
    )


def sum_kernel(a_ref, b_ref, out_ref):
    out_ref[...] = a_ref[...] + b_ref[...]


def left_kernel(sizes, swap_ref, along_ref, w0r, w0i, w1r, w1i, ur, ui, c1, s1, left_ref, gr, gi, hr, hi, mr, mi):
    stripe, tiles, _, _ = sizes
    main, _, _ = main_tile(sizes)
    tile = Tile(stripe, swap_ref.shape[1] // LANES, main.top, main.bottom)
    low_illum = place()[0] == 0
    blank_rims((gr, gi, hr, hi), tile)
    fill_target(
        tile, (mr, mi), low_illum, None,
        lambda t: other_near(swap_ref, stripe, low_illum, own_columns(t)),
        lambda t: along_ref[:, own_columns(t + 2 * tiles)],
        range(tile.tiles),
    )
    residual_of(tile, (gr, gi), (ur, ui), other_target(tile, lambda rows, t: swap_ref[rows, own_columns(t)], (mr, mi)))
    backward(tile, (gr, gi), (hr, hi), (w0r, w0i), (w1r, w1i), (c1, s1), put_in(left_ref))


def other_target(tile, swapped, edges, patch=None):
    def target(part, t, rows):
        if t != patch and 2 * RIM <= rows.start < 2 * RIM + tile.stripe:
            at = own_rows(rows)
            return swapped(slice(part * tile.stripe + at.start, part * tile.stripe + at.stop), t)
        return edges[part][t, rows, :]

    return target


class Joined:
    def __init__(self, main, patch, first):
        self.main, self.patch, self.first = main, patch, first

    def __getitem__(self, at):
        t = at[0] + self.first
        return self.main[(t,) + at[1:]] if t < self.main.shape[0] else self.patch[(0,) + at[1:]]


def finish_kernel(sizes, own_ref, left_ref, measured_ref, swap_ref, swap_rest_ref, along_ref, same_ref, rim_ref, relay_ref,
                  partner_relay_ref, *rest):
    main_fields, patch_fields, rest = rest[:8], rest[8:16], rest[16:]
    out_ref, patch, gr, gi, hr, hi, mr, mi, full, sems = rest
    stripe, tiles, total_rows, total_cols = sizes
    left_tiles = swap_ref.shape[1] // LANES
    begin = left_tiles - 1
    lone = tiles - begin
    w0r, w0i, w1r, w1i, ur, ui, c1, s1 = [Joined(a, b, begin) for a, b in zip(main_fields, patch_fields)]
    main, _, _ = main_tile(sizes)
    tile = Tile(stripe, lone + 1, main.top, main.bottom, patch_held(sizes)[0], lone, (lone,))
    illum, _, _ = place()
    low_illum = illum == 0
    blank_rims((gr, gi, hr, hi), tile)

    lane = lane_ids((8, LANES))
    last_rows = relay_ref.shape[0] - 8
    sums = jnp.maximum(relay_ref[last_rows:, :], partner_relay_ref[last_rows:, :])
    scales = []
    for which in range(2):
        here = jnp.where(lane == which, sums, 0.0)
        energy = jnp.sum(here[:1], axis=1, keepdims=True) / (total_rows * total_cols) + EPS_ENERGY
        scales.append(2.0 / energy)
    mine = jnp.where(low_illum, scales[0], scales[1])
    others = jnp.where(low_illum, scales[1], scales[0])

    first, last = own_columns(0), own_columns(tiles - 1)
    own_first = illum * stripe
    near_base = pl.multiple_of(stripe - 16 * illum, 16)
    near_rim = pl.multiple_of(stripe - 8 * illum, 8)

    def swapped(rows, t):
        t = t + begin
        return swap_ref[rows, own_columns(t)] if t < left_tiles else swap_rest_ref[rows, own_columns(t - left_tiles)]

    def other_rim(part, block):
        x = partner_relay_ref[2 * (block // 4 * 4) : 2 * (block // 4 * 4) + 8, :]
        shift = (LANES - 2 * RIM * (block % 4) + part * (LANES // 2)) % LANES
        return pltpu.roll(x, shift, 1) if shift else x

    def middle(part, t, r):
        at = slice(part * stripe + r, part * stripe + r + 16)
        rim = jnp.concatenate([other_rim(part, r // 8), other_rim(part, r // 8 + 1)], axis=0)
        other = join_edges(swap_ref[at, first], swapped(at, lone - 1), rim)
        at = pl.ds(pl.multiple_of(own_first + r, 16), 16)
        own = join_edges(*[measured_ref[part, 0, at, e].astype(F32) for e in (first, last)], rim_ref[part, at, :])
        return join_illums(own, other)

    def near_of(t):
        t = t + begin
        ref, t = (swap_ref, t) if t < left_tiles else (swap_rest_ref, t - left_tiles)
        return other_near(ref, stripe, low_illum, own_columns(t))

    def near(t):
        if t < lone:
            return near_of(t)
        rims = [other_rim(part, stripe // 8) for part in range(2)]
        other = [join_edges(*x) for x in zip(near_of(-begin), near_of(lone - 1), rims)]

        def rows(part, at):
            x = measured_ref[part, 0, pl.ds(near_base, 16), at].astype(F32)
            return jnp.where(low_illum, x[:8], x[8:])

        own = [join_edges(rows(part, first), rows(part, last), rim_ref[part, pl.ds(near_rim, 8), :]) for part in range(2)]
        return [join_illums(*x) for x in zip(own, other)]

    def far(t):
        if t < lone:
            return along_ref[:, own_columns(t + begin + 2 * tiles)]
        other = join_edges(*[along_ref[:, own_columns(e + 2 * tiles)] for e in (0, tiles - 1)], rim_ref[1, 2 * stripe :, :])
        own = join_edges(same_ref[:, first], same_ref[:, last], rim_ref[0, 2 * stripe :, :])
        return join_illums(own, other)

    copies = []

    def send(k, columns):
        copies.append(pltpu.make_async_copy(full.at[k, :, columns], out_ref.at[k, :, columns], sems.at[len(copies)]))
        copies[-1].start()

    for k in range(2):
        for t in range(left_tiles):
            at = own_columns(t)
            full[k, :, at] = own_ref[k, :, at] * mine + left_ref[k, :, at] * others
        if begin > 1:
            send(k, slice(LANES, begin * LANES))

    fill_target(tile, (mr, mi), low_illum, middle, near, far, range(lone))
    residual_of(tile, (gr, gi), (ur, ui), other_target(tile, swapped, (mr, mi), lone))

    def put(k, t, rows, value):
        rows = own_rows(rows)
        if t == lone:
            patch[k, rows, :] = value * mine + pltpu.roll(value, LANES - OTHER, 1) * others
            return
        at = own_columns(t + begin)
        value = own_ref[k, rows, at] * mine + value * others
        if t == 0:
            value = jnp.where(lane_ids(value.shape) < LANES // 2, full[k, rows, at], value)
        full[k, rows, at] = value

    def close(k):
        on = lane_ids(patch.shape[1:])
        full[k, :, first] = jnp.where(on < RIM, patch[k], full[k, :, first])
        full[k, :, last] = jnp.where(on >= LANES - RIM, pltpu.roll(patch[k], 56, 1), full[k, :, last])
        if begin > 0:
            send(k, first)
        send(k, slice(begin * LANES, tiles * LANES))

    backward(tile, (gr, gi), (hr, hi), (w0r, w0i), (w1r, w1i), (c1, s1), put, on_middle=functools.partial(close, 1))
    close(0)
    for copy in copies:
        copy.wait()


def like(x, held):
    shape, dtype = (x, F32) if isinstance(x, tuple) else (x.shape, x.dtype)
    return pltpu.VMEM(shape, dtype) if held else jax.ShapeDtypeStruct(shape, dtype)


def after(kernel, *refs):
    count = len(refs)

    def ordered(*args):
        return kernel(*args[count:])

    return ordered


def call(kernel, outs, *args, behind=(), scratch=(), in_place=0, flops=0, mib=8, held=(), far=0):
    kernel, args = after(kernel, *behind), (*behind, *args)
    in_place_specs = [pl.BlockSpec(memory_space=pltpu.HBM)] * in_place
    return pl.pallas_call(
        kernel,
        out_shape=[like(x, n in held) for n, x in enumerate(outs)],
        in_specs=in_place_specs
        + [pl.BlockSpec(memory_space=pltpu.VMEM)] * (len(args) - in_place),
        out_specs=[pl.BlockSpec(memory_space=pltpu.VMEM)] * (len(outs) - far) + [pl.BlockSpec(memory_space=pltpu.HBM)] * far,
        scratch_shapes=[pltpu.VMEM(s, F32) if isinstance(s, tuple) else s for s in scratch],
        compiler_params=pltpu.CompilerParams(vmem_limit_bytes=int(mib * 2**20)),
        cost_estimate=pl.CostEstimate(flops=flops, bytes_accessed=2**18, transcendentals=0),
    )(*args)


def paired(phase_delay, angles, measured):
    slices, stripe, width = phase_delay.shape
    rows, cols = lax.axis_size("row"), lax.axis_size("col")
    tiles = width // LANES
    sizes = (stripe, tiles, 2 * stripe * rows, width * cols)
    swap = [(0, 1), (1, 0)]
    along = []
    for c in range(cols):
        for r in range(rows - 1):
            below, above = ((rows + r) * cols + c, (r + 1) * cols + c)
            along += [(below, above), (above, below)]
        along += [(c, c ^ 1), ((2 * rows - 1) * cols + c, (2 * rows - 1) * cols + (c ^ 1))]
    same = [(r, (r + 1) % rows) for r in range(rows)] + [(rows + (r + 1) % rows, rows + r) for r in range(rows)]

    partner_out, along_out, same_out, known, note, measured = call(
        open_kernel, [(8, 2 * width + LANES), (8, 3 * width), (8, width), (8, LANES), (8, LANES), measured],
        phase_delay, measured, angles, in_place=3, mib=62, held=(5,),
        scratch=[
            (2, slices, 8, width), pltpu.VMEM(angles.shape, angles.dtype), pltpu.SemaphoreType.DMA((4,)),
        ],
    )
    along_in = lax.ppermute(along_out, ("illum", "row", "col"), along)
    partner_in = lax.ppermute(partner_out, "illum", swap)
    same_in = lax.ppermute(same_out, ("illum", "row"), same)
    core_note = lax.ppermute(note, "row", [(r, r ^ 1) for r in range(rows)])
    (pair,) = call(sum_kernel, [(8, LANES)], note, core_note)
    far = lax.ppermute(pair, "row", [(r, r ^ 2) for r in range(rows)])
    cut = max(tiles - 2, 1) * LANES
    rows_swapped = 2 * stripe + 8
    (swap_out,) = call(
        functools.partial(swap_kernel, slice(0, cut)), [(rows_swapped, cut)], measured, behind=[core_note]
    )
    swap_in = lax.ppermute(swap_out, "illum", swap)

    def fields(count):
        return [(count, stripe + 4 * RIM, LANES)]

    def tables(count):
        return [(stripe + 2 * RIM, LANES)] * 2 + [(-(-count // 8) * 8, LANES)] * 2

    own_trig = call(
        functools.partial(trig_kernel, sizes), [(tiles, stripe, LANES)] * 6 + tables(tiles), phase_delay, measured, known,
        flops=3*10**9)
    rims = 8 * (-(-(stripe // 4 + 1) // 4))
    first_out, second_packed, note = call(
        rim_pack_kernel, [(rims + 8, LANES), (rims, LANES), (8, LANES)], phase_delay, measured, pair, far, partner_in, along_in, same_in,
        behind=own_trig[:1],
    )
    first_in = lax.ppermute(first_out, "col", [(c, cols - 1 - c) for c in range(cols)])
    kept = call(
        functools.partial(ahead_kernel, sizes), fields(tiles) * 10, *own_trig[:4], partner_in, along_in,
        scratch=fields(tiles) * 2 + tables(tiles), flops=15*10**8, mib=16,
    )
    (second_out,) = call(second_kernel, [(rims + 8, LANES)], second_packed, note, first_in, behind=kept[:1])
    second_in = lax.ppermute(second_out, "col", [(c, c ^ 1) for c in range(cols)])

    own_kept = call(
        functools.partial(own_kernel, sizes), fields(tiles) * 6, *kept[:4], *own_trig[4:], measured, same_in,
        scratch=fields(tiles) * 2 + [(2, tiles, RIM, LANES)] * 2, flops=15*10**8, mib=16,
    )
    phase_rim, rim, relay = call(
        rim_unpack_kernel, [(2, stripe + 2 * RIM, LANES), (2, 2 * stripe + 8, LANES), (8 * (-(-(stripe // 8 + 1) // 4)) + 8, LANES)],
        first_in, second_in, note,
        behind=own_kept[:1],
    )
    partner_relay = lax.ppermute(relay, "illum", swap)
    (swap_out,) = call(
        functools.partial(swap_kernel, slice(cut, width)), [(rows_swapped, width - cut)], measured, behind=own_kept[:1]
    )
    swap_rest = lax.ppermute(swap_out, "illum", swap)
    (own,) = call(
        functools.partial(back_kernel, sizes), [phase_delay.shape], *kept[2:4], *own_kept,
        scratch=fields(tiles) * 4, flops=10**9, mib=12, behind=[relay],
    )
    patch_kept = call(
        functools.partial(patch_kernel, sizes), fields(1) * 8, phase_delay, known, partner_in, along_in, phase_rim,
        scratch=fields(1) * 4 + tables(1), flops=10**9, behind=[own],
    )
    (left,) = call(
        functools.partial(left_kernel, sizes), [(slices, stripe, cut)], swap_in, along_in, *kept[4:], *kept[2:4],
        behind=patch_kept[:1], scratch=fields(cut // LANES) * 6, flops=10**9, mib=12,
    )
    (out,) = call(
        functools.partial(finish_kernel, sizes), [phase_delay.shape],
        own, left, measured, swap_in, swap_rest, along_in, same_in, rim, relay, partner_relay,
        *kept[4:], *kept[2:4], *patch_kept,
        scratch=[(slices, stripe, LANES)] + fields(tiles - cut // LANES + 2) * 6
        + [phase_delay.shape, pltpu.SemaphoreType.DMA((6,))],
        mib=12, flops=0, far=1,
    )
    return out


def halo(x, axis, dim, width, index_of=None):
    peers = lax.axis_size(axis)
    up = [(i, i + 1) for i in range(peers - 1)]
    before = lax.ppermute(lax.slice_in_dim(x, x.shape[dim] - width, x.shape[dim], axis=dim), axis, up)
    after = lax.ppermute(lax.slice_in_dim(x, 0, width, axis=dim), axis, [(j, i) for i, j in up])
    return before, after


def with_column_rims(x, width):
    before, after = halo(x, "col", x.ndim - 1, width)
    gap = jnp.zeros(x.shape[:-1] + (LANES - 2 * width,), x.dtype)
    return jnp.concatenate([x, after, gap, before], axis=-1)


def stripe_halo(x, width):
    illums, rows = lax.axis_size("illum"), lax.axis_size("row")
    where = [(s % illums) * rows + s // illums for s in range(illums * rows)]
    up = [(where[s], where[s + 1]) for s in range(illums * rows - 1)]
    before = lax.ppermute(x[:, -width:], ("illum", "row"), up)
    after = lax.ppermute(x[:, :width], ("illum", "row"), [(b, a) for a, b in up])
    return jnp.concatenate([before, x, after], axis=1)


def per_device(phase_delay, angles, measured):
    illums = lax.axis_size("illum")
    if (illums, lax.axis_size("row"), lax.axis_size("col")) == (2, 4, 4):
        return paired(phase_delay, angles, measured)
    slices, stripe, width = phase_delay.shape
    tile_rows = measured.shape[2]
    total_rows, total_cols = tile_rows * lax.axis_size("row"), width * lax.axis_size("col")
    tiles = width // LANES + 1
    row_first = lax.axis_index("row") * tile_rows + lax.axis_index("illum") * stripe
    col_first = lax.axis_index("col") * width

    target = measured[:, 0].astype(F32)
    energy = lax.psum(jnp.sum(target * target).reshape(1), ("row", "col"))
    energies = lax.all_gather(energy, "illum", tiled=True) / (total_rows * total_cols) + EPS_ENERGY
    tilts = lax.all_gather(angles, "illum", tiled=True)

    phase = with_column_rims(stripe_halo(phase_delay, RIM), RIM)
    above, below = halo(target, "row", 1, REACH)
    target = with_column_rims(jnp.concatenate([above, target, below], axis=1), REACH)
    windows = jnp.stack([target[:, i * stripe : (i + 1) * stripe + 2 * REACH] for i in range(illums)])
    windows = lax.all_to_all(windows, "illum", 0, 0, tiled=True)
    windows = jnp.pad(windows, ((0, 0), (0, 0), (RIM - REACH, RIM - REACH), (0, 0)))

    field = pltpu.VMEM((tiles, stripe + 4 * RIM, LANES), F32)
    rows_all = stripe + 2 * RIM
    return pl.pallas_call(
        functools.partial(gradient_kernel, (stripe, tiles, illums, total_rows, total_cols)),
        out_shape=jax.ShapeDtypeStruct(phase_delay.shape, F32),
        in_specs=[pl.BlockSpec(memory_space=pltpu.SMEM)] * 3 + [pl.BlockSpec(memory_space=pltpu.VMEM)] * 2,
        out_specs=pl.BlockSpec(memory_space=pltpu.VMEM),
        scratch_shapes=[field] * 12
        + [pltpu.VMEM((rows_all, LANES), F32)] * 2
        + [pltpu.VMEM((-(-tiles // 8) * 8, LANES), F32)] * 2,
        compiler_params=pltpu.CompilerParams(vmem_limit_bytes=48 * 2**20),
    )(jnp.stack([row_first, col_first]), tilts, 2.0 / energies, phase, windows)


def solution(mesh):
    placed = (P(None, ("row", "illum"), "col"), P("illum", None), P(None, "illum", "row", "col"))
    return jax.shard_map(
        per_device,
        mesh=mesh,
        in_specs=placed,
        out_specs=P(None, ("row", "illum"), "col"),
        check_vma=False,
    )
```

```python
import functools
import math

import jax
import jax.numpy as jnp
from jax import lax
from jax.experimental import pallas as pl
from jax.experimental.pallas import tpu as pltpu
from jax.sharding import PartitionSpec as P

EPS_ENERGY = 1e-06
RIM = 8
REACH = 4
LANES = 128
F32 = jnp.float32


def sine_cosine(x):
    y = x * x
    s = -2.5052108385441718e-08
    for c in (2.7557319223985893e-06, -1.9841269841269841e-04, 8.333333333333333e-03, -1.6666666666666666e-01):
        s = s * y + c
    c_ = -2.7557319223985888e-07
    for c in (2.48015873015873e-05, -1.3888888888888889e-03, 4.1666666666666664e-02, -0.5, 1.0):
        c_ = c_ * y + c
    return x + x * y * s, c_


def sine_cosine_of_turns(turns):
    quarters = 4.0 * (turns - jnp.floor(turns))
    nearest = jnp.floor(quarters + 0.5)
    s, c = sine_cosine((quarters - nearest) * (0.5 * math.pi))
    odd = (nearest == 1.0) | (nearest == 3.0)
    s, c = jnp.where(odd, c, s), jnp.where(odd, s, c)
    s = jnp.where((nearest == 2.0) | (nearest == 3.0), -s, s)
    c = jnp.where((nearest == 1.0) | (nearest == 2.0), -c, c)
    return s, c


def lane_ids(shape):
    return lax.broadcasted_iota(jnp.int32, shape, len(shape) - 1)


class Tile:
    def __init__(self, stripe, tiles, top, bottom, lanes=None, rim=None, alone=()):
        self.stripe, self.tiles = stripe, tiles
        self.rows = stripe + 2 * RIM
        self.top, self.bottom, self.lanes, self.rim = top, bottom, lanes, rim
        self.alone = alone
        self.order = [*alone, *range(1, tiles - len(alone)), *([0] if tiles > len(alone) else [])]
        self.owned = tiles if rim in alone or rim is None else tiles - 1
        step = 32 if stripe % 32 == 0 else 8
        self.inner = [(2 * RIM + r, step, None) for r in range(0, stripe, step)]
        self.blocks = [(RIM, RIM, top)] + self.inner + [(2 * RIM + stripe, RIM, bottom)]

    def sweep(self, body, blocks, fields=()):
        for first, count, factor in blocks:
            rows = pl.ds(first, count)
            held = {}

            def load(ref, t, rows=rows, held=held):
                key = id(ref), t
                if key not in held:
                    held[key] = ref[t, rows, :]
                return held[key]

            for t in self.order:

                def mask(x, factor=factor, lanes=self.lanes if t == self.rim else None):
                    x = x if factor is None else x * factor
                    return x if lanes is None else x * lanes

                body(t, rows, mask, [self.beside(ref, t, rows, load) for ref in fields])

    def beside(self, ref, t, rows, load):
        above = pl.ds(rows.start - 1, rows.size)
        below = pl.ds(rows.start + 1, rows.size)
        here = load(ref, t)
        west = east = here
        if t not in self.alone:
            ring = self.tiles - len(self.alone)
            lane = lane_ids(here.shape)
            west = jnp.where(lane == LANES - 1, load(ref, (t - 1) % ring), here)
            east = jnp.where(lane == 0, load(ref, (t + 1) % ring), here)
        west, east = pltpu.roll(west, 1, 1), pltpu.roll(east, LANES - 1, 1)
        return here, (ref[t, above, :] + ref[t, below, :]) + (west + east)


def first_half(tile, field, half, sign, blocks):
    def body(t, rows, mask, sums):
        (real, beside_real), (imag, beside_imag) = sums
        half[0][t, rows, :] = mask(beside_real + (2.0 * sign) * imag)
        half[1][t, rows, :] = mask(beside_imag - (2.0 * sign) * real)

    tile.sweep(body, blocks, field)


def second_half(tile, field, half, blocks, use):
    def body(t, rows, mask, sums):
        (_, beside_real), (_, beside_imag) = sums
        use(t, rows, mask, 0.1 * beside_real - field[0][t, rows, :], 0.1 * beside_imag - field[1][t, rows, :])

    tile.sweep(body, blocks, half)


def blank_rims(refs, tile):
    for ref in refs:
        for first in (0, tile.rows + RIM):
            ref[:, first : first + RIM, :] = jnp.zeros((tile.tiles, RIM, LANES), F32)


def rim_columns(tile, col_first, shape):
    at, on = lax.broadcasted_iota(jnp.int32, shape, 0), lane_ids(shape)
    return col_first + jnp.where((at >= tile.owned) & (on >= LANES // 2), on - LANES, at * LANES + on)


def incident_tables(tile, tilts, row_first, columns, total_rows, total_cols, tables):
    row_r, row_i, col_r, col_i = tables
    ids = lax.broadcasted_iota(jnp.int32, (tile.rows, LANES), 0) + (row_first - RIM)
    s, c = sine_cosine_of_turns(ids.astype(F32) * tilts[0] / total_rows)
    row_r[...] = (-7.0 * c - 24.0 * s) * 0.04
    row_i[...] = (-7.0 * s + 24.0 * c) * 0.04
    col_i[...], col_r[...] = sine_cosine_of_turns(columns.astype(F32) * tilts[1] / total_cols)


def enter(tile, tables, trig, field):
    row_r, row_i, col_r, col_i = tables
    fr, fi = field

    def start(t, rows, mask, _):
        at = pl.ds(rows.start - RIM, rows.size)
        ar, ai = row_r[at, :], row_i[at, :]
        br, bi = col_r[t : t + 1, :], col_i[t : t + 1, :]
        ur, ui = ar * br - ai * bi, ar * bi + ai * br
        c, s = trig[0][t, rows, :], trig[1][t, rows, :]
        fr[t, rows, :] = mask(ur * c - ui * s)
        fi[t, rows, :] = mask(ur * s + ui * c)

    tile.sweep(start, tile.blocks)


def modulate_into(trig, field):
    def use(t, rows, mask, ur, ui):
        c, s = trig[0][t, rows, :], trig[1][t, rows, :]
        field[0][t, rows, :] = mask(ur * c - ui * s)
        field[1][t, rows, :] = mask(ur * s + ui * c)

    return use


def backward(*args, **kwargs):
    for _ in backward_steps(*args, **kwargs):
        pass


def backward_steps(tile, adjoint, half, w0, w1, trig1, put, between=None, on_middle=None, on_rows=None):
    between = between or adjoint
    gr, gi = between
    inner = [first for first, _, _ in tile.inner]

    def back(t, rows, mask, ur, ui):
        if t < tile.owned and rows.start in inner:
            put(1, t, rows, ui * w1[0][t, rows, :] - ur * w1[1][t, rows, :])
        c, s = trig1[0][t, rows, :], trig1[1][t, rows, :]
        gr[t, rows, :] = mask(ur * c + ui * s)
        gi[t, rows, :] = mask(ui * c - ur * s)

    def last(t, rows, mask, ur, ui):
        if t < tile.owned:
            put(0, t, rows, ui * w0[0][t, rows, :] - ur * w0[1][t, rows, :])

    first_half(tile, adjoint, half, -1.0, tile.blocks)
    yield
    second_half(tile, adjoint, half, tile.blocks, back)
    yield
    if on_middle:
        on_middle()
    first_half(tile, between, half, -1.0, tile.blocks)
    yield
    for block in tile.inner if on_rows is None else [(r, 16, None) for r in range(2 * RIM, 2 * RIM + tile.stripe, 16)]:
        second_half(tile, between, half, [block], last)
        if on_rows:
            on_rows(block[0] - 2 * RIM)


def own_columns(t):
    return slice(t * LANES, (t + 1) * LANES)


def own_rows(rows):
    return slice(rows.start - 2 * RIM, rows.start - 2 * RIM + rows.size)


def gradient_kernel(sizes, place_ref, angles_ref, scale_ref, phase_ref, target_ref, out_ref,
                    c0, s0, c1, s1, w0r, w0i, w1r, w1i, gr, gi, hr, hi, row_r, row_i, col_r, col_i):
    stripe, tiles, illums, total_rows, total_cols = sizes
    row_first, col_first = place_ref[0], place_ref[1]
    edges = edges_of(row_first, col_first, stripe, tiles, total_rows, total_cols)
    tile = Tile(stripe, tiles, *edges, rim=tiles - 1)
    blank_rims((w0r, w0i, w1r, w1i, gr, gi, hr, hi), tile)
    out_ref[...] = jnp.zeros(out_ref.shape, F32)
    span = slice(RIM, RIM + tile.rows)
    for t in range(tiles):
        for k, (c, s) in enumerate(((c0, s0), (c1, s1))):
            s[t, span, :], c[t, span, :] = sine_cosine(phase_ref[k, :, own_columns(t)])
    tables, half = (row_r, row_i, col_r, col_i), (hr, hi)

    def illum(j, carry):
        tilts = angles_ref[j, 0].astype(F32), angles_ref[j, 1].astype(F32)
        incident_tables(tile, tilts, row_first, rim_columns(tile, col_first, col_r.shape), total_rows, total_cols, tables)
        enter(tile, tables, (c0, s0), (w0r, w0i))
        first_half(tile, (w0r, w0i), half, 1.0, tile.blocks)
        second_half(tile, (w0r, w0i), half, tile.blocks, modulate_into((c1, s1), (w1r, w1i)))
        first_half(tile, (w1r, w1i), half, 1.0, tile.blocks)

        def residual(t, rows, mask, ur, ui):
            at = slice(rows.start - RIM, rows.start - RIM + rows.size)
            gr[t, rows, :] = mask(ur - target_ref[j, 0, at, own_columns(t)])
            gi[t, rows, :] = mask(ui - target_ref[j, 1, at, own_columns(t)])

        second_half(tile, (w1r, w1i), half, tile.blocks, residual)

        def put(k, t, rows, value):
            at = (k, own_rows(rows), own_columns(t))
            out_ref[at] = out_ref[at] + scale_ref[j] * value

        backward(tile, (gr, gi), half, (w0r, w0i), (w1r, w1i), (c1, s1), put)
        return carry

    lax.fori_loop(0, illums, illum, 0)


def edges_of(row_first, col_first, stripe, tiles, total_rows, total_cols):
    width = (tiles - 1) * LANES
    top = jnp.where(row_first == 0, 0.0, 1.0).astype(F32)
    bottom = jnp.where(row_first + stripe == total_rows, 0.0, 1.0).astype(F32)
    lane = lane_ids((1, LANES))
    in_west = (lane >= LANES - RIM) & (col_first > 0)
    in_east = (lane < RIM) & (col_first + width < total_cols)
    return top, bottom, jnp.where(in_west | in_east, 1.0, 0.0).astype(F32)


def place():
    return lax.axis_index("illum"), lax.axis_index("row"), lax.axis_index("col")


def pack_rows(real, imag, low):
    first = lax.broadcasted_iota(jnp.int32, real.shape, 0) < 4
    if low:
        return jnp.where(first, real, pltpu.roll(imag, 4, 0))
    return jnp.where(first, pltpu.roll(real, 4, 0), imag)


def unpack_rows(packed, low):
    turned = pltpu.roll(packed, 4, 0)
    return (packed, turned) if low else (turned, packed)


def edge_blocks(measured_ref, first):
    base = first // 16 * 16
    at = first - base
    return [measured_ref[p, 0, base : base + 16, :].astype(F32)[at : at + 8] for p in range(2)]


def open_kernel(phase_ref, measured_ref, tilt_ref, partner_ref, along_ref, same_ref, known_ref, note_ref, held, edge, tilt, sems):
    stripe, width = phase_ref.shape[1:]
    rows = 2 * stripe
    illum, _, _ = place()
    field_copy = pltpu.make_async_copy(measured_ref, held, sems.at[0])
    tilt_copy = pltpu.make_async_copy(tilt_ref, tilt, sems.at[3])
    edge_copies = [
        pltpu.make_async_copy(phase_ref.at[:, pl.ds(first, 8), :], edge.at[e], sems.at[1 + e])
        for e, first in enumerate((0, stripe - 8))
    ]
    for copy in edge_copies:
        copy.start()
    field_copy.start()
    tilt_copy.start()
    for copy in edge_copies:
        copy.wait()
    for k in range(2):
        top, bottom = edge[0, k], edge[1, k]
        along_ref[:, k * width : (k + 1) * width] = jnp.where(illum == 0, top, bottom)
        partner_ref[:, k * width : (k + 1) * width] = jnp.where(illum == 0, bottom, top)
    field_copy.wait()
    top, bottom = pack_rows(*edge_blocks(held, 0), True), pack_rows(*edge_blocks(held, rows - 8), False)
    along_ref[:, 2 * width :] = jnp.where(illum == 0, top, bottom)
    same_ref[...] = jnp.where(illum == 0, bottom, top)
    total = jnp.zeros((8, width), F32)
    for p in range(2):
        for r in range(0, rows, 16):
            x = held[p, 0, r : r + 16, :].astype(F32)
            x = x * x
            total = total + (x[:8] + x[8:])
    energy = jnp.sum(jnp.sum(total, axis=1, keepdims=True), axis=0, keepdims=True)
    lane = lane_ids((8, LANES))
    note_ref[...] = jnp.where(lane == illum, energy, 0.0)
    note = jnp.zeros((8, LANES), F32)
    tilt_copy.wait()
    for n in range(2):
        note = jnp.where(lane == 16 + n, tilt[:, n : n + 1].astype(F32), note)
    partner_ref[:, 2 * width :] = note
    known_ref[...] = note


def swap_kernel(columns, measured_ref, swap_ref):
    stripe = measured_ref.shape[2] // 2
    illum, _, _ = place()
    other = pl.multiple_of((1 - illum) * stripe, 16)
    for p in range(2):
        for r in range(0, stripe, 16):
            at = pl.ds(pl.multiple_of(other + r, 16), 16)
            swap_ref[p * stripe + r : p * stripe + r + 16, :] = measured_ref[p, 0, at, columns].astype(F32)
    above = pack_rows(*[x[:, columns] for x in edge_blocks(measured_ref, stripe - 8)], False)
    below = pack_rows(*[x[:, columns] for x in edge_blocks(measured_ref, stripe)], True)
    swap_ref[2 * stripe :, :] = jnp.where(illum == 0, above, below)


def rim_pack_kernel(phase_ref, measured_ref, pair_ref, far_ref, partner_ref, along_ref, same_ref, first_ref, second_ref, note_ref):
    stripe, width = phase_ref.shape[1:]
    rows = 2 * stripe
    illum, _, col = place()
    low_illum = illum == 0
    even = lax.rem(col, 2) == 0
    lane = lane_ids((8, LANES))
    note = pair_ref[...] + far_ref[...]
    note_ref[...] = note
    first_ref[first_ref.shape[0] - 8 :, :] = note

    def packed(east):
        edge = slice(width - LANES, width) if east else slice(0, LANES)
        base = LANES - RIM if east else 0
        groups = []
        for j in range(stripe // 8 + 2):
            items = []
            for k in range(2):
                tile = slice(k * width + edge.start, k * width + edge.stop)
                if j == 0:
                    items.append(jnp.where(low_illum, along_ref[:, tile], partner_ref[:, tile]))
                elif j == stripe // 8 + 1:
                    items.append(jnp.where(low_illum, partner_ref[:, tile], along_ref[:, tile]))
                else:
                    items.append(phase_ref[k, 8 * (j - 1) : 8 * j, edge])
            groups.append(items)
        while len(groups) < rows // 8 + 1:
            groups.append([None, None])
        for r in range(0, rows, 16):
            both = [measured_ref[p, 0, r : r + 16, edge].astype(F32) for p in range(2)]
            for h in range(2):
                groups[r // 8 + h] += [b[8 * h : 8 * h + 8] for b in both]
        groups[rows // 8] += [same_ref[:, edge], along_ref[:, 2 * width + edge.start : 2 * width + edge.stop]]
        for g in range(0, len(groups), 4):
            acc = jnp.zeros((8, LANES), F32)
            for q, items in enumerate(groups[g : g + 4]):
                for k, item in enumerate(items):
                    if item is not None:
                        slot = 4 * q + k
                        shift = (8 * slot - base) % LANES
                        moved = pltpu.roll(item, shift, 1) if shift else item
                        acc = jnp.where((lane >= 8 * slot) & (lane < 8 * slot + 8), moved, acc)
            yield 2 * g, acc

    for (at, east), (_, west) in zip(packed(True), packed(False)):
        first_ref[at : at + 8, :] = jnp.where(even, west, east)
        second_ref[at : at + 8, :] = jnp.where(even, east, west)


def second_kernel(packed_ref, note_ref, first_ref, out_ref):
    rims = packed_ref.shape[0]
    out_ref[:rims, :] = packed_ref[...]
    out_ref[rims:, :] = note_ref[...] + first_ref[rims:, :]


def rim_unpack_kernel(first_ref, second_ref, note_ref, phase_rim_ref, rim_ref, relay_ref):
    stripe = phase_rim_ref.shape[1] - 2 * RIM
    rims, rows = first_ref.shape[0] - 8, 2 * stripe
    illum, _, col = place()
    even = lax.rem(col, 2) == 0
    lane = lane_ids((8, LANES))
    in_west = (lane >= LANES - RIM) & (col > 0)
    in_east = (lane < RIM) & (col < lax.axis_size("col") - 1)
    for g in range(0, rows // 8 + 1, 4):
        first, second = first_ref[2 * g : 2 * g + 8, :], second_ref[2 * g : 2 * g + 8, :]
        a, b = jnp.where(even, first, second), jnp.where(even, second, first)
        for j in range(g, min(g + 4, rows // 8 + 1)):
            for k in range(4):
                if k < 2 and j >= stripe // 8 + 2:
                    continue
                slot = 4 * (j - g) + k
                from_west = pltpu.roll(a, (LANES - RIM - 8 * slot) % LANES, 1)
                from_east = pltpu.roll(b, (-8 * slot) % LANES, 1) if slot else b
                item = jnp.where(in_west, from_west, jnp.where(in_east, from_east, 0.0))
                (phase_rim_ref if k < 2 else rim_ref)[k % 2, 8 * j : 8 * j + 8, :] = item
    other = pl.multiple_of((1 - illum) * stripe, 8)
    near = pl.multiple_of(stripe - 8 + 8 * illum, 8)
    blocks = [pl.multiple_of(other + r, 8) for r in range(0, stripe, 8)] + [near]
    for g in range(0, len(blocks), 4):
        packed = jnp.zeros((8, LANES), F32)
        for q, first in enumerate(blocks[g : g + 4]):
            at = pl.ds(first, 8)
            x = rim_ref[0, at, :] + pltpu.roll(rim_ref[1, at, :], LANES // 2, 1)
            packed = packed + (pltpu.roll(x, 2 * RIM * q, 1) if q else x)
        relay_ref[2 * g : 2 * g + 8, :] = packed
    relay_ref[relay_ref.shape[0] - 8 :, :] = note_ref[...] + first_ref[rims:, :] + second_ref[rims:, :]


def fill_target(tile, target, low_illum, middle, near, far, plain=()):
    end = 2 * RIM + tile.stripe
    for t in range(tile.tiles):
        beside_rows, packed = near(t), far(t)
        for part, ref in enumerate(target):
            for r in range(0, tile.stripe, 16) if t not in plain else ():
                ref[t, 2 * RIM + r : 2 * RIM + r + 16, :] = middle(part, t, r)
            ref[t, RIM : 2 * RIM, :] = jnp.where(low_illum, unpack_rows(packed, False)[part], beside_rows[part])
            ref[t, end : end + RIM, :] = jnp.where(low_illum, beside_rows[part], unpack_rows(packed, True)[part])


def fill_trig(tile, trig, low_illum, middle, near, far):
    for t in range(tile.tiles):
        for k, (c, s) in enumerate(trig):
            above, below = far(k, t), near(k, t)
            here = [(RIM, jnp.where(low_illum, above, below)), (2 * RIM + tile.stripe, jnp.where(low_illum, below, above))]
            here += [(2 * RIM + r, middle(k, t, r)) for r in range(0, tile.stripe, 16)]
            for first, x in here:
                s[t, first : first + x.shape[0], :], c[t, first : first + x.shape[0], :] = sine_cosine(x)


def tilts_of(note):
    lane = lane_ids(note.shape)
    return [jnp.sum(jnp.where(lane == n, note, 0.0)[:1], axis=1, keepdims=True) for n in (16, 17)]


def forward(tile, tilts, columns, row_first, totals, trig, half, tables, w0, w1, use):
    incident_tables(tile, tilts, row_first, columns, *totals, tables)
    propagate(tile, tables, trig, half, w0, w1, use)


def propagate(*args):
    for _ in propagate_steps(*args):
        pass


def propagate_steps(tile, tables, trig, half, w0, w1, use):
    enter(tile, tables, trig[0], w0)
    first_half(tile, w0, half, 1.0, tile.blocks)
    yield
    second_half(tile, w0, half, tile.blocks, modulate_into(trig[1], w1))
    yield
    first_half(tile, w1, half, 1.0, tile.blocks)
    yield
    second_half(tile, w1, half, tile.blocks, use)


def keep_in(field):
    def use(t, rows, mask, ur, ui):
        field[0][t, rows, :] = ur
        field[1][t, rows, :] = ui

    return use


def residual_in(field, target):
    def use(t, rows, mask, ur, ui):
        field[0][t, rows, :] = mask(ur - target[0][t, rows, :])
        field[1][t, rows, :] = mask(ui - target[1][t, rows, :])

    return use


def residual_of(tile, field, exit_field, target):
    def body(t, rows, mask, _):
        for part, (g, u) in enumerate(zip(field, exit_field)):
            g[t, rows, :] = mask(u[t, rows, :] - target(part, t, rows))

    tile.sweep(body, tile.blocks)


def put_in(ref):
    def put(k, t, rows, value):
        ref[k, own_rows(rows), own_columns(t)] = value

    return put


def main_tile(sizes):
    stripe, tiles, total_rows, total_cols = sizes
    illum, row, col = place()
    row_first = (row * 2 + illum) * stripe
    top, bottom, _ = edges_of(row_first, 0, stripe, tiles + 1, total_rows, total_cols)
    return Tile(stripe, tiles, top, bottom), row_first, col * tiles * LANES


OTHER = 28


def patch_lanes():
    lane = lane_ids((1, LANES))
    other = ((lane >= OTHER - RIM) & (lane < OTHER + 16)) | ((lane >= 56 + OTHER) & (lane < 80 + OTHER))
    return other, jnp.where(other, (lane + (LANES - OTHER)) % LANES, lane)


def patch_held(sizes):
    stripe, tiles, total_rows, total_cols = sizes
    _, _, col_first = main_tile(sizes)
    width = tiles * LANES
    _, at = patch_lanes()
    held = (at < 16) | ((at >= 56) & (at < 72))
    held = held | ((at >= 72) & (at < 80) & (col_first + width < total_cols))
    held = held | ((at >= LANES - RIM) & (col_first > 0))
    columns = jnp.where(at < 16, at, jnp.where(at < 80, at - 72 + width, at - LANES)) + col_first
    return jnp.where(held, 1.0, 0.0).astype(F32), jnp.broadcast_to(columns, (8, LANES))


def join_edges(west, east, rim):
    lane = lane_ids(west.shape)
    moved = pltpu.roll(jnp.where(lane < RIM, rim, east), 72, 1)
    return jnp.where(lane < 16, west, jnp.where(lane >= LANES - RIM, rim, moved))


def join_illums(own, other):
    return jnp.where(patch_lanes()[0], pltpu.roll(other, OTHER, 1), own)


def trig_kernel(sizes, phase_ref, measured_ref, known_ref, c0, s0, c1, s1, mr, mi, row_r, row_i, col_r, col_i):
    stripe, tiles, total_rows, total_cols = sizes
    tile, row_first, col_first = main_tile(sizes)
    illum, _, _ = place()
    columns = rim_columns(tile, col_first, col_r.shape)
    tables = (row_r, row_i, col_r, col_i)
    incident_tables(tile, tilts_of(known_ref[...]), row_first, columns, total_rows, total_cols, tables)
    for part, m in enumerate((mr, mi)):
        for t in range(tiles):
            for r in range(0, stripe, 16):
                at = pl.ds(pl.multiple_of(illum * stripe + r, 16), 16)
                m[t, r : r + 16, :] = measured_ref[part, 0, at, own_columns(t)].astype(F32)
    for t in range(c0.shape[0]):
        for k, (c, s) in enumerate(((c0, s0), (c1, s1))):
            for r in range(0, c.shape[1], 16):
                s[t, r : r + 16, :], c[t, r : r + 16, :] = sine_cosine(phase_ref[k, r : r + 16, own_columns(t)])


def ahead_kernel(sizes, own_c0, own_s0, own_c1, own_s1, partner_ref, along_ref,
                 c0, s0, c1, s1, w0r, w0i, w1r, w1i, ur_ref, ui_ref, hr, hi, row_r, row_i, col_r, col_i):
    stripe, tiles, total_rows, total_cols = sizes
    tile, row_first, col_first = main_tile(sizes)
    illum, _, _ = place()
    low_illum = illum == 0
    blank_rims((w0r, w0i, w1r, w1i, hr, hi), tile)
    trig = (c0, s0), (c1, s1)
    end = 2 * RIM + stripe
    for t in range(tiles):
        for k, (mine, here) in enumerate((((own_c0, own_s0), trig[0]), ((own_c1, own_s1), trig[1]))):
            far, near = along_ref[:, own_columns(t + k * tiles)], partner_ref[:, own_columns(t + k * tiles)]
            above = sine_cosine(jnp.where(low_illum, far, near))
            below = sine_cosine(jnp.where(low_illum, near, far))
            for part in range(2):
                here[part][t, 2 * RIM : end, :] = mine[part][t]
                here[part][t, RIM : 2 * RIM, :] = above[1 - part]
                here[part][t, end : end + RIM, :] = below[1 - part]
    forward(
        tile, tilts_of(partner_ref[:, 2 * tiles * LANES :]), rim_columns(tile, col_first, col_r.shape), row_first,
        (total_rows, total_cols), trig, (hr, hi), (row_r, row_i, col_r, col_i),
        (w0r, w0i), (w1r, w1i), keep_in((ur_ref, ui_ref)),
    )


def own_kernel(sizes, c0, s0, c1, s1, mr, mi, row_r, row_i, col_r, col_i, measured_ref, same_ref,
               w0r, w0i, w1r, w1i, gr, gi, hr, hi, above, below):
    stripe, tiles, total_rows, total_cols = sizes
    tile, row_first, col_first = main_tile(sizes)
    illum, _, _ = place()
    low_illum = illum == 0
    blank_rims((w0r, w0i, w1r, w1i, gr, gi, hr, hi), tile)
    trig = (c0, s0), (c1, s1)
    near_base = pl.multiple_of(stripe - 16 * illum, 16)
    for t in range(tiles):
        both = [measured_ref[part, 0, pl.ds(near_base, 16), own_columns(t)].astype(F32) for part in range(2)]
        near = [jnp.where(low_illum, x[:8], x[8:]) for x in both]
        far = same_ref[:, own_columns(t)]
        for part in range(2):
            above[part, t] = jnp.where(low_illum, unpack_rows(far, False)[part], near[part])
            below[part, t] = jnp.where(low_illum, near[part], unpack_rows(far, True)[part])

    def residual(t, rows, mask, ur, ui):
        for part, (g, u, m) in enumerate(((gr, ur, mr), (gi, ui, mi))):
            if rows.start == RIM:
                target = above[part, t]
            elif rows.start == 2 * RIM + stripe:
                target = below[part, t]
            else:
                target = m[t, own_rows(rows), :]
            g[t, rows, :] = mask(u - target)

    propagate(tile, (row_r, row_i, col_r, col_i), trig, (hr, hi), (w0r, w0i), (w1r, w1i), residual)


def other_near(swap_ref, stripe, low_illum, columns):
    packed = swap_ref[2 * stripe :, columns]
    high, low = unpack_rows(packed, False), unpack_rows(packed, True)
    return [jnp.where(low_illum, low[part], high[part]) for part in range(2)]


def back_kernel(sizes, main_c1, main_s1, main_w0r, main_w0i, main_w1r, main_w1i, gr, gi,
                phase_ref, known_ref, partner_ref, along_ref, phase_rim_ref,
                own_ref, w0r, w0i, w1r, w1i, ur_ref, ui_ref, c1, s1,
                ar, ai, main_hr, main_hi, c0, s0, hr, hi, row_r, row_i, col_r, col_i):
    stripe, tiles, total_rows, total_cols = sizes
    main, row_first, _ = main_tile(sizes)
    held, columns = patch_held(sizes)
    tile = Tile(stripe, 1, main.top, main.bottom, held, 0, (0,))
    low_illum = place()[0] == 0
    blank_rims((ar, ai, main_hr, main_hi), main)
    blank_rims((w0r, w0i, w1r, w1i, hr, hi), tile)
    trig = (c0, s0), (c1, s1)
    end = stripe + RIM

    def joined(get, rim):
        x = join_edges(get(0), get(tiles - 1), rim)
        return join_illums(x, x)

    fill_trig(
        tile, trig, low_illum,
        lambda k, t, r: joined(lambda e: phase_ref[k, r : r + 16, own_columns(e)], phase_rim_ref[k, RIM + r : RIM + r + 16, :]),
        lambda k, t: joined(
            lambda e: partner_ref[:, own_columns(e + k * tiles)],
            jnp.where(low_illum, phase_rim_ref[k, end:, :], phase_rim_ref[k, :RIM, :]),
        ),
        lambda k, t: joined(
            lambda e: along_ref[:, own_columns(e + k * tiles)],
            jnp.where(low_illum, phase_rim_ref[k, :RIM, :], phase_rim_ref[k, end:, :]),
        ),
    )
    note = jnp.where(patch_lanes()[0], 0.0, 1.0)
    tilts = [a * note + b * (1.0 - note) for a, b in zip(tilts_of(known_ref[...]), tilts_of(partner_ref[:, 2 * tiles * LANES :]))]
    tables = (row_r, row_i, col_r, col_i)
    incident_tables(tile, tilts, row_first, columns, total_rows, total_cols, tables)
    ways = [
        propagate_steps(tile, tables, trig, (hr, hi), (w0r, w0i), (w1r, w1i), keep_in((ur_ref, ui_ref))),
        backward_steps(
            main, (gr, gi), (main_hr, main_hi), (main_w0r, main_w0i), (main_w1r, main_w1i), (main_c1, main_s1),
            put_in(own_ref), (ar, ai),
        ),
    ]
    for _ in range(4):
        for way in ways:
            next(way, None)


def sum_kernel(a_ref, b_ref, out_ref):
    out_ref[...] = a_ref[...] + b_ref[...]


def left_kernel(sizes, swap_ref, along_ref, w0r, w0i, w1r, w1i, ur, ui, c1, s1, left_ref, gr, gi, hr, hi, mr, mi):
    stripe, tiles, _, _ = sizes
    main, _, _ = main_tile(sizes)
    tile = Tile(stripe, swap_ref.shape[1] // LANES, main.top, main.bottom)
    low_illum = place()[0] == 0
    blank_rims((gr, gi, hr, hi), tile)
    fill_target(
        tile, (mr, mi), low_illum, None,
        lambda t: other_near(swap_ref, stripe, low_illum, own_columns(t)),
        lambda t: along_ref[:, own_columns(t + 2 * tiles)],
        range(tile.tiles),
    )
    residual_of(tile, (gr, gi), (ur, ui), other_target(tile, lambda rows, t: swap_ref[rows, own_columns(t)], (mr, mi)))
    backward(tile, (gr, gi), (hr, hi), (w0r, w0i), (w1r, w1i), (c1, s1), put_in(left_ref))


def other_target(tile, swapped, edges, patch=None):
    def target(part, t, rows):
        if t != patch and 2 * RIM <= rows.start < 2 * RIM + tile.stripe:
            at = own_rows(rows)
            return swapped(slice(part * tile.stripe + at.start, part * tile.stripe + at.stop), t)
        return edges[part][t, rows, :]

    return target


class Joined:
    def __init__(self, main, patch, first):
        self.main, self.patch, self.first = main, patch, first

    def __getitem__(self, at):
        t = at[0] + self.first
        return self.main[(t,) + at[1:]] if t < self.main.shape[0] else self.patch[(0,) + at[1:]]


def finish_kernel(sizes, own_ref, left_ref, measured_ref, swap_ref, swap_rest_ref, along_ref, same_ref, rim_ref, relay_ref,
                  partner_relay_ref, *rest):
    main_fields, patch_fields, rest = rest[:8], rest[8:16], rest[16:]
    out_ref, patch, gr, gi, hr, hi, mr, mi, full, sems = rest
    stripe, tiles, total_rows, total_cols = sizes
    left_tiles = swap_ref.shape[1] // LANES
    begin = left_tiles - 1
    lone = tiles - begin
    w0r, w0i, w1r, w1i, ur, ui, c1, s1 = [Joined(a, b, begin) for a, b in zip(main_fields, patch_fields)]
    main, _, _ = main_tile(sizes)
    tile = Tile(stripe, lone + 1, main.top, main.bottom, patch_held(sizes)[0], lone, (lone,))
    illum, _, _ = place()
    low_illum = illum == 0
    blank_rims((gr, gi, hr, hi), tile)

    lane = lane_ids((8, LANES))
    last_rows = relay_ref.shape[0] - 8
    sums = jnp.maximum(relay_ref[last_rows:, :], partner_relay_ref[last_rows:, :])
    scales = []
    for which in range(2):
        here = jnp.where(lane == which, sums, 0.0)
        energy = jnp.sum(here[:1], axis=1, keepdims=True) / (total_rows * total_cols) + EPS_ENERGY
        scales.append(2.0 / energy)
    mine = jnp.where(low_illum, scales[0], scales[1])
    others = jnp.where(low_illum, scales[1], scales[0])

    first, last = own_columns(0), own_columns(tiles - 1)
    own_first = illum * stripe
    near_base = pl.multiple_of(stripe - 16 * illum, 16)
    near_rim = pl.multiple_of(stripe - 8 * illum, 8)

    def swapped(rows, t):
        t = t + begin
        return swap_ref[rows, own_columns(t)] if t < left_tiles else swap_rest_ref[rows, own_columns(t - left_tiles)]

    def other_rim(part, block):
        x = partner_relay_ref[2 * (block // 4 * 4) : 2 * (block // 4 * 4) + 8, :]
        shift = (LANES - 2 * RIM * (block % 4) + part * (LANES // 2)) % LANES
        return pltpu.roll(x, shift, 1) if shift else x

    def middle(part, t, r):
        at = slice(part * stripe + r, part * stripe + r + 16)
        rim = jnp.concatenate([other_rim(part, r // 8), other_rim(part, r // 8 + 1)], axis=0)
        other = join_edges(swap_ref[at, first], swapped(at, lone - 1), rim)
        at = pl.ds(pl.multiple_of(own_first + r, 16), 16)
        own = join_edges(*[measured_ref[part, 0, at, e].astype(F32) for e in (first, last)], rim_ref[part, at, :])
        return join_illums(own, other)

    def near_of(t):
        t = t + begin
        ref, t = (swap_ref, t) if t < left_tiles else (swap_rest_ref, t - left_tiles)
        return other_near(ref, stripe, low_illum, own_columns(t))

    def near(t):
        if t < lone:
            return near_of(t)
        rims = [other_rim(part, stripe // 8) for part in range(2)]
        other = [join_edges(*x) for x in zip(near_of(-begin), near_of(lone - 1), rims)]

        def rows(part, at):
            x = measured_ref[part, 0, pl.ds(near_base, 16), at].astype(F32)
            return jnp.where(low_illum, x[:8], x[8:])

        own = [join_edges(rows(part, first), rows(part, last), rim_ref[part, pl.ds(near_rim, 8), :]) for part in range(2)]
        return [join_illums(*x) for x in zip(own, other)]

    def far(t):
        if t < lone:
            return along_ref[:, own_columns(t + begin + 2 * tiles)]
        other = join_edges(*[along_ref[:, own_columns(e + 2 * tiles)] for e in (0, tiles - 1)], rim_ref[1, 2 * stripe :, :])
        own = join_edges(same_ref[:, first], same_ref[:, last], rim_ref[0, 2 * stripe :, :])
        return join_illums(own, other)

    copies = []

    def send(k, columns):
        copies.append(pltpu.make_async_copy(full.at[k, :, columns], out_ref.at[k, :, columns], sems.at[len(copies)]))
        copies[-1].start()

    for k in range(2):
        for t in range(left_tiles):
            at = own_columns(t)
            full[k, :, at] = own_ref[k, :, at] * mine + left_ref[k, :, at] * others
        if begin > 1:
            send(k, slice(LANES, begin * LANES))

    fill_target(tile, (mr, mi), low_illum, middle, near, far, range(lone))
    residual_of(tile, (gr, gi), (ur, ui), other_target(tile, swapped, (mr, mi), lone))

    def put(k, t, rows, value):
        rows = own_rows(rows)
        if t == lone:
            patch[k, rows, :] = value * mine + pltpu.roll(value, LANES - OTHER, 1) * others
            return
        at = own_columns(t + begin)
        value = own_ref[k, rows, at] * mine + value * others
        if t == 0:
            value = jnp.where(lane_ids(value.shape) < LANES // 2, full[k, rows, at], value)
        full[k, rows, at] = value

    def close(k):
        on = lane_ids(patch.shape[1:])
        full[k, :, first] = jnp.where(on < RIM, patch[k], full[k, :, first])
        full[k, :, last] = jnp.where(on >= LANES - RIM, pltpu.roll(patch[k], 56, 1), full[k, :, last])
        if begin > 0:
            send(k, first)
        send(k, slice(begin * LANES, tiles * LANES))

    backward(tile, (gr, gi), (hr, hi), (w0r, w0i), (w1r, w1i), (c1, s1), put, on_middle=functools.partial(close, 1))
    close(0)
    for copy in copies:
        copy.wait()


def like(x, held):
    shape, dtype = (x, F32) if isinstance(x, tuple) else (x.shape, x.dtype)
    return pltpu.VMEM(shape, dtype) if held else jax.ShapeDtypeStruct(shape, dtype)


def after(kernel, *refs):
    count = len(refs)

    def ordered(*args):
        return kernel(*args[count:])

    return ordered


def call(kernel, outs, *args, behind=(), scratch=(), in_place=0, flops=0, mib=8, held=(), far=0):
    kernel, args = after(kernel, *behind), (*behind, *args)
    in_place_specs = [pl.BlockSpec(memory_space=pltpu.HBM)] * in_place
    return pl.pallas_call(
        kernel,
        out_shape=[like(x, n in held) for n, x in enumerate(outs)],
        in_specs=in_place_specs
        + [pl.BlockSpec(memory_space=pltpu.VMEM)] * (len(args) - in_place),
        out_specs=[pl.BlockSpec(memory_space=pltpu.VMEM)] * (len(outs) - far) + [pl.BlockSpec(memory_space=pltpu.HBM)] * far,
        scratch_shapes=[pltpu.VMEM(s, F32) if isinstance(s, tuple) else s for s in scratch],
        compiler_params=pltpu.CompilerParams(vmem_limit_bytes=int(mib * 2**20)),
        cost_estimate=pl.CostEstimate(flops=flops, bytes_accessed=2**18, transcendentals=0),
    )(*args)


def paired(phase_delay, angles, measured):
    slices, stripe, width = phase_delay.shape
    rows, cols = lax.axis_size("row"), lax.axis_size("col")
    tiles = width // LANES
    sizes = (stripe, tiles, 2 * stripe * rows, width * cols)
    swap = [(0, 1), (1, 0)]
    along = []
    for c in range(cols):
        for r in range(rows - 1):
            below, above = ((rows + r) * cols + c, (r + 1) * cols + c)
            along += [(below, above), (above, below)]
        along += [(c, c ^ 1), ((2 * rows - 1) * cols + c, (2 * rows - 1) * cols + (c ^ 1))]
    same = [(r, (r + 1) % rows) for r in range(rows)] + [(rows + (r + 1) % rows, rows + r) for r in range(rows)]

    partner_out, along_out, same_out, known, note, measured = call(
        open_kernel, [(8, 2 * width + LANES), (8, 3 * width), (8, width), (8, LANES), (8, LANES), measured],
        phase_delay, measured, angles, in_place=3, mib=62, held=(0, 1, 2, 3, 4, 5),
        scratch=[
            (2, slices, 8, width), pltpu.VMEM(angles.shape, angles.dtype), pltpu.SemaphoreType.DMA((4,)),
        ],
    )
    along_in = lax.ppermute(along_out, ("illum", "row", "col"), along)
    partner_in = lax.ppermute(partner_out, "illum", swap)
    same_in = lax.ppermute(same_out, ("illum", "row"), same)
    core_note = lax.ppermute(note, "row", [(r, r ^ 1) for r in range(rows)])
    (pair,) = call(sum_kernel, [(8, LANES)], note, core_note)
    far = lax.ppermute(pair, "row", [(r, r ^ 2) for r in range(rows)])
    cut = max(tiles - 2, 1) * LANES
    rows_swapped = 2 * stripe + 8
    (swap_out,) = call(
        functools.partial(swap_kernel, slice(0, cut)), [(rows_swapped, cut)], measured, behind=[core_note]
    )
    swap_in = lax.ppermute(swap_out, "illum", swap)

    def fields(count):
        return [(count, stripe + 4 * RIM, LANES)]

    def tables(count):
        return [(stripe + 2 * RIM, LANES)] * 2 + [(-(-count // 8) * 8, LANES)] * 2

    own_trig = call(
        functools.partial(trig_kernel, sizes), [(tiles, stripe, LANES)] * 6 + tables(tiles), phase_delay, measured, known,
        flops=3*10**9)
    rims = 8 * (-(-(stripe // 4 + 1) // 4))
    first_out, second_packed, note = call(
        rim_pack_kernel, [(rims + 8, LANES), (rims, LANES), (8, LANES)], phase_delay, measured, pair, far, partner_in, along_in, same_in,
        behind=own_trig[:1],
    )
    first_in = lax.ppermute(first_out, "col", [(c, cols - 1 - c) for c in range(cols)])
    kept = call(
        functools.partial(ahead_kernel, sizes), fields(tiles) * 10, *own_trig[:4], partner_in, along_in,
        scratch=fields(tiles) * 2 + tables(tiles), flops=15*10**8, mib=16,
    )
    (second_out,) = call(second_kernel, [(rims + 8, LANES)], second_packed, note, first_in, behind=kept[:1])
    second_in = lax.ppermute(second_out, "col", [(c, c ^ 1) for c in range(cols)])

    own_kept = call(
        functools.partial(own_kernel, sizes), fields(tiles) * 6, *kept[:4], *own_trig[4:], measured, same_in,
        scratch=fields(tiles) * 2 + [(2, tiles, RIM, LANES)] * 2, flops=15*10**8, mib=16,
    )
    phase_rim, rim, relay = call(
        rim_unpack_kernel, [(2, stripe + 2 * RIM, LANES), (2, 2 * stripe + 8, LANES), (8 * (-(-(stripe // 8 + 1) // 4)) + 8, LANES)],
        first_in, second_in, note,
        behind=own_kept[:1],
    )
    partner_relay = lax.ppermute(relay, "illum", swap)
    (swap_out,) = call(
        functools.partial(swap_kernel, slice(cut, width)), [(rows_swapped, width - cut)], measured, behind=own_kept[:1]
    )
    swap_rest = lax.ppermute(swap_out, "illum", swap)
    own, *patch_kept = call(
        functools.partial(back_kernel, sizes), [phase_delay.shape] + fields(1) * 8, *kept[2:4], *own_kept,
        phase_delay, known, partner_in, along_in, phase_rim,
        behind=[relay], scratch=fields(tiles) * 4 + fields(1) * 4 + tables(1), flops=10**9, mib=12,
    )
    (left,) = call(
        functools.partial(left_kernel, sizes), [(slices, stripe, cut)], swap_in, along_in, *kept[4:], *kept[2:4],
        behind=patch_kept[:1], scratch=fields(cut // LANES) * 6, flops=10**9, mib=12,
    )
    (out,) = call(
        functools.partial(finish_kernel, sizes), [phase_delay.shape],
        own, left, measured, swap_in, swap_rest, along_in, same_in, rim, relay, partner_relay,
        *kept[4:], *kept[2:4], *patch_kept,
        scratch=[(slices, stripe, LANES)] + fields(tiles - cut // LANES + 2) * 6
        + [phase_delay.shape, pltpu.SemaphoreType.DMA((6,))],
        mib=12, flops=0, far=1,
    )
    return out


def halo(x, axis, dim, width, index_of=None):
    peers = lax.axis_size(axis)
    up = [(i, i + 1) for i in range(peers - 1)]
    before = lax.ppermute(lax.slice_in_dim(x, x.shape[dim] - width, x.shape[dim], axis=dim), axis, up)
    after = lax.ppermute(lax.slice_in_dim(x, 0, width, axis=dim), axis, [(j, i) for i, j in up])
    return before, after


def with_column_rims(x, width):
    before, after = halo(x, "col", x.ndim - 1, width)
    gap = jnp.zeros(x.shape[:-1] + (LANES - 2 * width,), x.dtype)
    return jnp.concatenate([x, after, gap, before], axis=-1)


def stripe_halo(x, width):
    illums, rows = lax.axis_size("illum"), lax.axis_size("row")
    where = [(s % illums) * rows + s // illums for s in range(illums * rows)]
    up = [(where[s], where[s + 1]) for s in range(illums * rows - 1)]
    before = lax.ppermute(x[:, -width:], ("illum", "row"), up)
    after = lax.ppermute(x[:, :width], ("illum", "row"), [(b, a) for a, b in up])
    return jnp.concatenate([before, x, after], axis=1)


def per_device(phase_delay, angles, measured):
    illums = lax.axis_size("illum")
    if (illums, lax.axis_size("row"), lax.axis_size("col")) == (2, 4, 4):
        return paired(phase_delay, angles, measured)
    slices, stripe, width = phase_delay.shape
    tile_rows = measured.shape[2]
    total_rows, total_cols = tile_rows * lax.axis_size("row"), width * lax.axis_size("col")
    tiles = width // LANES + 1
    row_first = lax.axis_index("row") * tile_rows + lax.axis_index("illum") * stripe
    col_first = lax.axis_index("col") * width

    target = measured[:, 0].astype(F32)
    energy = lax.psum(jnp.sum(target * target).reshape(1), ("row", "col"))
    energies = lax.all_gather(energy, "illum", tiled=True) / (total_rows * total_cols) + EPS_ENERGY
    tilts = lax.all_gather(angles, "illum", tiled=True)

    phase = with_column_rims(stripe_halo(phase_delay, RIM), RIM)
    above, below = halo(target, "row", 1, REACH)
    target = with_column_rims(jnp.concatenate([above, target, below], axis=1), REACH)
    windows = jnp.stack([target[:, i * stripe : (i + 1) * stripe + 2 * REACH] for i in range(illums)])
    windows = lax.all_to_all(windows, "illum", 0, 0, tiled=True)
    windows = jnp.pad(windows, ((0, 0), (0, 0), (RIM - REACH, RIM - REACH), (0, 0)))

    field = pltpu.VMEM((tiles, stripe + 4 * RIM, LANES), F32)
    rows_all = stripe + 2 * RIM
    return pl.pallas_call(
        functools.partial(gradient_kernel, (stripe, tiles, illums, total_rows, total_cols)),
        out_shape=jax.ShapeDtypeStruct(phase_delay.shape, F32),
        in_specs=[pl.BlockSpec(memory_space=pltpu.SMEM)] * 3 + [pl.BlockSpec(memory_space=pltpu.VMEM)] * 2,
        out_specs=pl.BlockSpec(memory_space=pltpu.VMEM),
        scratch_shapes=[field] * 12
        + [pltpu.VMEM((rows_all, LANES), F32)] * 2
        + [pltpu.VMEM((-(-tiles // 8) * 8, LANES), F32)] * 2,
        compiler_params=pltpu.CompilerParams(vmem_limit_bytes=48 * 2**20),
    )(jnp.stack([row_first, col_first]), tilts, 2.0 / energies, phase, windows)


def solution(mesh):
    placed = (P(None, ("row", "illum"), "col"), P("illum", None), P(None, "illum", "row", "col"))
    return jax.shard_map(
        per_device,
        mesh=mesh,
        in_specs=placed,
        out_specs=P(None, ("row", "illum"), "col"),
        check_vma=False,
    )
```

```python
import functools
import math

import jax
import jax.numpy as jnp
from jax import lax
from jax.experimental import pallas as pl
from jax.experimental.pallas import tpu as pltpu
from jax.sharding import PartitionSpec as P

EPS_ENERGY = 1e-06
RIM = 8
REACH = 4
LANES = 128
F32 = jnp.float32


def sine_cosine(x):
    y = x * x
    s = -2.5052108385441718e-08
    for c in (2.7557319223985893e-06, -1.9841269841269841e-04, 8.333333333333333e-03, -1.6666666666666666e-01):
        s = s * y + c
    c_ = -2.7557319223985888e-07
    for c in (2.48015873015873e-05, -1.3888888888888889e-03, 4.1666666666666664e-02, -0.5, 1.0):
        c_ = c_ * y + c
    return x + x * y * s, c_


def sine_cosine_of_turns(turns):
    quarters = 4.0 * (turns - jnp.floor(turns))
    nearest = jnp.floor(quarters + 0.5)
    s, c = sine_cosine((quarters - nearest) * (0.5 * math.pi))
    odd = (nearest == 1.0) | (nearest == 3.0)
    s, c = jnp.where(odd, c, s), jnp.where(odd, s, c)
    s = jnp.where((nearest == 2.0) | (nearest == 3.0), -s, s)
    c = jnp.where((nearest == 1.0) | (nearest == 2.0), -c, c)
    return s, c


def lane_ids(shape):
    return lax.broadcasted_iota(jnp.int32, shape, len(shape) - 1)


class Tile:
    def __init__(self, stripe, tiles, top, bottom, lanes=None, rim=None, alone=()):
        self.stripe, self.tiles = stripe, tiles
        self.rows = stripe + 2 * RIM
        self.top, self.bottom, self.lanes, self.rim = top, bottom, lanes, rim
        self.alone = alone
        self.order = [*alone, *range(1, tiles - len(alone)), *([0] if tiles > len(alone) else [])]
        self.owned = tiles if rim in alone or rim is None else tiles - 1
        step = 32 if stripe % 32 == 0 else 8
        self.inner = [(2 * RIM + r, step, None) for r in range(0, stripe, step)]
        self.blocks = [(RIM, RIM, top)] + self.inner + [(2 * RIM + stripe, RIM, bottom)]

    def sweep(self, body, blocks, fields=()):
        for first, count, factor in blocks:
            rows = pl.ds(first, count)
            held = {}

            def load(ref, t, rows=rows, held=held):
                key = id(ref), t
                if key not in held:
                    held[key] = ref[t, rows, :]
                return held[key]

            for t in self.order:

                def mask(x, factor=factor, lanes=self.lanes if t == self.rim else None):
                    x = x if factor is None else x * factor
                    return x if lanes is None else x * lanes

                body(t, rows, mask, [self.beside(ref, t, rows, load) for ref in fields])

    def beside(self, ref, t, rows, load):
        above = pl.ds(rows.start - 1, rows.size)
        below = pl.ds(rows.start + 1, rows.size)
        here = load(ref, t)
        west = east = here
        if t not in self.alone:
            ring = self.tiles - len(self.alone)
            lane = lane_ids(here.shape)
            west = jnp.where(lane == LANES - 1, load(ref, (t - 1) % ring), here)
            east = jnp.where(lane == 0, load(ref, (t + 1) % ring), here)
        west, east = pltpu.roll(west, 1, 1), pltpu.roll(east, LANES - 1, 1)
        return here, (ref[t, above, :] + ref[t, below, :]) + (west + east)


def first_half(tile, field, half, sign, blocks):
    def body(t, rows, mask, sums):
        (real, beside_real), (imag, beside_imag) = sums
        half[0][t, rows, :] = mask(beside_real + (2.0 * sign) * imag)
        half[1][t, rows, :] = mask(beside_imag - (2.0 * sign) * real)

    tile.sweep(body, blocks, field)


def second_half(tile, field, half, blocks, use):
    def body(t, rows, mask, sums):
        (_, beside_real), (_, beside_imag) = sums
        use(t, rows, mask, 0.1 * beside_real - field[0][t, rows, :], 0.1 * beside_imag - field[1][t, rows, :])

    tile.sweep(body, blocks, half)


def blank_rims(refs, tile):
    for ref in refs:
        for first in (0, tile.rows + RIM):
            ref[:, first : first + RIM, :] = jnp.zeros((tile.tiles, RIM, LANES), F32)


def rim_columns(tile, col_first, shape):
    at, on = lax.broadcasted_iota(jnp.int32, shape, 0), lane_ids(shape)
    return col_first + jnp.where((at >= tile.owned) & (on >= LANES // 2), on - LANES, at * LANES + on)


def incident_tables(tile, tilts, row_first, columns, total_rows, total_cols, tables):
    row_r, row_i, col_r, col_i = tables
    ids = lax.broadcasted_iota(jnp.int32, (tile.rows, LANES), 0) + (row_first - RIM)
    s, c = sine_cosine_of_turns(ids.astype(F32) * tilts[0] / total_rows)
    row_r[...] = (-7.0 * c - 24.0 * s) * 0.04
    row_i[...] = (-7.0 * s + 24.0 * c) * 0.04
    col_i[...], col_r[...] = sine_cosine_of_turns(columns.astype(F32) * tilts[1] / total_cols)


def enter(tile, tables, trig, field):
    row_r, row_i, col_r, col_i = tables
    fr, fi = field

    def start(t, rows, mask, _):
        at = pl.ds(rows.start - RIM, rows.size)
        ar, ai = row_r[at, :], row_i[at, :]
        br, bi = col_r[t : t + 1, :], col_i[t : t + 1, :]
        ur, ui = ar * br - ai * bi, ar * bi + ai * br
        c, s = trig[0][t, rows, :], trig[1][t, rows, :]
        fr[t, rows, :] = mask(ur * c - ui * s)
        fi[t, rows, :] = mask(ur * s + ui * c)

    tile.sweep(start, tile.blocks)


def modulate_into(trig, field):
    def use(t, rows, mask, ur, ui):
        c, s = trig[0][t, rows, :], trig[1][t, rows, :]
        field[0][t, rows, :] = mask(ur * c - ui * s)
        field[1][t, rows, :] = mask(ur * s + ui * c)

    return use


def backward(*args, **kwargs):
    for _ in backward_steps(*args, **kwargs):
        pass


def backward_steps(tile, adjoint, half, w0, w1, trig1, put, between=None, on_middle=None, on_rows=None):
    between = between or adjoint
    gr, gi = between
    inner = [first for first, _, _ in tile.inner]

    def back(t, rows, mask, ur, ui):
        if t < tile.owned and rows.start in inner:
            put(1, t, rows, ui * w1[0][t, rows, :] - ur * w1[1][t, rows, :])
        c, s = trig1[0][t, rows, :], trig1[1][t, rows, :]
        gr[t, rows, :] = mask(ur * c + ui * s)
        gi[t, rows, :] = mask(ui * c - ur * s)

    def last(t, rows, mask, ur, ui):
        if t < tile.owned:
            put(0, t, rows, ui * w0[0][t, rows, :] - ur * w0[1][t, rows, :])

    first_half(tile, adjoint, half, -1.0, tile.blocks)
    yield
    second_half(tile, adjoint, half, tile.blocks, back)
    yield
    if on_middle:
        on_middle()
    first_half(tile, between, half, -1.0, tile.blocks)
    yield
    for block in tile.inner if on_rows is None else [(r, 16, None) for r in range(2 * RIM, 2 * RIM + tile.stripe, 16)]:
        second_half(tile, between, half, [block], last)
        if on_rows:
            on_rows(block[0] - 2 * RIM)


def own_columns(t):
    return slice(t * LANES, (t + 1) * LANES)


def own_rows(rows):
    return slice(rows.start - 2 * RIM, rows.start - 2 * RIM + rows.size)


def gradient_kernel(sizes, place_ref, angles_ref, scale_ref, phase_ref, target_ref, out_ref,
                    c0, s0, c1, s1, w0r, w0i, w1r, w1i, gr, gi, hr, hi, row_r, row_i, col_r, col_i):
    stripe, tiles, illums, total_rows, total_cols = sizes
    row_first, col_first = place_ref[0], place_ref[1]
    edges = edges_of(row_first, col_first, stripe, tiles, total_rows, total_cols)
    tile = Tile(stripe, tiles, *edges, rim=tiles - 1)
    blank_rims((w0r, w0i, w1r, w1i, gr, gi, hr, hi), tile)
    out_ref[...] = jnp.zeros(out_ref.shape, F32)
    span = slice(RIM, RIM + tile.rows)
    for t in range(tiles):
        for k, (c, s) in enumerate(((c0, s0), (c1, s1))):
            s[t, span, :], c[t, span, :] = sine_cosine(phase_ref[k, :, own_columns(t)])
    tables, half = (row_r, row_i, col_r, col_i), (hr, hi)

    def illum(j, carry):
        tilts = angles_ref[j, 0].astype(F32), angles_ref[j, 1].astype(F32)
        incident_tables(tile, tilts, row_first, rim_columns(tile, col_first, col_r.shape), total_rows, total_cols, tables)
        enter(tile, tables, (c0, s0), (w0r, w0i))
        first_half(tile, (w0r, w0i), half, 1.0, tile.blocks)
        second_half(tile, (w0r, w0i), half, tile.blocks, modulate_into((c1, s1), (w1r, w1i)))
        first_half(tile, (w1r, w1i), half, 1.0, tile.blocks)

        def residual(t, rows, mask, ur, ui):
            at = slice(rows.start - RIM, rows.start - RIM + rows.size)
            gr[t, rows, :] = mask(ur - target_ref[j, 0, at, own_columns(t)])
            gi[t, rows, :] = mask(ui - target_ref[j, 1, at, own_columns(t)])

        second_half(tile, (w1r, w1i), half, tile.blocks, residual)

        def put(k, t, rows, value):
            at = (k, own_rows(rows), own_columns(t))
            out_ref[at] = out_ref[at] + scale_ref[j] * value

        backward(tile, (gr, gi), half, (w0r, w0i), (w1r, w1i), (c1, s1), put)
        return carry

    lax.fori_loop(0, illums, illum, 0)


def edges_of(row_first, col_first, stripe, tiles, total_rows, total_cols):
    width = (tiles - 1) * LANES
    top = jnp.where(row_first == 0, 0.0, 1.0).astype(F32)
    bottom = jnp.where(row_first + stripe == total_rows, 0.0, 1.0).astype(F32)
    lane = lane_ids((1, LANES))
    in_west = (lane >= LANES - RIM) & (col_first > 0)
    in_east = (lane < RIM) & (col_first + width < total_cols)
    return top, bottom, jnp.where(in_west | in_east, 1.0, 0.0).astype(F32)


def place():
    return lax.axis_index("illum"), lax.axis_index("row"), lax.axis_index("col")


def pack_rows(real, imag, low):
    first = lax.broadcasted_iota(jnp.int32, real.shape, 0) < 4
    if low:
        return jnp.where(first, real, pltpu.roll(imag, 4, 0))
    return jnp.where(first, pltpu.roll(real, 4, 0), imag)


def unpack_rows(packed, low):
    turned = pltpu.roll(packed, 4, 0)
    return (packed, turned) if low else (turned, packed)


def edge_blocks(measured_ref, first):
    base = first // 16 * 16
    at = first - base
    return [measured_ref[p, 0, base : base + 16, :].astype(F32)[at : at + 8] for p in range(2)]


def open_kernel(phase_ref, measured_ref, tilt_ref, partner_ref, along_ref, same_ref, known_ref, note_ref, held, edge, tilt, sems):
    stripe, width = phase_ref.shape[1:]
    rows = 2 * stripe
    illum, _, _ = place()
    field_copy = pltpu.make_async_copy(measured_ref, held, sems.at[0])
    tilt_copy = pltpu.make_async_copy(tilt_ref, tilt, sems.at[3])
    edge_copies = [
        pltpu.make_async_copy(phase_ref.at[:, pl.ds(first, 8), :], edge.at[e], sems.at[1 + e])
        for e, first in enumerate((0, stripe - 8))
    ]
    for copy in edge_copies:
        copy.start()
    field_copy.start()
    tilt_copy.start()
    for copy in edge_copies:
        copy.wait()
    for k in range(2):
        top, bottom = edge[0, k], edge[1, k]
        along_ref[:, k * width : (k + 1) * width] = jnp.where(illum == 0, top, bottom)
        partner_ref[:, k * width : (k + 1) * width] = jnp.where(illum == 0, bottom, top)
    field_copy.wait()
    top, bottom = pack_rows(*edge_blocks(held, 0), True), pack_rows(*edge_blocks(held, rows - 8), False)
    along_ref[:, 2 * width :] = jnp.where(illum == 0, top, bottom)
    same_ref[...] = jnp.where(illum == 0, bottom, top)
    total = jnp.zeros((8, width), F32)
    for p in range(2):
        for r in range(0, rows, 16):
            x = held[p, 0, r : r + 16, :].astype(F32)
            x = x * x
            total = total + (x[:8] + x[8:])
    energy = jnp.sum(jnp.sum(total, axis=1, keepdims=True), axis=0, keepdims=True)
    lane = lane_ids((8, LANES))
    note_ref[...] = jnp.where(lane == illum, energy, 0.0)
    note = jnp.zeros((8, LANES), F32)
    tilt_copy.wait()
    for n in range(2):
        note = jnp.where(lane == 16 + n, tilt[:, n : n + 1].astype(F32), note)
    partner_ref[:, 2 * width :] = note
    known_ref[...] = note


def swap_kernel(columns, measured_ref, swap_ref):
    stripe = measured_ref.shape[2] // 2
    illum, _, _ = place()
    other = pl.multiple_of((1 - illum) * stripe, 16)
    for p in range(2):
        for r in range(0, stripe, 16):
            at = pl.ds(pl.multiple_of(other + r, 16), 16)
            swap_ref[p * stripe + r : p * stripe + r + 16, :] = measured_ref[p, 0, at, columns].astype(F32)
    above = pack_rows(*[x[:, columns] for x in edge_blocks(measured_ref, stripe - 8)], False)
    below = pack_rows(*[x[:, columns] for x in edge_blocks(measured_ref, stripe)], True)
    swap_ref[2 * stripe :, :] = jnp.where(illum == 0, above, below)


def rim_pack_kernel(phase_ref, measured_ref, pair_ref, far_ref, partner_ref, along_ref, same_ref, first_ref, second_ref, note_ref):
    stripe, width = phase_ref.shape[1:]
    rows = 2 * stripe
    illum, _, col = place()
    low_illum = illum == 0
    even = lax.rem(col, 2) == 0
    lane = lane_ids((8, LANES))
    note = pair_ref[...] + far_ref[...]
    note_ref[...] = note
    first_ref[first_ref.shape[0] - 8 :, :] = note

    def packed(east):
        edge = slice(width - LANES, width) if east else slice(0, LANES)
        base = LANES - RIM if east else 0
        groups = []
        for j in range(stripe // 8 + 2):
            items = []
            for k in range(2):
                tile = slice(k * width + edge.start, k * width + edge.stop)
                if j == 0:
                    items.append(jnp.where(low_illum, along_ref[:, tile], partner_ref[:, tile]))
                elif j == stripe // 8 + 1:
                    items.append(jnp.where(low_illum, partner_ref[:, tile], along_ref[:, tile]))
                else:
                    items.append(phase_ref[k, 8 * (j - 1) : 8 * j, edge])
            groups.append(items)
        while len(groups) < rows // 8 + 1:
            groups.append([None, None])
        for r in range(0, rows, 16):
            both = [measured_ref[p, 0, r : r + 16, edge].astype(F32) for p in range(2)]
            for h in range(2):
                groups[r // 8 + h] += [b[8 * h : 8 * h + 8] for b in both]
        groups[rows // 8] += [same_ref[:, edge], along_ref[:, 2 * width + edge.start : 2 * width + edge.stop]]
        for g in range(0, len(groups), 4):
            acc = jnp.zeros((8, LANES), F32)
            for q, items in enumerate(groups[g : g + 4]):
                for k, item in enumerate(items):
                    if item is not None:
                        slot = 4 * q + k
                        shift = (8 * slot - base) % LANES
                        moved = pltpu.roll(item, shift, 1) if shift else item
                        acc = jnp.where((lane >= 8 * slot) & (lane < 8 * slot + 8), moved, acc)
            yield 2 * g, acc

    for (at, east), (_, west) in zip(packed(True), packed(False)):
        first_ref[at : at + 8, :] = jnp.where(even, west, east)
        second_ref[at : at + 8, :] = jnp.where(even, east, west)


def second_kernel(packed_ref, note_ref, first_ref, out_ref):
    rims = packed_ref.shape[0]
    out_ref[:rims, :] = packed_ref[...]
    out_ref[rims:, :] = note_ref[...] + first_ref[rims:, :]


def rim_unpack_kernel(first_ref, second_ref, note_ref, phase_rim_ref, rim_ref, relay_ref):
    stripe = phase_rim_ref.shape[1] - 2 * RIM
    rims, rows = first_ref.shape[0] - 8, 2 * stripe
    illum, _, col = place()
    even = lax.rem(col, 2) == 0
    lane = lane_ids((8, LANES))
    in_west = (lane >= LANES - RIM) & (col > 0)
    in_east = (lane < RIM) & (col < lax.axis_size("col") - 1)
    for g in range(0, rows // 8 + 1, 4):
        first, second = first_ref[2 * g : 2 * g + 8, :], second_ref[2 * g : 2 * g + 8, :]
        a, b = jnp.where(even, first, second), jnp.where(even, second, first)
        for j in range(g, min(g + 4, rows // 8 + 1)):
            for k in range(4):
                if k < 2 and j >= stripe // 8 + 2:
                    continue
                slot = 4 * (j - g) + k
                from_west = pltpu.roll(a, (LANES - RIM - 8 * slot) % LANES, 1)
                from_east = pltpu.roll(b, (-8 * slot) % LANES, 1) if slot else b
                item = jnp.where(in_west, from_west, jnp.where(in_east, from_east, 0.0))
                (phase_rim_ref if k < 2 else rim_ref)[k % 2, 8 * j : 8 * j + 8, :] = item
    other = pl.multiple_of((1 - illum) * stripe, 8)
    near = pl.multiple_of(stripe - 8 + 8 * illum, 8)
    blocks = [pl.multiple_of(other + r, 8) for r in range(0, stripe, 8)] + [near]
    for g in range(0, len(blocks), 4):
        packed = jnp.zeros((8, LANES), F32)
        for q, first in enumerate(blocks[g : g + 4]):
            at = pl.ds(first, 8)
            x = rim_ref[0, at, :] + pltpu.roll(rim_ref[1, at, :], LANES // 2, 1)
            packed = packed + (pltpu.roll(x, 2 * RIM * q, 1) if q else x)
        relay_ref[2 * g : 2 * g + 8, :] = packed
    relay_ref[relay_ref.shape[0] - 8 :, :] = note_ref[...] + first_ref[rims:, :] + second_ref[rims:, :]


def fill_target(tile, target, low_illum, middle, near, far, plain=()):
    end = 2 * RIM + tile.stripe
    for t in range(tile.tiles):
        beside_rows, packed = near(t), far(t)
        for part, ref in enumerate(target):
            for r in range(0, tile.stripe, 16) if t not in plain else ():
                ref[t, 2 * RIM + r : 2 * RIM + r + 16, :] = middle(part, t, r)
            ref[t, RIM : 2 * RIM, :] = jnp.where(low_illum, unpack_rows(packed, False)[part], beside_rows[part])
            ref[t, end : end + RIM, :] = jnp.where(low_illum, beside_rows[part], unpack_rows(packed, True)[part])


def fill_trig(tile, trig, low_illum, middle, near, far):
    for t in range(tile.tiles):
        for k, (c, s) in enumerate(trig):
            above, below = far(k, t), near(k, t)
            here = [(RIM, jnp.where(low_illum, above, below)), (2 * RIM + tile.stripe, jnp.where(low_illum, below, above))]
            here += [(2 * RIM + r, middle(k, t, r)) for r in range(0, tile.stripe, 16)]
            for first, x in here:
                s[t, first : first + x.shape[0], :], c[t, first : first + x.shape[0], :] = sine_cosine(x)


def tilts_of(note):
    lane = lane_ids(note.shape)
    return [jnp.sum(jnp.where(lane == n, note, 0.0)[:1], axis=1, keepdims=True) for n in (16, 17)]


def forward(tile, tilts, columns, row_first, totals, trig, half, tables, w0, w1, use):
    incident_tables(tile, tilts, row_first, columns, *totals, tables)
    propagate(tile, tables, trig, half, w0, w1, use)


def propagate(*args):
    for _ in propagate_steps(*args):
        pass


def propagate_steps(tile, tables, trig, half, w0, w1, use):
    enter(tile, tables, trig[0], w0)
    first_half(tile, w0, half, 1.0, tile.blocks)
    yield
    second_half(tile, w0, half, tile.blocks, modulate_into(trig[1], w1))
    yield
    first_half(tile, w1, half, 1.0, tile.blocks)
    yield
    second_half(tile, w1, half, tile.blocks, use)


def keep_in(field):
    def use(t, rows, mask, ur, ui):
        field[0][t, rows, :] = ur
        field[1][t, rows, :] = ui

    return use


def residual_in(field, target):
    def use(t, rows, mask, ur, ui):
        field[0][t, rows, :] = mask(ur - target[0][t, rows, :])
        field[1][t, rows, :] = mask(ui - target[1][t, rows, :])

    return use


def residual_of(tile, field, exit_field, target):
    def body(t, rows, mask, _):
        for part, (g, u) in enumerate(zip(field, exit_field)):
            g[t, rows, :] = mask(u[t, rows, :] - target(part, t, rows))

    tile.sweep(body, tile.blocks)


def put_in(ref):
    def put(k, t, rows, value):
        ref[k, own_rows(rows), own_columns(t)] = value

    return put


def main_tile(sizes):
    stripe, tiles, total_rows, total_cols = sizes
    illum, row, col = place()
    row_first = (row * 2 + illum) * stripe
    top, bottom, _ = edges_of(row_first, 0, stripe, tiles + 1, total_rows, total_cols)
    return Tile(stripe, tiles, top, bottom), row_first, col * tiles * LANES


OTHER = 28


def patch_lanes():
    lane = lane_ids((1, LANES))
    other = ((lane >= OTHER - RIM) & (lane < OTHER + 16)) | ((lane >= 56 + OTHER) & (lane < 80 + OTHER))
    return other, jnp.where(other, (lane + (LANES - OTHER)) % LANES, lane)


def patch_held(sizes):
    stripe, tiles, total_rows, total_cols = sizes
    _, _, col_first = main_tile(sizes)
    width = tiles * LANES
    _, at = patch_lanes()
    held = (at < 16) | ((at >= 56) & (at < 72))
    held = held | ((at >= 72) & (at < 80) & (col_first + width < total_cols))
    held = held | ((at >= LANES - RIM) & (col_first > 0))
    columns = jnp.where(at < 16, at, jnp.where(at < 80, at - 72 + width, at - LANES)) + col_first
    return jnp.where(held, 1.0, 0.0).astype(F32), jnp.broadcast_to(columns, (8, LANES))


def join_edges(west, east, rim):
    lane = lane_ids(west.shape)
    moved = pltpu.roll(jnp.where(lane < RIM, rim, east), 72, 1)
    return jnp.where(lane < 16, west, jnp.where(lane >= LANES - RIM, rim, moved))


def join_illums(own, other):
    return jnp.where(patch_lanes()[0], pltpu.roll(other, OTHER, 1), own)


def trig_kernel(sizes, phase_ref, measured_ref, known_ref, c0, s0, c1, s1, mr, mi, row_r, row_i, col_r, col_i):
    stripe, tiles, total_rows, total_cols = sizes
    tile, row_first, col_first = main_tile(sizes)
    illum, _, _ = place()
    columns = rim_columns(tile, col_first, col_r.shape)
    tables = (row_r, row_i, col_r, col_i)
    incident_tables(tile, tilts_of(known_ref[...]), row_first, columns, total_rows, total_cols, tables)
    for part, m in enumerate((mr, mi)):
        for t in range(tiles):
            for r in range(0, stripe, 16):
                at = pl.ds(pl.multiple_of(illum * stripe + r, 16), 16)
                m[t, r : r + 16, :] = measured_ref[part, 0, at, own_columns(t)].astype(F32)
    for t in range(c0.shape[0]):
        for k, (c, s) in enumerate(((c0, s0), (c1, s1))):
            for r in range(0, c.shape[1], 16):
                s[t, r : r + 16, :], c[t, r : r + 16, :] = sine_cosine(phase_ref[k, r : r + 16, own_columns(t)])


def ahead_kernel(sizes, own_c0, own_s0, own_c1, own_s1, partner_ref, along_ref,
                 c0, s0, c1, s1, w0r, w0i, w1r, w1i, ur_ref, ui_ref, hr, hi, row_r, row_i, col_r, col_i):
    stripe, tiles, total_rows, total_cols = sizes
    tile, row_first, col_first = main_tile(sizes)
    illum, _, _ = place()
    low_illum = illum == 0
    blank_rims((w0r, w0i, w1r, w1i, hr, hi), tile)
    trig = (c0, s0), (c1, s1)
    end = 2 * RIM + stripe
    for t in range(tiles):
        for k, (mine, here) in enumerate((((own_c0, own_s0), trig[0]), ((own_c1, own_s1), trig[1]))):
            far, near = along_ref[:, own_columns(t + k * tiles)], partner_ref[:, own_columns(t + k * tiles)]
            above = sine_cosine(jnp.where(low_illum, far, near))
            below = sine_cosine(jnp.where(low_illum, near, far))
            for part in range(2):
                here[part][t, 2 * RIM : end, :] = mine[part][t]
                here[part][t, RIM : 2 * RIM, :] = above[1 - part]
                here[part][t, end : end + RIM, :] = below[1 - part]
    forward(
        tile, tilts_of(partner_ref[:, 2 * tiles * LANES :]), rim_columns(tile, col_first, col_r.shape), row_first,
        (total_rows, total_cols), trig, (hr, hi), (row_r, row_i, col_r, col_i),
        (w0r, w0i), (w1r, w1i), keep_in((ur_ref, ui_ref)),
    )


def own_kernel(sizes, c0, s0, c1, s1, mr, mi, row_r, row_i, col_r, col_i, measured_ref, same_ref,
               w0r, w0i, w1r, w1i, gr, gi, hr, hi, above, below):
    stripe, tiles, total_rows, total_cols = sizes
    tile, row_first, col_first = main_tile(sizes)
    illum, _, _ = place()
    low_illum = illum == 0
    blank_rims((w0r, w0i, w1r, w1i, gr, gi, hr, hi), tile)
    trig = (c0, s0), (c1, s1)
    near_base = pl.multiple_of(stripe - 16 * illum, 16)
    for t in range(tiles):
        both = [measured_ref[part, 0, pl.ds(near_base, 16), own_columns(t)].astype(F32) for part in range(2)]
        near = [jnp.where(low_illum, x[:8], x[8:]) for x in both]
        far = same_ref[:, own_columns(t)]
        for part in range(2):
            above[part, t] = jnp.where(low_illum, unpack_rows(far, False)[part], near[part])
            below[part, t] = jnp.where(low_illum, near[part], unpack_rows(far, True)[part])

    def residual(t, rows, mask, ur, ui):
        for part, (g, u, m) in enumerate(((gr, ur, mr), (gi, ui, mi))):
            if rows.start == RIM:
                target = above[part, t]
            elif rows.start == 2 * RIM + stripe:
                target = below[part, t]
            else:
                target = m[t, own_rows(rows), :]
            g[t, rows, :] = mask(u - target)

    propagate(tile, (row_r, row_i, col_r, col_i), trig, (hr, hi), (w0r, w0i), (w1r, w1i), residual)


def other_near(swap_ref, stripe, low_illum, columns):
    packed = swap_ref[2 * stripe :, columns]
    high, low = unpack_rows(packed, False), unpack_rows(packed, True)
    return [jnp.where(low_illum, low[part], high[part]) for part in range(2)]


def back_kernel(sizes, main_c1, main_s1, main_w0r, main_w0i, main_w1r, main_w1i, gr, gi,
                phase_ref, known_ref, partner_ref, along_ref, phase_rim_ref,
                own_ref, w0r, w0i, w1r, w1i, ur_ref, ui_ref, c1, s1,
                ar, ai, main_hr, main_hi, c0, s0, hr, hi, row_r, row_i, col_r, col_i):
    stripe, tiles, total_rows, total_cols = sizes
    main, row_first, _ = main_tile(sizes)
    held, columns = patch_held(sizes)
    tile = Tile(stripe, 1, main.top, main.bottom, held, 0, (0,))
    low_illum = place()[0] == 0
    blank_rims((ar, ai, main_hr, main_hi), main)
    blank_rims((w0r, w0i, w1r, w1i, hr, hi), tile)
    trig = (c0, s0), (c1, s1)
    end = stripe + RIM

    def joined(get, rim):
        x = join_edges(get(0), get(tiles - 1), rim)
        return join_illums(x, x)

    fill_trig(
        tile, trig, low_illum,
        lambda k, t, r: joined(lambda e: phase_ref[k, r : r + 16, own_columns(e)], phase_rim_ref[k, RIM + r : RIM + r + 16, :]),
        lambda k, t: joined(
            lambda e: partner_ref[:, own_columns(e + k * tiles)],
            jnp.where(low_illum, phase_rim_ref[k, end:, :], phase_rim_ref[k, :RIM, :]),
        ),
        lambda k, t: joined(
            lambda e: along_ref[:, own_columns(e + k * tiles)],
            jnp.where(low_illum, phase_rim_ref[k, :RIM, :], phase_rim_ref[k, end:, :]),
        ),
    )
    note = jnp.where(patch_lanes()[0], 0.0, 1.0)
    tilts = [a * note + b * (1.0 - note) for a, b in zip(tilts_of(known_ref[...]), tilts_of(partner_ref[:, 2 * tiles * LANES :]))]
    tables = (row_r, row_i, col_r, col_i)
    incident_tables(tile, tilts, row_first, columns, total_rows, total_cols, tables)
    ways = [
        propagate_steps(tile, tables, trig, (hr, hi), (w0r, w0i), (w1r, w1i), keep_in((ur_ref, ui_ref))),
        backward_steps(
            main, (gr, gi), (main_hr, main_hi), (main_w0r, main_w0i), (main_w1r, main_w1i), (main_c1, main_s1),
            put_in(own_ref), (ar, ai),
        ),
    ]
    for _ in range(4):
        for way in ways:
            next(way, None)


def sum_kernel(a_ref, b_ref, out_ref):
    out_ref[...] = a_ref[...] + b_ref[...]


def left_kernel(sizes, swap_ref, along_ref, w0r, w0i, w1r, w1i, ur, ui, c1, s1, left_ref, gr, gi, hr, hi, mr, mi):
    stripe, tiles, _, _ = sizes
    main, _, _ = main_tile(sizes)
    tile = Tile(stripe, swap_ref.shape[1] // LANES, main.top, main.bottom)
    low_illum = place()[0] == 0
    blank_rims((gr, gi, hr, hi), tile)
    fill_target(
        tile, (mr, mi), low_illum, None,
        lambda t: other_near(swap_ref, stripe, low_illum, own_columns(t)),
        lambda t: along_ref[:, own_columns(t + 2 * tiles)],
        range(tile.tiles),
    )
    residual_of(tile, (gr, gi), (ur, ui), other_target(tile, lambda rows, t: swap_ref[rows, own_columns(t)], (mr, mi)))
    backward(tile, (gr, gi), (hr, hi), (w0r, w0i), (w1r, w1i), (c1, s1), put_in(left_ref))


def other_target(tile, swapped, edges, patch=None):
    def target(part, t, rows):
        if t != patch and 2 * RIM <= rows.start < 2 * RIM + tile.stripe:
            at = own_rows(rows)
            return swapped(slice(part * tile.stripe + at.start, part * tile.stripe + at.stop), t)
        return edges[part][t, rows, :]

    return target


def back_and_left_kernel(sizes, *refs):
    back_in, left_in, refs = refs[:13], refs[13:23], refs[23:]
    back_out, left_out, refs = refs[:9], refs[9], refs[10:]
    back_kernel(sizes, *back_in, *back_out, *refs[:12])
    left_kernel(sizes, *left_in, left_out, *refs[12:])


class Joined:
    def __init__(self, main, patch, first):
        self.main, self.patch, self.first = main, patch, first

    def __getitem__(self, at):
        t = at[0] + self.first
        return self.main[(t,) + at[1:]] if t < self.main.shape[0] else self.patch[(0,) + at[1:]]


def finish_kernel(sizes, own_ref, left_ref, measured_ref, swap_ref, swap_rest_ref, along_ref, same_ref, rim_ref, relay_ref,
                  partner_relay_ref, *rest):
    main_fields, patch_fields, rest = rest[:8], rest[8:16], rest[16:]
    out_ref, patch, gr, gi, hr, hi, mr, mi, full, sems = rest
    stripe, tiles, total_rows, total_cols = sizes
    left_tiles = swap_ref.shape[1] // LANES
    begin = left_tiles - 1
    lone = tiles - begin
    w0r, w0i, w1r, w1i, ur, ui, c1, s1 = [Joined(a, b, begin) for a, b in zip(main_fields, patch_fields)]
    main, _, _ = main_tile(sizes)
    tile = Tile(stripe, lone + 1, main.top, main.bottom, patch_held(sizes)[0], lone, (lone,))
    illum, _, _ = place()
    low_illum = illum == 0
    blank_rims((gr, gi, hr, hi), tile)

    lane = lane_ids((8, LANES))
    last_rows = relay_ref.shape[0] - 8
    sums = jnp.maximum(relay_ref[last_rows:, :], partner_relay_ref[last_rows:, :])
    scales = []
    for which in range(2):
        here = jnp.where(lane == which, sums, 0.0)
        energy = jnp.sum(here[:1], axis=1, keepdims=True) / (total_rows * total_cols) + EPS_ENERGY
        scales.append(2.0 / energy)
    mine = jnp.where(low_illum, scales[0], scales[1])
    others = jnp.where(low_illum, scales[1], scales[0])

    first, last = own_columns(0), own_columns(tiles - 1)
    own_first = illum * stripe
    near_base = pl.multiple_of(stripe - 16 * illum, 16)
    near_rim = pl.multiple_of(stripe - 8 * illum, 8)

    def swapped(rows, t):
        t = t + begin
        return swap_ref[rows, own_columns(t)] if t < left_tiles else swap_rest_ref[rows, own_columns(t - left_tiles)]

    def other_rim(part, block):
        x = partner_relay_ref[2 * (block // 4 * 4) : 2 * (block // 4 * 4) + 8, :]
        shift = (LANES - 2 * RIM * (block % 4) + part * (LANES // 2)) % LANES
        return pltpu.roll(x, shift, 1) if shift else x

    def middle(part, t, r):
        at = slice(part * stripe + r, part * stripe + r + 16)
        rim = jnp.concatenate([other_rim(part, r // 8), other_rim(part, r // 8 + 1)], axis=0)
        other = join_edges(swap_ref[at, first], swapped(at, lone - 1), rim)
        at = pl.ds(pl.multiple_of(own_first + r, 16), 16)
        own = join_edges(*[measured_ref[part, 0, at, e].astype(F32) for e in (first, last)], rim_ref[part, at, :])
        return join_illums(own, other)

    def near_of(t):
        t = t + begin
        ref, t = (swap_ref, t) if t < left_tiles else (swap_rest_ref, t - left_tiles)
        return other_near(ref, stripe, low_illum, own_columns(t))

    def near(t):
        if t < lone:
            return near_of(t)
        rims = [other_rim(part, stripe // 8) for part in range(2)]
        other = [join_edges(*x) for x in zip(near_of(-begin), near_of(lone - 1), rims)]

        def rows(part, at):
            x = measured_ref[part, 0, pl.ds(near_base, 16), at].astype(F32)
            return jnp.where(low_illum, x[:8], x[8:])

        own = [join_edges(rows(part, first), rows(part, last), rim_ref[part, pl.ds(near_rim, 8), :]) for part in range(2)]
        return [join_illums(*x) for x in zip(own, other)]

    def far(t):
        if t < lone:
            return along_ref[:, own_columns(t + begin + 2 * tiles)]
        other = join_edges(*[along_ref[:, own_columns(e + 2 * tiles)] for e in (0, tiles - 1)], rim_ref[1, 2 * stripe :, :])
        own = join_edges(same_ref[:, first], same_ref[:, last], rim_ref[0, 2 * stripe :, :])
        return join_illums(own, other)

    copies = []

    def send(k, columns):
        copies.append(pltpu.make_async_copy(full.at[k, :, columns], out_ref.at[k, :, columns], sems.at[len(copies)]))
        copies[-1].start()

    for k in range(2):
        for t in range(left_tiles):
            at = own_columns(t)
            full[k, :, at] = own_ref[k, :, at] * mine + left_ref[k, :, at] * others
        if begin > 1:
            send(k, slice(LANES, begin * LANES))

    fill_target(tile, (mr, mi), low_illum, middle, near, far, range(lone))
    residual_of(tile, (gr, gi), (ur, ui), other_target(tile, swapped, (mr, mi), lone))

    def put(k, t, rows, value):
        rows = own_rows(rows)
        if t == lone:
            patch[k, rows, :] = value * mine + pltpu.roll(value, LANES - OTHER, 1) * others
            return
        at = own_columns(t + begin)
        value = own_ref[k, rows, at] * mine + value * others
        if t == 0:
            value = jnp.where(lane_ids(value.shape) < LANES // 2, full[k, rows, at], value)
        full[k, rows, at] = value

    def close(k):
        on = lane_ids(patch.shape[1:])
        full[k, :, first] = jnp.where(on < RIM, patch[k], full[k, :, first])
        full[k, :, last] = jnp.where(on >= LANES - RIM, pltpu.roll(patch[k], 56, 1), full[k, :, last])
        if begin > 0:
            send(k, first)
        send(k, slice(begin * LANES, tiles * LANES))

    backward(tile, (gr, gi), (hr, hi), (w0r, w0i), (w1r, w1i), (c1, s1), put, on_middle=functools.partial(close, 1))
    close(0)
    for copy in copies:
        copy.wait()


def like(x, held):
    shape, dtype = (x, F32) if isinstance(x, tuple) else (x.shape, x.dtype)
    return pltpu.VMEM(shape, dtype) if held else jax.ShapeDtypeStruct(shape, dtype)


def after(kernel, *refs):
    count = len(refs)

    def ordered(*args):
        return kernel(*args[count:])

    return ordered


def call(kernel, outs, *args, behind=(), scratch=(), in_place=0, flops=0, mib=8, held=(), far=0):
    kernel, args = after(kernel, *behind), (*behind, *args)
    in_place_specs = [pl.BlockSpec(memory_space=pltpu.HBM)] * in_place
    return pl.pallas_call(
        kernel,
        out_shape=[like(x, n in held) for n, x in enumerate(outs)],
        in_specs=in_place_specs
        + [pl.BlockSpec(memory_space=pltpu.VMEM)] * (len(args) - in_place),
        out_specs=[pl.BlockSpec(memory_space=pltpu.VMEM)] * (len(outs) - far) + [pl.BlockSpec(memory_space=pltpu.HBM)] * far,
        scratch_shapes=[pltpu.VMEM(s, F32) if isinstance(s, tuple) else s for s in scratch],
        compiler_params=pltpu.CompilerParams(vmem_limit_bytes=int(mib * 2**20)),
        cost_estimate=pl.CostEstimate(flops=flops, bytes_accessed=2**18, transcendentals=0),
    )(*args)


def paired(phase_delay, angles, measured):
    slices, stripe, width = phase_delay.shape
    rows, cols = lax.axis_size("row"), lax.axis_size("col")
    tiles = width // LANES
    sizes = (stripe, tiles, 2 * stripe * rows, width * cols)
    swap = [(0, 1), (1, 0)]
    along = []
    for c in range(cols):
        for r in range(rows - 1):
            below, above = ((rows + r) * cols + c, (r + 1) * cols + c)
            along += [(below, above), (above, below)]
        along += [(c, c ^ 1), ((2 * rows - 1) * cols + c, (2 * rows - 1) * cols + (c ^ 1))]
    same = [(r, (r + 1) % rows) for r in range(rows)] + [(rows + (r + 1) % rows, rows + r) for r in range(rows)]

    partner_out, along_out, same_out, known, note, measured = call(
        open_kernel, [(8, 2 * width + LANES), (8, 3 * width), (8, width), (8, LANES), (8, LANES), measured],
        phase_delay, measured, angles, in_place=3, mib=62, held=(0, 1, 2, 3, 4, 5),
        scratch=[
            (2, slices, 8, width), pltpu.VMEM(angles.shape, angles.dtype), pltpu.SemaphoreType.DMA((4,)),
        ],
    )
    along_in = lax.ppermute(along_out, ("illum", "row", "col"), along)
    partner_in = lax.ppermute(partner_out, "illum", swap)
    same_in = lax.ppermute(same_out, ("illum", "row"), same)
    core_note = lax.ppermute(note, "row", [(r, r ^ 1) for r in range(rows)])
    (pair,) = call(sum_kernel, [(8, LANES)], note, core_note)
    far = lax.ppermute(pair, "row", [(r, r ^ 2) for r in range(rows)])
    cut = max(tiles - 2, 1) * LANES
    rows_swapped = 2 * stripe + 8
    (swap_out,) = call(
        functools.partial(swap_kernel, slice(0, cut)), [(rows_swapped, cut)], measured, behind=[core_note]
    )
    swap_in = lax.ppermute(swap_out, "illum", swap)

    def fields(count):
        return [(count, stripe + 4 * RIM, LANES)]

    def tables(count):
        return [(stripe + 2 * RIM, LANES)] * 2 + [(-(-count // 8) * 8, LANES)] * 2

    own_trig = call(
        functools.partial(trig_kernel, sizes), [(tiles, stripe, LANES)] * 6 + tables(tiles), phase_delay, measured, known,
        flops=3*10**9)
    rims = 8 * (-(-(stripe // 4 + 1) // 4))
    first_out, second_packed, note = call(
        rim_pack_kernel, [(rims + 8, LANES), (rims, LANES), (8, LANES)], phase_delay, measured, pair, far, partner_in, along_in, same_in,
        behind=own_trig[:1],
    )
    first_in = lax.ppermute(first_out, "col", [(c, cols - 1 - c) for c in range(cols)])
    kept = call(
        functools.partial(ahead_kernel, sizes), fields(tiles) * 10, *own_trig[:4], partner_in, along_in,
        scratch=fields(tiles) * 2 + tables(tiles), flops=15*10**8, mib=16,
    )
    (second_out,) = call(second_kernel, [(rims + 8, LANES)], second_packed, note, first_in, behind=kept[:1])
    second_in = lax.ppermute(second_out, "col", [(c, c ^ 1) for c in range(cols)])

    own_kept = call(
        functools.partial(own_kernel, sizes), fields(tiles) * 6, *kept[:4], *own_trig[4:], measured, same_in,
        scratch=fields(tiles) * 2 + [(2, tiles, RIM, LANES)] * 2, flops=15*10**8, mib=16,
    )
    phase_rim, rim, relay = call(
        rim_unpack_kernel, [(2, stripe + 2 * RIM, LANES), (2, 2 * stripe + 8, LANES), (8 * (-(-(stripe // 8 + 1) // 4)) + 8, LANES)],
        first_in, second_in, note,
        behind=own_kept[:1],
    )
    partner_relay = lax.ppermute(relay, "illum", swap)
    (swap_out,) = call(
        functools.partial(swap_kernel, slice(cut, width)), [(rows_swapped, width - cut)], measured, behind=own_kept[:1]
    )
    swap_rest = lax.ppermute(swap_out, "illum", swap)
    own, *patch_kept, left = call(
        functools.partial(back_and_left_kernel, sizes),
        [phase_delay.shape] + fields(1) * 8 + [(slices, stripe, cut)],
        *kept[2:4], *own_kept, phase_delay, known, partner_in, along_in, phase_rim,
        swap_in, along_in, *kept[4:], *kept[2:4],
        behind=[relay], scratch=fields(tiles) * 4 + fields(1) * 4 + tables(1) + fields(cut // LANES) * 6,
        flops=2*10**9, mib=16,
    )
    (out,) = call(
        functools.partial(finish_kernel, sizes), [phase_delay.shape],
        own, left, measured, swap_in, swap_rest, along_in, same_in, rim, relay, partner_relay,
        *kept[4:], *kept[2:4], *patch_kept,
        scratch=[(slices, stripe, LANES)] + fields(tiles - cut // LANES + 2) * 6
        + [phase_delay.shape, pltpu.SemaphoreType.DMA((6,))],
        mib=12, flops=0, far=1,
    )
    return out


def halo(x, axis, dim, width, index_of=None):
    peers = lax.axis_size(axis)
    up = [(i, i + 1) for i in range(peers - 1)]
    before = lax.ppermute(lax.slice_in_dim(x, x.shape[dim] - width, x.shape[dim], axis=dim), axis, up)
    after = lax.ppermute(lax.slice_in_dim(x, 0, width, axis=dim), axis, [(j, i) for i, j in up])
    return before, after


def with_column_rims(x, width):
    before, after = halo(x, "col", x.ndim - 1, width)
    gap = jnp.zeros(x.shape[:-1] + (LANES - 2 * width,), x.dtype)
    return jnp.concatenate([x, after, gap, before], axis=-1)


def stripe_halo(x, width):
    illums, rows = lax.axis_size("illum"), lax.axis_size("row")
    where = [(s % illums) * rows + s // illums for s in range(illums * rows)]
    up = [(where[s], where[s + 1]) for s in range(illums * rows - 1)]
    before = lax.ppermute(x[:, -width:], ("illum", "row"), up)
    after = lax.ppermute(x[:, :width], ("illum", "row"), [(b, a) for a, b in up])
    return jnp.concatenate([before, x, after], axis=1)


def per_device(phase_delay, angles, measured):
    illums = lax.axis_size("illum")
    if (illums, lax.axis_size("row"), lax.axis_size("col")) == (2, 4, 4):
        return paired(phase_delay, angles, measured)
    slices, stripe, width = phase_delay.shape
    tile_rows = measured.shape[2]
    total_rows, total_cols = tile_rows * lax.axis_size("row"), width * lax.axis_size("col")
    tiles = width // LANES + 1
    row_first = lax.axis_index("row") * tile_rows + lax.axis_index("illum") * stripe
    col_first = lax.axis_index("col") * width

    target = measured[:, 0].astype(F32)
    energy = lax.psum(jnp.sum(target * target).reshape(1), ("row", "col"))
    energies = lax.all_gather(energy, "illum", tiled=True) / (total_rows * total_cols) + EPS_ENERGY
    tilts = lax.all_gather(angles, "illum", tiled=True)

    phase = with_column_rims(stripe_halo(phase_delay, RIM), RIM)
    above, below = halo(target, "row", 1, REACH)
    target = with_column_rims(jnp.concatenate([above, target, below], axis=1), REACH)
    windows = jnp.stack([target[:, i * stripe : (i + 1) * stripe + 2 * REACH] for i in range(illums)])
    windows = lax.all_to_all(windows, "illum", 0, 0, tiled=True)
    windows = jnp.pad(windows, ((0, 0), (0, 0), (RIM - REACH, RIM - REACH), (0, 0)))

    field = pltpu.VMEM((tiles, stripe + 4 * RIM, LANES), F32)
    rows_all = stripe + 2 * RIM
    return pl.pallas_call(
        functools.partial(gradient_kernel, (stripe, tiles, illums, total_rows, total_cols)),
        out_shape=jax.ShapeDtypeStruct(phase_delay.shape, F32),
        in_specs=[pl.BlockSpec(memory_space=pltpu.SMEM)] * 3 + [pl.BlockSpec(memory_space=pltpu.VMEM)] * 2,
        out_specs=pl.BlockSpec(memory_space=pltpu.VMEM),
        scratch_shapes=[field] * 12
        + [pltpu.VMEM((rows_all, LANES), F32)] * 2
        + [pltpu.VMEM((-(-tiles // 8) * 8, LANES), F32)] * 2,
        compiler_params=pltpu.CompilerParams(vmem_limit_bytes=48 * 2**20),
    )(jnp.stack([row_first, col_first]), tilts, 2.0 / energies, phase, windows)


def solution(mesh):
    placed = (P(None, ("row", "illum"), "col"), P("illum", None), P(None, "illum", "row", "col"))
    return jax.shard_map(
        per_device,
        mesh=mesh,
        in_specs=placed,
        out_specs=P(None, ("row", "illum"), "col"),
        check_vma=False,
    )
```
